256 devices in a mesh: gx: 8 (over y_lo, x), row: 16 (over z, y_hi), rep: 2 (over core).
Axes of the slice: x: 4, y: 4 (y_hi: 2, y_lo: 2; y = y_hi * 2 + y_lo), z: 8, core: 2. Of those that a mesh axis runs over, the one named last changes fastest.
Arguments:
- samples: bfloat16 [2, 64, 32, 64, 128], P('rep', None, 'gx', 'row'), may hold values from -6 to 6
- cotangent: bfloat16 [2, 64, 32, 64, 128], P('rep', None, 'gx', 'row'), may hold values from -6 to 6
- kernel_0: bfloat16 [16, 27, 64], replicated, may hold values from -0.15625 to 0.15625
- kernel_1: bfloat16 [16, 27, 80], replicated, may hold values from -0.125 to 0.125
- kernel_2: bfloat16 [16, 27, 96], replicated, may hold values from -0.125 to 0.125
- kernel_3: bfloat16 [16, 27, 112], replicated, may hold values from -0.109375 to 0.109375
- layer_bias: bfloat16 [4, 16], replicated, may hold values from -3 to 3
- merging_weight: bfloat16 [64, 128], replicated, may hold values from -0.5 to 0.5
- merging_bias: bfloat16 [64], replicated, may hold values from -3 to 3
Outputs:
- output: float32 [2, 64, 32, 64, 128], P('rep', None, 'gx', 'row')
- grad_input: float32 [2, 64, 32, 64, 128], P('rep', None, 'gx', 'row')
- grad_kernel_0: float32 [16, 27, 64], replicated
- grad_kernel_1: float32 [16, 27, 80], replicated
- grad_kernel_2: float32 [16, 27, 96], replicated
- grad_kernel_3: float32 [16, 27, 112], replicated
- grad_layer_bias: float32 [4, 16], replicated
- grad_merging_weight: float32 [64, 128], replicated
- grad_merging_bias: float32 [64], replicated
The draws below stay inside these ranges and needn't reach their ends.
All inputs are finite; a program needn't handle non-finite values.
Results may differ from the reference program's by a relative error of at most 0.009.
Values may be sent and summed in bfloat16 or wider, within the bound.
No kernel may reach another device: no remote copies, remote signals or barrier semaphores. Data moves between devices by JAX's collectives and lax.ppermute only.
A program may use at most 256 MiB of HBM per device.

```python
import math
import jax
import jax.numpy as jnp
from jax import lax

C = 64
G = 16
BATCH = 2
NX = 32
NY = 64
NZ = 128


def shard_levels(stream_key, shape, shards, least, largest):
    def one(axis_at, shards_of):
        steps = jax.random.uniform(jax.random.fold_in(jax.random.fold_in(stream_key, 6), axis_at), (shards_of,), jnp.float32, least / len(shards), largest / len(shards))
        return jnp.repeat(jnp.exp(steps), shape[axis_at] // shards_of).reshape((-1,) + (1,) * (len(shape) - axis_at - 1))

    factor_of = one(*shards[0])
    for cut in shards[1:]:
        factor_of = factor_of * one(*cut)
    return factor_of


def centred(rng, extent, scale, bound, split=(), dtype=jnp.bfloat16):
    drawn = scale * jax.random.normal(rng, extent, jnp.float32)
    if split:
        drawn = drawn * shard_levels(rng, extent, split, -0.22, 0.18)
    return jnp.clip(drawn, -bound, bound).astype(dtype)


def setup_inputs(seed: int = 0) -> dict:
    key_of = jax.random.split(jax.random.key(seed), 10)
    return {
        "samples": centred(key_of[0], (BATCH, C, NX, NY, NZ), 1.0, 6.0, ((0, 2), (2, 8), (3, 16))),
        "cotangent": centred(key_of[1], (BATCH, C, NX, NY, NZ), 1.0, 6.0, ((0, 2), (2, 8), (3, 16))),
        "kernel_0": centred(key_of[2], (G, 27, C), (27 * C) ** -0.5, 0.15625),
        "kernel_1": centred(key_of[3], (G, 27, C + G), (27 * (C + G)) ** -0.5, 0.125),
        "kernel_2": centred(key_of[4], (G, 27, C + 2 * G), (27 * (C + 2 * G)) ** -0.5, 0.125),
        "kernel_3": centred(key_of[5], (G, 27, C + 3 * G), (27 * (C + 3 * G)) ** -0.5, 0.109375),
        "layer_bias": centred(key_of[6], (4, G), 1.0, 3.0),
        "merging_weight": centred(key_of[7], (C, C + 4 * G), (C + 4 * G) ** -0.5, 0.5),
        "merging_bias": centred(key_of[8], (C,), 1.0, 3.0),
    }


BETA = 0.2

def activate(value):
    return 0.2 * value + 0.8 * value * jax.nn.sigmoid(value)

def slope_of(value):
    sigmoid_v = jax.nn.sigmoid(value)
    return 0.2 + 0.8 * (sigmoid_v + value * sigmoid_v * (1.0 - sigmoid_v))

def convolve(stacked, kernel):
    growth = kernel.shape[0]
    in_chans = kernel.shape[2]
    shaped = kernel.reshape(growth, 3, 3, 3, in_chans).transpose(0, 4, 1, 2, 3)
    return lax.conv_general_dilated(stacked, shaped, (1, 1, 1), ((1, 1), (1, 1), (1, 1)), dimension_numbers=('NCDHW', 'OIDHW', 'NCDHW'), precision=lax.Precision.HIGHEST)

def round_half(value):
    rounded = value.astype(jnp.bfloat16)
    rounded = lax.optimization_barrier(rounded)
    return rounded.astype(jnp.float32)

def reference(samples, cotangent, kernel_0, kernel_1, kernel_2, kernel_3, layer_bias, merging_weight, merging_bias):
    kernels = (kernel_0, kernel_1, kernel_2, kernel_3)
    channels = samples.shape[1]
    growth = layer_bias.shape[1]
    norm_scale = 1.0 / math.sqrt(samples.shape[0] * samples.shape[2] * samples.shape[3] * samples.shape[4])
    samples_f = samples.astype(jnp.float32)
    biases = layer_bias.astype(jnp.float32)
    features = [samples_f]
    pre_acts = []
    for layer_num in range(4):
        stacked = jnp.concatenate(features, axis=1)
        pre_act = convolve(stacked, kernels[layer_num].astype(jnp.float32)) + biases[layer_num][None, :, None, None, None]
        pre_acts.append(pre_act)
        features.append(round_half(activate(pre_act)))
    joined = jnp.concatenate(features, axis=1)
    weight_f = merging_weight.astype(jnp.float32)
    merged = jnp.einsum('oc,bcxyz->boxyz', weight_f, joined, precision=lax.Precision.HIGHEST)
    merged = merged + merging_bias.astype(jnp.float32)[None, :, None, None, None]
    output = samples_f + BETA * merged
    grad_out = cotangent.astype(jnp.float32)
    merge_grad = round_half(BETA * grad_out)
    grad_merging_weight = jnp.einsum('boxyz,bcxyz->oc', merge_grad, joined, precision=lax.Precision.HIGHEST) * norm_scale
    grad_merging_bias = lax.optimization_barrier(jnp.sum(merge_grad, axis=(0, 2, 3, 4))) * norm_scale
    carried = jnp.einsum('oc,boxyz->bcxyz', weight_f, merge_grad, precision=lax.Precision.HIGHEST)
    grad_acc = grad_out + carried[:, :channels]
    hidden_grads = [carried[:, channels + k * growth:channels + (k + 1) * growth] for k in range(4)]
    grad_kernels = [None, None, None, None]
    grad_biases = [None, None, None, None]
    for layer_num in (3, 2, 1, 0):
        pre_grad = round_half(hidden_grads[layer_num] * slope_of(pre_acts[layer_num]))
        grad_biases[layer_num] = lax.optimization_barrier(jnp.sum(pre_grad, axis=(0, 2, 3, 4))) * norm_scale
        stacked = jnp.concatenate(features[:layer_num + 1], axis=1)
        unused, pullback = jax.vjp(convolve, stacked, kernels[layer_num].astype(jnp.float32))
        pulled, kernel_bar = pullback(pre_grad)
        grad_kernels[layer_num] = kernel_bar * norm_scale
        grad_acc = grad_acc + pulled[:, :channels]
        for other in range(layer_num):
            hidden_grads[other] = hidden_grads[other] + pulled[:, channels + other * growth:channels + (other + 1) * growth]
    grad_layer_bias = jnp.stack(grad_biases, axis=0)
    return (output, grad_acc, grad_kernels[0], grad_kernels[1], grad_kernels[2], grad_kernels[3], grad_layer_bias, grad_merging_weight, grad_merging_bias)
```

```python
import functools
import math

import jax
import jax.numpy as jnp
from jax import lax
from jax.experimental import pallas as pl
from jax.experimental.pallas import tpu as pltpu
from jax.sharding import PartitionSpec as P

BETA = 0.2
BF16, F32 = jnp.bfloat16, jnp.float32
Z = 128
B = 4
H = 2
N = B + 2 * H
MID = slice(H * Z, (H + B) * Z)
RING = slice((H - 1) * Z, (H + B + 1) * Z)
DEVICES = 256
ROWS = 8
VMEM_LIMIT = 24 * 2**20


def shape(dims, dtype):
    return jax.ShapeDtypeStruct(dims, dtype)


def call(kernel, outs, args, scratch=(), flops=1_000_000, name=None):
    moved = sum(math.prod(a.shape) * a.dtype.itemsize for a in list(args) + list(outs))
    return pl.pallas_call(
        kernel,
        out_shape=list(outs),
        in_specs=[pl.BlockSpec(memory_space=pltpu.VMEM)] * len(args),
        out_specs=[pl.BlockSpec(memory_space=pltpu.VMEM)] * len(outs),
        scratch_shapes=list(scratch),
        compiler_params=pltpu.CompilerParams(vmem_limit_bytes=VMEM_LIMIT),
        cost_estimate=pl.CostEstimate(flops=flops, bytes_accessed=moved, transcendentals=0),
        name=name,
    )(*args)


def lane_moves(rows, width):
    lane = lax.broadcasted_iota(jnp.int32, (rows, width), 1) % Z
    return lane != 0, lane != Z - 1


def from_left(v, keep):
    return jnp.where(keep, pltpu.roll(v, 1, 1), 0.0)


def from_right(v, keep):
    return jnp.where(keep, pltpu.roll(v, v.shape[1] - 1, 1), 0.0)


def spread(v):
    not_first, not_last = lane_moves(*v.shape)
    return jnp.concatenate([from_right(v, not_last), v, from_left(v, not_first)], axis=0).astype(BF16)


def conv_row(kernel_ref, sources, i, lanes):
    n = lanes.stop - lanes.start
    acc = jnp.zeros((48, n), F32)
    for a in range(3):
        for b in range(3):
            cut = pl.ds(lanes.start + (b - 1) * Z, n)
            rhs = [s[i + a - 1, :, cut] for s in sources]
            rhs = rhs[0] if len(rhs) == 1 else jnp.concatenate(rhs, axis=0)
            acc = acc + jnp.dot(kernel_ref[3 * a + b], rhs, preferred_element_type=F32)
    not_first, not_last = lane_moves(16, n)
    return from_left(acc[:16], not_first) + acc[16:32] + from_right(acc[32:], not_last)


def back_row(weights, spread_ref, i, lanes):
    n = lanes.stop - lanes.start
    pieces = [
        spread_ref[i + 1 - a, :, pl.ds(lanes.start + (1 - b) * Z, n)]
        for a in range(3)
        for b in range(3)
    ]
    return jnp.dot(weights, jnp.concatenate(pieces, axis=0), preferred_element_type=F32)


def kernel_gradient(out_ref, own, sources):
    for a in range(3):
        for b in range(3):
            cut = pl.ds((H + b - 1) * Z, B * Z)
            rhs = jnp.concatenate(
                [jnp.concatenate([s[H + i + a - 1, :, cut] for s in sources], axis=0) for i in range(B)],
                axis=1,
            )
            got = lax.dot_general(own, rhs, (((1,), (1,)), ((), ())), preferred_element_type=F32)
            t = 48 * (3 * a + b)
            out_ref[t : t + 48, : got.shape[1]] = got.astype(BF16)
            if got.shape[1] < Z:
                out_ref[t : t + 48, got.shape[1] :] = jnp.zeros((48, Z - got.shape[1]), BF16)


def own_cells(spread_ref):
    return jnp.concatenate([spread_ref[H + i, :, MID] for i in range(B)], axis=1)


def activate(value):
    sigmoid = jax.nn.sigmoid(value)
    return 0.2 * value + 0.8 * value * sigmoid, 0.2 + 0.8 * (
        sigmoid + value * sigmoid * (1.0 - sigmoid)
    )


def assemble(parts, frame):
    before, top, bottom, after, left, right = parts
    frame[0:2, :, MID] = before[...]
    frame[2:4, :, MID] = top[...]
    frame[4:6, :, MID] = bottom[...]
    frame[6:8, :, MID] = after[...]
    frame[:, :, : H * Z] = left[...]
    frame[:, :, (H + B) * Z :] = right[...]


def wide_sum(v):
    return jnp.broadcast_to(jnp.sum(v, axis=1, keepdims=True), (v.shape[0], Z))


def pack_kernel(x_ref, top_ref, bottom_ref, wide):
    wide[...] = x_ref[...].astype(F32)
    for i in range(B):
        out = top_ref if i < 2 else bottom_ref
        for j in range(B):
            got = wide[pl.ds(B * i + j, 64, stride=B * B), :]
            out[i % 2, :, j * Z : (j + 1) * Z] = got.astype(BF16)


def columns_kernel(before, top, bottom, after, left, right):
    for r, ref in enumerate((before, top, bottom, after)):
        left[2 * r : 2 * r + 2] = ref[:, :, : H * Z]
        right[2 * r : 2 * r + 2] = ref[:, :, (B - H) * Z :]


def prepare_kernel(cot_ref, merge_t, k0, k1, k2, k3, base, carried, merge_grad, w0, w1, w2, w3, wide):
    for k_ref, w_ref in ((k0, w0), (k1, w1), (k2, w2), (k3, w3)):
        w_ref[...] = jnp.transpose(k_ref[...].astype(F32)).astype(BF16)
    wide[...] = cot_ref[...].astype(F32)
    for i in range(B):
        cot = jnp.concatenate(
            [wide[pl.ds(B * i + j, 64, stride=B * B), :] for j in range(B)], axis=1
        )
        grad = (BETA * cot).astype(BF16)
        merge_grad[i] = grad
        back = jnp.dot(merge_t[...], grad, preferred_element_type=F32)
        base[i] = cot + back[:64]
        carried[i] = back[64:]


def first_kernel(
    before, top, bottom, after, left, right, k0, k1, bias, mask,
    frame, hidden_0, slope_0, slope_1, send_top, send_bottom,
):
    assemble((before, top, bottom, after, left, right), frame)

    def ring(i, carry):
        pre = conv_row(k0, [frame], i, RING) + bias[0:16, 0:1]
        value, slope = activate(pre)
        slope_0[i] = slope
        hidden_0[i, :, RING] = (value * mask[pl.ds(i, 1), RING]).astype(BF16)
        return carry

    lax.fori_loop(H - 1, H + B + 1, ring, 0)
    for i in range(B):
        pre = conv_row(k1, [frame, hidden_0], H + i, MID) + bias[16:32, 0:1]
        value, slope = activate(pre)
        slope_1[i] = slope
        send = send_top if i < 2 else send_bottom
        send[i % 2, 0:16] = hidden_0[H + i, :, MID]
        send[i % 2, 16:32] = value.astype(BF16)


def second_kernel(
    before, top, bottom, after, left, right, frame, k2, k3, bias, mask, carried,
    hidden_01, hidden_2, hidden_3, slope_2, own_3, send_top, send_bottom,
):
    assemble((before, top, bottom, after, left, right), hidden_01)

    def ring(i, carry):
        pre = conv_row(k2, [frame, hidden_01], i, RING) + bias[32:48, 0:1]
        value, slope = activate(pre)
        slope_2[i] = slope
        hidden_2[i, :, RING] = (value * mask[pl.ds(i, 1), RING]).astype(BF16)
        return carry

    lax.fori_loop(H - 1, H + B + 1, ring, 0)
    for i in range(B):
        pre = conv_row(k3, [frame, hidden_01, hidden_2], H + i, MID) + bias[48:64, 0:1]
        value, slope = activate(pre)
        hidden_3[i] = value.astype(BF16)
        grad = (carried[i, 48:64] * slope).astype(BF16)
        own_3[i] = spread(grad.astype(F32))
        send = send_top if i < 2 else send_bottom
        send[i % 2, 0:16] = grad
        send[i % 2, 16:32] = carried[i, 32:48].astype(BF16)


def merge_kernel(
    frame, hidden_01, hidden_2, hidden_3, own_3, merge, merge_bias, merge_grad,
    out_ref, grad_3, grad_merge,
):
    total = jnp.zeros((64, 128), F32)
    total_bias = jnp.zeros((64, B * Z), F32)
    for i in range(B):
        base = frame[H + i, :, MID]
        joined = jnp.concatenate(
            [base, hidden_01[H + i, :, MID], hidden_2[H + i, :, MID], hidden_3[i]], axis=0
        )
        merged = jnp.dot(merge[...], joined, preferred_element_type=F32) + merge_bias[:, 0:1]
        out = base.astype(F32) + BETA * merged
        for j in range(B):
            out_ref[pl.ds(B * i + j, 64, stride=B * B), :] = out[:, j * Z : (j + 1) * Z]
        grad = merge_grad[i]
        total = total + lax.dot_general(
            grad, joined, (((1,), (1,)), ((), ())), preferred_element_type=F32
        )
        total_bias = total_bias + grad.astype(F32)
    grad_merge[0:64] = total.astype(BF16)
    grad_merge[64:128] = wide_sum(total_bias).astype(BF16)
    own = jnp.concatenate([own_3[i] for i in range(B)], axis=1)
    grad_merge[128:144] = wide_sum(own[16:32].astype(F32)).astype(BF16)
    kernel_gradient(grad_3, own, [frame, hidden_01, hidden_2])


def third_kernel(
    before, top, bottom, after, left, right, w2, w3, slope_1, slope_2, mask, carried,
    spread_3, spread_2, own_1, send_top, send_bottom, pieces, held,
):
    assemble((before, top, bottom, after, left, right), pieces)
    held[...] = pieces[:, 16:32, :].astype(F32)
    for i in range(B):
        held[H + i, :, MID] = carried[i, 32:48]

    def move(i, carry):
        spread_3[i] = spread(pieces[i, 0:16].astype(F32))
        return carry

    lax.fori_loop(0, N, move, 0)

    def ring(i, carry):
        got = held[i, :, RING] + back_row(w3[96:112], spread_3, i, RING)
        grad = (got * slope_2[i] * mask[pl.ds(i, 1), RING]).astype(BF16)
        spread_2[i, :, RING] = spread(grad.astype(F32))
        return carry

    lax.fori_loop(H - 1, H + B + 1, ring, 0)
    for i in range(B):
        got = (
            carried[i, 16:32]
            + back_row(w3[80:96], spread_3, H + i, MID)
            + back_row(w2[80:96], spread_2, H + i, MID)
        )
        grad = (got * slope_1[i]).astype(BF16)
        own_1[i] = spread(grad.astype(F32))
        send = send_top if i < 2 else send_bottom
        send[i % 2, 0:16] = spread_2[H + i, 16:32, MID]
        send[i % 2, 16:32] = grad
        send[i % 2, 32:48] = carried[i, 0:16].astype(BF16)


def beside_kernel(
    frame, hidden_01, spread_3, spread_2, own_1, w3, base,
    grad_2, grad_1, grad_bias, part_0, part_base,
):
    own = jnp.concatenate([own_1[i] for i in range(B)], axis=1)
    grad_bias[0:16] = wide_sum(own[16:32].astype(F32)).astype(BF16)
    kernel_gradient(grad_1, own, [frame, hidden_01.at[:, 0:16, :]])
    own = own_cells(spread_2)
    grad_bias[16:32] = wide_sum(own[16:32].astype(F32)).astype(BF16)
    kernel_gradient(grad_2, own, [frame, hidden_01])

    def ring(i, carry):
        part_0[i] = back_row(w3[64:80], spread_3, i, RING)
        return carry

    lax.fori_loop(H - 1, H + B + 1, ring, 0)
    for i in range(B):
        part_base[i] = base[i] + back_row(w3[0:64], spread_3, H + i, MID)


def fourth_kernel(
    before, top, bottom, after, left, right, w1, w2, slope_0, mask, carried, part_0, frame,
    grad_1, grad_2, grad_3, grad_merge, grad_bias,
    spread_2, spread_1, spread_0, sums, pieces, held,
):
    assemble((before, top, bottom, after, left, right), pieces)
    held[...] = pieces[:, 32:48, :].astype(F32)
    for i in range(B):
        held[H + i, :, MID] = carried[i, 0:16]

    def move(i, carry):
        spread_2[i] = spread(pieces[i, 0:16].astype(F32))
        spread_1[i] = spread(pieces[i, 16:32].astype(F32))
        return carry

    lax.fori_loop(0, N, move, 0)

    def ring(i, carry):
        got = (
            held[i, :, RING]
            + part_0[i]
            + back_row(w2[64:80], spread_2, i, RING)
            + back_row(w1[64:80], spread_1, i, RING)
        )
        grad = (got * slope_0[i] * mask[pl.ds(i, 1), RING]).astype(BF16)
        spread_0[i, :, RING] = spread(grad.astype(F32))
        return carry

    lax.fori_loop(H - 1, H + B + 1, ring, 0)
    own = own_cells(spread_0)
    kernel_gradient(sums.at[0:432], own, [frame])
    sums[432:864] = grad_1[...]
    sums[864:1296] = grad_2[...]
    sums[1296:1728] = grad_3[...]
    sums[1728:1856] = grad_merge[0:128]
    sums[1856:1872] = wide_sum(own[16:32].astype(F32)).astype(BF16)
    sums[1872:1904] = grad_bias[...]
    sums[1904:1920] = grad_merge[128:144]
    sums[1920:2048] = jnp.zeros((128, Z), BF16)


def last_kernel(spread_2, spread_1, spread_0, w0, w1, w2, part_base, out_ref):
    for i in range(B):
        out = (
            part_base[i]
            + back_row(w2[0:64], spread_2, H + i, MID)
            + back_row(w1[0:64], spread_1, H + i, MID)
            + back_row(w0[...], spread_0, H + i, MID)
        )
        for j in range(B):
            out_ref[pl.ds(B * i + j, 64, stride=B * B), :] = out[:, j * Z : (j + 1) * Z]


def add_kernel(x_ref, out_ref):
    def step(k, acc):
        block = x_ref[pl.ds(pl.multiple_of(k * 128, 128), 128), :].astype(F32)
        return acc + block

    acc = lax.fori_loop(0, DEVICES * ROWS // 128, step, jnp.zeros((128, Z), F32))
    total = acc[0:ROWS]
    for k in range(1, 128 // ROWS):
        total = total + acc[k * ROWS : (k + 1) * ROWS]
    block = jnp.concatenate([total] * (128 // ROWS), axis=0).astype(BF16)

    def put(k, carry):
        out_ref[pl.ds(pl.multiple_of(k * 128, 128), 128), :] = block
        return carry

    lax.fori_loop(0, DEVICES * ROWS // 128, put, 0)


def turned(block, scale):
    rows = lax.broadcasted_iota(jnp.int32, block.shape, 0)
    lanes = lax.broadcasted_iota(jnp.int32, block.shape, 1)
    return jnp.sum(jnp.where(rows == lanes, block, 0.0), axis=0, keepdims=True) * scale


def unpack_kernel(scale, x_ref, g0, g1, g2, g3, bias, weight, weight_bias):
    for k, g in enumerate((g0, g1, g2, g3)):
        g[...] = x_ref[432 * k : 432 * (k + 1), : g.shape[1]].astype(F32) * scale
    weight[...] = x_ref[1728:1792].astype(F32) * scale
    weight_bias[...] = turned(x_ref[1792:1856].astype(F32), scale)[:, :64]
    for k in range(4):
        block = x_ref[1856 + 16 * k : 1872 + 16 * k].astype(F32)
        bias[k : k + 1] = turned(block, scale)[:, :16]


def exchange(top, bottom):
    channels = top.shape[1]
    up = [(i, i + 1) for i in range(lax.axis_size("gx") - 1)]
    before = lax.ppermute(bottom, "gx", up)
    after = lax.ppermute(top, "gx", [(j, i) for i, j in up])
    side = shape((N, channels, H * Z), BF16)
    left, right = call(
        columns_kernel, [side, side], [before, top, bottom, after], name="columns"
    )
    up = [(i, i + 1) for i in range(lax.axis_size("row") - 1)]
    from_before = lax.ppermute(right, "row", up)
    from_after = lax.ppermute(left, "row", [(j, i) for i, j in up])
    return [before, top, bottom, after, from_before, from_after]


def grid_mask():
    steps = jnp.arange(N) - H
    gx = lax.axis_index("gx") * B + steps
    gy = lax.axis_index("row") * B + steps
    inside_x = (gx >= 0) & (gx < lax.axis_size("gx") * B)
    inside_y = (gy >= 0) & (gy < lax.axis_size("row") * B)
    inside = (inside_x[:, None] & inside_y[None, :]).astype(F32)
    return jnp.repeat(inside, Z, axis=1)


def body(samples, cotangent, kernel_0, kernel_1, kernel_2, kernel_3, layer_bias, merging_weight, merging_bias):
    kernels = (kernel_0, kernel_1, kernel_2, kernel_3)
    cells = B * B * Z * lax.axis_size("gx") * lax.axis_size("row") * lax.axis_size("rep")
    scale = 1.0 / math.sqrt(cells)
    taps = [k.transpose(1, 0, 2).reshape(9, 48, k.shape[2]) for k in kernels]
    flat = [k.transpose(1, 0, 2).reshape(432, k.shape[2]) for k in kernels]
    bias = jnp.broadcast_to(layer_bias.astype(F32).reshape(64, 1), (64, Z))
    merge_bias = jnp.broadcast_to(merging_bias.astype(F32)[:, None], (64, Z))
    mask = grid_mask()
    half = shape((2, 64, B * Z), BF16)
    wide = pltpu.VMEM((1024, Z), F32)
    top, bottom = call(
        pack_kernel, [half, half], [samples.reshape(1024, Z)], [wide], name="pack"
    )
    base, carried, merge_grad, w0, w1, w2, w3 = call(
        prepare_kernel,
        [shape((B, 64, B * Z), F32)] * 2
        + [shape((B, 64, B * Z), BF16)]
        + [shape((k.shape[2], 432), BF16) for k in kernels],
        [cotangent.reshape(1024, Z), merging_weight.T] + flat,
        [wide],
        flops=40_000_000,
        name="prepare",
    )
    parts = exchange(top, bottom)
    ring = shape((N, 16, (B + 2) * Z), F32)
    send = shape((2, 32, B * Z), BF16)
    frame, hidden_0, slope_0, slope_1, top, bottom = call(
        first_kernel,
        [shape((N, 64, N * Z), BF16), shape((N, 16, N * Z), BF16), ring, shape((B, 16, B * Z), F32), send, send],
        parts + [taps[0], taps[1], bias, mask],
        name="layers_0_1",
    )
    parts = exchange(top, bottom)
    hidden_01, hidden_2, hidden_3, slope_2, own_3, top, bottom = call(
        second_kernel,
        [
            shape((N, 32, N * Z), BF16),
            shape((N, 16, N * Z), BF16),
            shape((B, 16, B * Z), BF16),
            ring,
            shape((B, 48, B * Z), BF16),
            send,
            send,
        ],
        parts + [frame, taps[2], taps[3], bias, mask, carried],
        name="layers_2_3",
    )
    parts = exchange(top, bottom)
    grads = shape((432, Z), BF16)
    output, grad_3, grad_merge = call(
        merge_kernel,
        [shape((1024, Z), F32), grads, shape((144, Z), BF16)],
        [frame, hidden_01, hidden_2, hidden_3, own_3, merging_weight, merge_bias, merge_grad],
        flops=100_000_000,
        name="merge",
    )
    send = shape((2, 48, B * Z), BF16)
    spreads = shape((N, 48, N * Z), BF16)
    spread_3, spread_2, own_1, top, bottom = call(
        third_kernel,
        [spreads, spreads, shape((B, 48, B * Z), BF16), send, send],
        parts + [w2, w3, slope_1, slope_2, mask, carried],
        [pltpu.VMEM((N, 32, N * Z), BF16), pltpu.VMEM((N, 16, N * Z), F32)],
        name="gradients_2_1",
    )
    parts = exchange(top, bottom)
    grad_2, grad_1, grad_bias, part_0, part_base = call(
        beside_kernel,
        [grads, grads, shape((32, Z), BF16), ring, shape((B, 64, B * Z), F32)],
        [frame, hidden_01, spread_3, spread_2, own_1, w3, base],
        flops=200_000_000,
        name="kernel_gradients_2_1",
    )
    spread_2, spread_1, spread_0, sums = call(
        fourth_kernel,
        [spreads, spreads, spreads, shape((DEVICES * ROWS, Z), BF16)],
        parts
        + [w1, w2, slope_0, mask, carried, part_0, frame]
        + [grad_1, grad_2, grad_3, grad_merge, grad_bias],
        [pltpu.VMEM((N, 48, N * Z), BF16), pltpu.VMEM((N, 16, N * Z), F32)],
        name="gradient_0",
    )
    axes = ("gx", "row", "rep")
    spread_sums = lax.all_to_all(sums.reshape(DEVICES, ROWS, Z), axes, 0, 0, tiled=True)
    (added,) = call(
        add_kernel,
        [shape((DEVICES * ROWS, Z), BF16)],
        [spread_sums.reshape(DEVICES * ROWS, Z)],
        name="add",
    )
    totals = lax.all_to_all(added.reshape(DEVICES, ROWS, Z), axes, 0, 0, tiled=True)
    (grad_input,) = call(
        last_kernel,
        [shape((1024, Z), F32)],
        [spread_2, spread_1, spread_0, w0, w1, w2, part_base],
        flops=300_000_000,
        name="input_gradient",
    )
    unpacked = call(
        functools.partial(unpack_kernel, scale),
        [shape((432, k.shape[2]), F32) for k in kernels]
        + [shape((4, 16), F32), shape((64, 128), F32), shape((1, 64), F32)],
        [totals.reshape(DEVICES * ROWS, Z)],
        name="unpack",
    )
    grad_kernels = [g.reshape(27, 16, g.shape[1]).transpose(1, 0, 2) for g in unpacked[:4]]
    out_shape = (1, 64, B, B, Z)
    return (
        output.reshape(out_shape),
        grad_input.reshape(out_shape),
        *grad_kernels,
        unpacked[4],
        unpacked[5],
        unpacked[6].reshape(64),
    )


def solution(mesh):
    split = P("rep", None, "gx", "row", None)
    return jax.shard_map(
        body,
        mesh=mesh,
        in_specs=(split, split) + (P(),) * 7,
        out_specs=(split, split) + (P(),) * 7,
        check_vma=False,
    )
```

```python
import functools
import math

import jax
import jax.numpy as jnp
from jax import lax
from jax.experimental import pallas as pl
from jax.experimental.pallas import tpu as pltpu
from jax.sharding import PartitionSpec as P

BETA = 0.2
BF16, F32 = jnp.bfloat16, jnp.float32
Z = 128
B = 4
H = 2
N = B + 2 * H
MID = slice(H * Z, (H + B) * Z)
RING = slice((H - 1) * Z, (H + B + 1) * Z)
GROUP = 128
ROWS = 8
HALF = GROUP * ROWS
VMEM_LIMIT = 24 * 2**20


def shape(dims, dtype):
    return jax.ShapeDtypeStruct(dims, dtype)


def call(kernel, outs, args, scratch=(), flops=1_000_000, name=None):
    moved = sum(math.prod(a.shape) * a.dtype.itemsize for a in list(args) + list(outs))
    return pl.pallas_call(
        kernel,
        out_shape=list(outs),
        in_specs=[
            pl.BlockSpec(memory_space=pltpu.SMEM if a.dtype == jnp.int32 else pltpu.VMEM) for a in args
        ],
        out_specs=[pl.BlockSpec(memory_space=pltpu.VMEM)] * len(outs),
        scratch_shapes=list(scratch),
        compiler_params=pltpu.CompilerParams(vmem_limit_bytes=VMEM_LIMIT),
        cost_estimate=pl.CostEstimate(flops=flops, bytes_accessed=moved, transcendentals=0),
        name=name,
    )(*args)


def lane_moves(rows, width):
    lane = lax.broadcasted_iota(jnp.int32, (rows, width), 1) % Z
    return lane != 0, lane != Z - 1


def from_left(v, keep):
    return jnp.where(keep, pltpu.roll(v, 1, 1), 0.0)


def from_right(v, keep):
    return jnp.where(keep, pltpu.roll(v, v.shape[1] - 1, 1), 0.0)


def spread(v):
    not_first, not_last = lane_moves(*v.shape)
    return jnp.concatenate([from_right(v, not_last), v, from_left(v, not_first)], axis=0).astype(BF16)


def conv_row(kernel_ref, sources, i, lanes):
    n = lanes.stop - lanes.start
    cut = slice(lanes.start - Z, lanes.stop + Z)
    rhs = jnp.concatenate([s[i + a - 1, :, cut] for a in range(3) for s in sources], axis=0)
    got = jnp.dot(kernel_ref[...], rhs, preferred_element_type=F32)
    acc = got[:48, :n] + got[48:96, Z : Z + n] + got[96:, 2 * Z :]
    not_first, not_last = lane_moves(16, n)
    return from_left(acc[:16], not_first) + acc[16:32] + from_right(acc[32:], not_last)


def back_row(turned_ref, channels, spread_ref, i, lanes):
    n, q = lanes.stop - lanes.start, channels.stop - channels.start
    cut = slice(lanes.start - Z, lanes.stop + Z)
    lhs = jnp.concatenate([turned_ref[b, channels] for b in range(3)], axis=0)
    rhs = jnp.concatenate([spread_ref[i + 1 - a, :, cut] for a in range(3)], axis=0)
    got = jnp.dot(lhs, rhs, preferred_element_type=F32)
    return got[:q, 2 * Z :] + got[q : 2 * q, Z : Z + n] + got[2 * q :, :n]


def kernel_gradient(out_ref, own, sources):
    gap = jnp.zeros((48, Z), BF16)
    lhs = jnp.concatenate(
        [
            jnp.concatenate(
                [
                    jnp.concatenate([gap] * b + [rows] + [gap] * (2 - b), axis=1)
                    for b in range(3)
                ],
                axis=0,
            )
            for rows in own
        ],
        axis=1,
    )
    for a in range(3):
        rhs = jnp.concatenate(
            [jnp.concatenate([s[H + i + a - 1, :, RING] for s in sources], axis=0) for i in range(B)],
            axis=1,
        )
        got = lax.dot_general(lhs, rhs, (((1,), (1,)), ((), ())), preferred_element_type=F32)
        rows = slice(144 * a, 144 * (a + 1))
        out_ref[rows, : got.shape[1]] = got.astype(out_ref.dtype)
        if got.shape[1] < Z:
            out_ref[rows, got.shape[1] :] = jnp.zeros((144, Z - got.shape[1]), out_ref.dtype)


def own_cells(spread_ref):
    return [spread_ref[H + i, :, MID] for i in range(B)]


def activate(value):
    sigmoid = jax.nn.sigmoid(value)
    return 0.2 * value + 0.8 * value * sigmoid, 0.2 + 0.8 * (
        sigmoid + value * sigmoid * (1.0 - sigmoid)
    )


def assemble(parts, frame):
    before, top, bottom, after, left, right = parts
    frame[0:2, :, MID] = before[...]
    frame[2:4, :, MID] = top[...]
    frame[4:6, :, MID] = bottom[...]
    frame[6:8, :, MID] = after[...]
    frame[:, :, : H * Z] = left[...]
    frame[:, :, (H + B) * Z :] = right[...]


def wide_sum(blocks):
    total = sum(block.astype(F32) for block in blocks)
    return jnp.broadcast_to(jnp.sum(total, axis=1, keepdims=True), (total.shape[0], Z))


def cell_sum(own):
    return wide_sum([rows[16:32] for rows in own])


def pack_kernel(x_ref, top_ref, bottom_ref, wide):
    wide[...] = x_ref[...].astype(F32)
    for i in range(B):
        out = top_ref if i < 2 else bottom_ref
        for j in range(B):
            got = wide[pl.ds(B * i + j, 64, stride=B * B), :]
            out[i % 2, :, j * Z : (j + 1) * Z] = got.astype(BF16)


def columns_kernel(before, top, bottom, after, left, right):
    for r, ref in enumerate((before, top, bottom, after)):
        left[2 * r : 2 * r + 2] = ref[:, :, : H * Z]
        right[2 * r : 2 * r + 2] = ref[:, :, (B - H) * Z :]


def prepare_kernel(cot_ref, merge_t, k0, k1, k2, k3, base, carried, merge_grad, w0, w1, w2, w3, t0, t1, t2, t3, wide):
    for k_ref, w_ref, t_ref in ((k0, w0, t0), (k1, w1, t1), (k2, w2, t2), (k3, w3, t3)):
        w_ref[...] = jnp.concatenate([k_ref[144 * a : 144 * (a + 1)] for a in range(3)], axis=1)
        for b in range(3):
            rows = [k_ref[48 * t : 48 * (t + 1)] for t in (b, 3 + b, 6 + b)]
            t_ref[b] = jnp.transpose(jnp.concatenate(rows, axis=0).astype(F32)).astype(BF16)
    wide[...] = cot_ref[...].astype(F32)
    for i in range(B):
        cot = jnp.concatenate(
            [wide[pl.ds(B * i + j, 64, stride=B * B), :] for j in range(B)], axis=1
        )
        grad = (BETA * cot).astype(BF16)
        merge_grad[i] = grad
        back = jnp.dot(merge_t[...], grad, preferred_element_type=F32)
        base[i] = cot + back[:64]
        carried[i] = back[64:]


def first_kernel(
    before, top, bottom, after, left, right, k0, k1, bias, mask,
    frame, hidden_0, slope_0, slope_1, send_top, send_bottom,
):
    assemble((before, top, bottom, after, left, right), frame)

    def ring(i, carry):
        pre = conv_row(k0, [frame], i, RING) + bias[0:16, 0:1]
        value, slope = activate(pre)
        slope_0[i] = slope
        hidden_0[i, :, RING] = (value * mask[pl.ds(i, 1), RING]).astype(BF16)
        return carry

    lax.fori_loop(H - 1, H + B + 1, ring, 0)
    for i in range(B):
        pre = conv_row(k1, [frame, hidden_0], H + i, MID) + bias[16:32, 0:1]
        value, slope = activate(pre)
        slope_1[i] = slope
        send = send_top if i < 2 else send_bottom
        send[i % 2, 0:16] = hidden_0[H + i, :, MID]
        send[i % 2, 16:32] = value.astype(BF16)


def second_kernel(
    before, top, bottom, after, left, right, frame, k2, k3, bias, mask, carried,
    hidden_01, hidden_2, hidden_3, slope_2, own_3, send_top, send_bottom,
):
    assemble((before, top, bottom, after, left, right), hidden_01)

    def ring(i, carry):
        pre = conv_row(k2, [frame, hidden_01], i, RING) + bias[32:48, 0:1]
        value, slope = activate(pre)
        slope_2[i] = slope
        hidden_2[i, :, RING] = (value * mask[pl.ds(i, 1), RING]).astype(BF16)
        return carry

    lax.fori_loop(H - 1, H + B + 1, ring, 0)
    for i in range(B):
        pre = conv_row(k3, [frame, hidden_01, hidden_2], H + i, MID) + bias[48:64, 0:1]
        value, slope = activate(pre)
        hidden_3[i] = value.astype(BF16)
        grad = (carried[i, 48:64] * slope).astype(BF16)
        own_3[i] = spread(grad.astype(F32))
        send = send_top if i < 2 else send_bottom
        send[i % 2, 0:16] = grad
        send[i % 2, 16:32] = carried[i, 32:48].astype(BF16)


def merge_kernel(
    frame, hidden_01, hidden_2, hidden_3, own_3, merge, merge_bias, merge_grad,
    out_ref, grad_3, grad_merge,
):
    total = jnp.zeros((64, 128), F32)
    for i in range(B):
        base = frame[H + i, :, MID]
        joined = jnp.concatenate(
            [base, hidden_01[H + i, :, MID], hidden_2[H + i, :, MID], hidden_3[i]], axis=0
        )
        merged = jnp.dot(merge[...], joined, preferred_element_type=F32) + merge_bias[:, 0:1]
        out = base.astype(F32) + BETA * merged
        for j in range(B):
            out_ref[pl.ds(B * i + j, 64, stride=B * B), :] = out[:, j * Z : (j + 1) * Z]
        grad = merge_grad[i]
        total = total + lax.dot_general(
            grad, joined, (((1,), (1,)), ((), ())), preferred_element_type=F32
        )
    grad_merge[0:64] = total
    grad_merge[64:128] = wide_sum([merge_grad[i] for i in range(B)])
    own = [own_3[i] for i in range(B)]
    grad_merge[128:144] = cell_sum(own)
    kernel_gradient(grad_3, own, [frame, hidden_01, hidden_2])


def third_kernel(
    before, top, bottom, after, left, right, t2, t3, slope_1, slope_2, mask, carried,
    spread_3, spread_2, own_1, send_top, send_bottom, pieces, held,
):
    assemble((before, top, bottom, after, left, right), pieces)
    held[...] = pieces[:, 16:32, :].astype(F32)
    for i in range(B):
        held[H + i, :, MID] = carried[i, 32:48]

    def move(i, carry):
        spread_3[i] = spread(pieces[i, 0:16].astype(F32))
        return carry

    lax.fori_loop(0, N, move, 0)

    def ring(i, carry):
        got = held[i, :, RING] + back_row(t3, slice(96, 112), spread_3, i, RING)
        grad = (got * slope_2[i] * mask[pl.ds(i, 1), RING]).astype(BF16)
        spread_2[i, :, RING] = spread(grad.astype(F32))
        return carry

    lax.fori_loop(H - 1, H + B + 1, ring, 0)
    for i in range(B):
        got = (
            carried[i, 16:32]
            + back_row(t3, slice(80, 96), spread_3, H + i, MID)
            + back_row(t2, slice(80, 96), spread_2, H + i, MID)
        )
        grad = (got * slope_1[i]).astype(BF16)
        own_1[i] = spread(grad.astype(F32))
        send = send_top if i < 2 else send_bottom
        send[i % 2, 0:16] = spread_2[H + i, 16:32, MID]
        send[i % 2, 16:32] = grad
        send[i % 2, 32:48] = carried[i, 0:16].astype(BF16)


def beside_kernel(
    frame, hidden_01, spread_3, spread_2, own_1, t3, base,
    grad_2, grad_1, grad_bias, part_0, part_base,
):
    own = [own_1[i] for i in range(B)]
    grad_bias[0:16] = cell_sum(own)
    kernel_gradient(grad_1, own, [frame, hidden_01.at[:, 0:16, :]])
    own = own_cells(spread_2)
    grad_bias[16:32] = cell_sum(own)
    kernel_gradient(grad_2, own, [frame, hidden_01])

    def ring(i, carry):
        part_0[i] = back_row(t3, slice(64, 80), spread_3, i, RING)
        return carry

    lax.fori_loop(H - 1, H + B + 1, ring, 0)
    for i in range(B):
        part_base[i] = base[i] + back_row(t3, slice(0, 64), spread_3, H + i, MID)


def fourth_kernel(
    before, top, bottom, after, left, right, t1, t2, slope_0, mask, carried, part_0, frame,
    grad_1, grad_2, grad_3, grad_merge, grad_bias,
    place, spread_2, spread_1, spread_0, kept, sent, sums, pieces, held,
):
    assemble((before, top, bottom, after, left, right), pieces)
    held[...] = pieces[:, 32:48, :].astype(F32)
    for i in range(B):
        held[H + i, :, MID] = carried[i, 0:16]

    def move(i, carry):
        spread_2[i] = spread(pieces[i, 0:16].astype(F32))
        spread_1[i] = spread(pieces[i, 16:32].astype(F32))
        return carry

    lax.fori_loop(0, N, move, 0)

    def ring(i, carry):
        got = (
            held[i, :, RING]
            + part_0[i]
            + back_row(t2, slice(64, 80), spread_2, i, RING)
            + back_row(t1, slice(64, 80), spread_1, i, RING)
        )
        grad = (got * slope_0[i] * mask[pl.ds(i, 1), RING]).astype(BF16)
        spread_0[i, :, RING] = spread(grad.astype(F32))
        return carry

    lax.fori_loop(H - 1, H + B + 1, ring, 0)
    own = own_cells(spread_0)
    kernel_gradient(sums.at[0:432], own, [frame])
    sums[432:864] = grad_1[...]
    sums[864:1296] = grad_2[...]
    sums[1296:1728] = grad_3[...]
    sums[1728:1856] = grad_merge[0:128]
    sums[1856:1872] = cell_sum(own)
    sums[1872:1904] = grad_bias[...]
    sums[1904:1920] = grad_merge[128:144]
    sums[1920:] = jnp.zeros((2 * HALF - 1920, Z), F32)
    mine = pl.multiple_of(place[0] * HALF, HALF)
    other = pl.multiple_of(HALF - place[0] * HALF, HALF)
    kept[...] = sums[pl.ds(mine, HALF), :]
    sent[...] = sums[pl.ds(other, HALF), :].astype(BF16)


def last_kernel(spread_2, spread_1, spread_0, t0, t1, t2, part_base, out_ref):
    for i in range(B):
        out = (
            part_base[i]
            + back_row(t2, slice(0, 64), spread_2, H + i, MID)
            + back_row(t1, slice(0, 64), spread_1, H + i, MID)
            + back_row(t0, slice(0, 64), spread_0, H + i, MID)
        )
        for j in range(B):
            out_ref[pl.ds(B * i + j, 64, stride=B * B), :] = out[:, j * Z : (j + 1) * Z]


def pair_kernel(kept, came, out_ref):
    out_ref[...] = (kept[...] + came[...].astype(F32)).astype(BF16)


def add_kernel(x_ref, out_ref):
    def step(k, acc):
        return acc + x_ref[pl.ds(pl.multiple_of(k * 128, 128), 128), :].astype(F32)

    acc = lax.fori_loop(0, HALF // 128, step, jnp.zeros((128, Z), F32))
    total = acc[0:ROWS]
    for k in range(1, 128 // ROWS):
        total = total + acc[k * ROWS : (k + 1) * ROWS]
    block = jnp.concatenate([total] * (128 // ROWS), axis=0).astype(BF16)

    def put(k, carry):
        out_ref[pl.ds(pl.multiple_of(k * 128, 128), 128), :] = block
        return carry

    lax.fori_loop(0, HALF // 128, put, 0)


def turned(block):
    rows = lax.broadcasted_iota(jnp.int32, block.shape, 0)
    lanes = lax.broadcasted_iota(jnp.int32, block.shape, 1)
    return jnp.sum(jnp.where(rows == lanes, block, 0.0), axis=0, keepdims=True)


def unpack_kernel(scale, mine, other, place, g0, g1, g2, g3, bias, weight, weight_bias, sums):
    sums[pl.ds(pl.multiple_of(place[0] * HALF, HALF), HALF), :] = mine[...].astype(F32) * scale
    sums[pl.ds(pl.multiple_of(HALF - place[0] * HALF, HALF), HALF), :] = (
        other[...].astype(F32) * scale
    )
    for k, g in enumerate((g0, g1, g2, g3)):
        g[...] = sums[432 * k : 432 * (k + 1), : g.shape[1]]
    weight[...] = sums[1728:1792]
    weight_bias[...] = turned(sums[1792:1856])[:, :64]
    for k in range(4):
        bias[k : k + 1] = turned(sums[1856 + 16 * k : 1872 + 16 * k])[:, :16]


def exchange(top, bottom):
    channels = top.shape[1]
    up = [(i, i + 1) for i in range(lax.axis_size("gx") - 1)]
    before = lax.ppermute(bottom, "gx", up)
    after = lax.ppermute(top, "gx", [(j, i) for i, j in up])
    side = shape((N, channels, H * Z), BF16)
    left, right = call(
        columns_kernel, [side, side], [before, top, bottom, after], name="columns"
    )
    up = [(i, i + 1) for i in range(lax.axis_size("row") - 1)]
    from_before = lax.ppermute(right, "row", up)
    from_after = lax.ppermute(left, "row", [(j, i) for i, j in up])
    return [before, top, bottom, after, from_before, from_after]


def grid_mask():
    steps = jnp.arange(N) - H
    gx = lax.axis_index("gx") * B + steps
    gy = lax.axis_index("row") * B + steps
    inside_x = (gx >= 0) & (gx < lax.axis_size("gx") * B)
    inside_y = (gy >= 0) & (gy < lax.axis_size("row") * B)
    inside = (inside_x[:, None] & inside_y[None, :]).astype(F32)
    return jnp.repeat(inside, Z, axis=1)


def body(samples, cotangent, kernel_0, kernel_1, kernel_2, kernel_3, layer_bias, merging_weight, merging_bias):
    kernels = (kernel_0, kernel_1, kernel_2, kernel_3)
    cells = B * B * Z * lax.axis_size("gx") * lax.axis_size("row") * lax.axis_size("rep")
    scale = 1.0 / math.sqrt(cells)
    flat = [k.transpose(1, 0, 2).reshape(432, k.shape[2]) for k in kernels]
    bias = jnp.broadcast_to(layer_bias.astype(F32).reshape(64, 1), (64, Z))
    merge_bias = jnp.broadcast_to(merging_bias.astype(F32)[:, None], (64, Z))
    mask = grid_mask()
    half = shape((2, 64, B * Z), BF16)
    wide = pltpu.VMEM((1024, Z), F32)
    top, bottom = call(
        pack_kernel, [half, half], [samples.reshape(1024, Z)], [wide], name="pack"
    )
    place = lax.axis_index("rep").astype(jnp.int32).reshape(1)
    base, carried, merge_grad, w0, w1, w2, w3, t0, t1, t2, t3 = call(
        prepare_kernel,
        [shape((B, 64, B * Z), F32)] * 2
        + [shape((B, 64, B * Z), BF16)]
        + [shape((144, 3 * k.shape[2]), BF16) for k in kernels]
        + [shape((3, k.shape[2], 144), BF16) for k in kernels],
        [cotangent.reshape(1024, Z), merging_weight.T] + flat,
        [wide],
        flops=40_000_000,
        name="prepare",
    )
    parts = exchange(top, bottom)
    ring = shape((N, 16, (B + 2) * Z), F32)
    send = shape((2, 32, B * Z), BF16)
    frame, hidden_0, slope_0, slope_1, top, bottom = call(
        first_kernel,
        [shape((N, 64, N * Z), BF16), shape((N, 16, N * Z), BF16), ring, shape((B, 16, B * Z), F32), send, send],
        parts + [w0, w1, bias, mask],
        name="layers_0_1",
    )
    parts = exchange(top, bottom)
    hidden_01, hidden_2, hidden_3, slope_2, own_3, top, bottom = call(
        second_kernel,
        [
            shape((N, 32, N * Z), BF16),
            shape((N, 16, N * Z), BF16),
            shape((B, 16, B * Z), BF16),
            ring,
            shape((B, 48, B * Z), BF16),
            send,
            send,
        ],
        parts + [frame, w2, w3, bias, mask, carried],
        name="layers_2_3",
    )
    parts = exchange(top, bottom)
    grads = shape((432, Z), F32)
    output, grad_3, grad_merge = call(
        merge_kernel,
        [shape((1024, Z), F32), grads, shape((144, Z), F32)],
        [frame, hidden_01, hidden_2, hidden_3, own_3, merging_weight, merge_bias, merge_grad],
        flops=100_000_000,
        name="merge",
    )
    send = shape((2, 48, B * Z), BF16)
    spreads = shape((N, 48, N * Z), BF16)
    spread_3, spread_2, own_1, top, bottom = call(
        third_kernel,
        [spreads, spreads, shape((B, 48, B * Z), BF16), send, send],
        parts + [t2, t3, slope_1, slope_2, mask, carried],
        [pltpu.VMEM((N, 32, N * Z), BF16), pltpu.VMEM((N, 16, N * Z), F32)],
        name="gradients_2_1",
    )
    parts = exchange(top, bottom)
    grad_2, grad_1, grad_bias, part_0, part_base = call(
        beside_kernel,
        [grads, grads, shape((32, Z), F32), ring, shape((B, 64, B * Z), F32)],
        [frame, hidden_01, spread_3, spread_2, own_1, t3, base],
        flops=200_000_000,
        name="kernel_gradients_2_1",
    )
    spread_2, spread_1, spread_0, kept, sent = call(
        fourth_kernel,
        [spreads, spreads, spreads, shape((HALF, Z), F32), shape((HALF, Z), BF16)],
        parts
        + [t1, t2, slope_0, mask, carried, part_0, frame]
        + [grad_1, grad_2, grad_3, grad_merge, grad_bias, place],
        [pltpu.VMEM((2 * HALF, Z), F32), pltpu.VMEM((N, 48, N * Z), BF16), pltpu.VMEM((N, 16, N * Z), F32)],
        name="gradient_0",
    )
    axes = ("gx", "row")
    swap = [(0, 1), (1, 0)]
    half_sum = shape((HALF, Z), BF16)
    (paired,) = call(pair_kernel, [half_sum], [kept, lax.ppermute(sent, "rep", swap)], name="pair")
    spread_sums = lax.all_to_all(paired.reshape(GROUP, ROWS, Z), axes, 0, 0, tiled=True)
    (added,) = call(add_kernel, [half_sum], [spread_sums.reshape(HALF, Z)], name="add")
    totals = lax.all_to_all(added.reshape(GROUP, ROWS, Z), axes, 0, 0, tiled=True)
    totals = totals.reshape(HALF, Z)
    others = lax.ppermute(totals, "rep", swap)
    (grad_input,) = call(
        last_kernel,
        [shape((1024, Z), F32)],
        [spread_2, spread_1, spread_0, t0, t1, t2, part_base],
        flops=300_000_000,
        name="input_gradient",
    )
    unpacked = call(
        functools.partial(unpack_kernel, scale),
        [shape((432, k.shape[2]), F32) for k in kernels]
        + [shape((4, 16), F32), shape((64, 128), F32), shape((1, 64), F32)],
        [totals, others, place],
        [pltpu.VMEM((2 * HALF, Z), F32)],
        name="unpack",
    )
    grad_kernels = [g.reshape(27, 16, g.shape[1]).transpose(1, 0, 2) for g in unpacked[:4]]
    out_shape = (1, 64, B, B, Z)
    return (
        output.reshape(out_shape),
        grad_input.reshape(out_shape),
        *grad_kernels,
        unpacked[4],
        unpacked[5],
        unpacked[6].reshape(64),
    )


def solution(mesh):
    split = P("rep", None, "gx", "row", None)
    return jax.shard_map(
        body,
        mesh=mesh,
        in_specs=(split, split) + (P(),) * 7,
        out_specs=(split, split) + (P(),) * 7,
        check_vma=False,
    )
```

```python
import functools
import math

import jax
import jax.numpy as jnp
from jax import lax
from jax.experimental import pallas as pl
from jax.experimental.pallas import tpu as pltpu
from jax.sharding import PartitionSpec as P

BETA = 0.2
BF16, F32 = jnp.bfloat16, jnp.float32
Z = 128
B = 4
H = 2
N = B + 2 * H
MID = slice(H * Z, (H + B) * Z)
RING = slice((H - 1) * Z, (H + B + 1) * Z)
GROUP = 128
ROWS = 8
HALF = GROUP * ROWS
VMEM_LIMIT = 24 * 2**20


def shape(dims, dtype):
    return jax.ShapeDtypeStruct(dims, dtype)


def call(kernel, outs, args, scratch=(), flops=1_000_000, name=None):
    moved = sum(math.prod(a.shape) * a.dtype.itemsize for a in list(args) + list(outs))
    return pl.pallas_call(
        kernel,
        out_shape=list(outs),
        in_specs=[pl.BlockSpec(memory_space=pltpu.VMEM)] * len(args),
        out_specs=[pl.BlockSpec(memory_space=pltpu.VMEM)] * len(outs),
        scratch_shapes=list(scratch),
        compiler_params=pltpu.CompilerParams(vmem_limit_bytes=VMEM_LIMIT),
        cost_estimate=pl.CostEstimate(flops=flops, bytes_accessed=moved, transcendentals=0),
        name=name,
    )(*args)


def lane_moves(rows, width):
    lane = lax.broadcasted_iota(jnp.int32, (rows, width), 1) % Z
    return lane != 0, lane != Z - 1


def from_left(v, keep):
    return jnp.where(keep, pltpu.roll(v, 1, 1), 0.0)


def from_right(v, keep):
    return jnp.where(keep, pltpu.roll(v, v.shape[1] - 1, 1), 0.0)


def one_cell_moves():
    row = lax.broadcasted_iota(jnp.int32, (Z, 2 * Z), 0)
    lane = lax.broadcasted_iota(jnp.int32, (Z, 2 * Z), 1)
    return jnp.where((row == lane + 1) | (row == lane - Z - 1), 1.0, 0.0).astype(BF16)


def spread(v, moves):
    blocks = v.shape[1] // Z
    tall = jnp.concatenate([v[:, k * Z : (k + 1) * Z] for k in range(blocks)], axis=0)
    got = jnp.dot(tall, moves, preferred_element_type=F32).astype(BF16)
    later, earlier = (
        jnp.concatenate([half[16 * k : 16 * (k + 1)] for k in range(blocks)], axis=1)
        for half in (got[:, :Z], got[:, Z:])
    )
    return jnp.concatenate([later, v, earlier], axis=0)


def inside(i):
    x = lax.axis_index("gx") * B + i - H
    block = lax.broadcasted_iota(jnp.int32, (1, (B + 2) * Z), 1) // Z
    y = lax.axis_index("row") * B + block + 1 - H
    in_x = (x >= 0) & (x < lax.axis_size("gx") * B)
    in_y = (y >= 0) & (y < lax.axis_size("row") * B)
    return jnp.where(in_y, 1.0, 0.0) * jnp.where(in_x, 1.0, 0.0)


def as_column(row):
    n = row.shape[1]
    rows = lax.broadcasted_iota(jnp.int32, (n, n), 0)
    lanes = lax.broadcasted_iota(jnp.int32, (n, n), 1)
    return jnp.sum(jnp.where(rows == lanes, row, 0.0), axis=1, keepdims=True)


def conv_row(kernel_ref, sources, i, lanes):
    n = lanes.stop - lanes.start
    cut = slice(lanes.start - Z, lanes.stop + Z)
    rhs = jnp.concatenate([s[i + a - 1, :, cut] for a in range(3) for s in sources], axis=0)
    got = jnp.dot(kernel_ref[...], rhs, preferred_element_type=F32)
    acc = got[:48, :n] + got[48:96, Z : Z + n] + got[96:, 2 * Z :]
    not_first, not_last = lane_moves(16, n)
    return from_left(acc[:16], not_first) + acc[16:32] + from_right(acc[32:], not_last)


def back_row(turned_ref, channels, spread_ref, i, lanes):
    n, q = lanes.stop - lanes.start, channels.stop - channels.start
    cut = slice(lanes.start - Z, lanes.stop + Z)
    lhs = jnp.concatenate([turned_ref[b, channels] for b in range(3)], axis=0)
    rhs = jnp.concatenate([spread_ref[i + 1 - a, :, cut] for a in range(3)], axis=0)
    got = jnp.dot(lhs, rhs, preferred_element_type=F32)
    return got[:q, 2 * Z :] + got[q : 2 * q, Z : Z + n] + got[2 * q :, :n]


def kernel_gradient(out_ref, own, sources):
    gap = jnp.zeros((48, Z), BF16)
    lhs = jnp.concatenate(
        [
            jnp.concatenate(
                [
                    jnp.concatenate([gap] * b + [rows] + [gap] * (2 - b), axis=1)
                    for b in range(3)
                ],
                axis=0,
            )
            for rows in own
        ],
        axis=1,
    )
    for a in range(3):
        rhs = jnp.concatenate(
            [jnp.concatenate([s[H + i + a - 1, :, RING] for s in sources], axis=0) for i in range(B)],
            axis=1,
        )
        got = lax.dot_general(lhs, rhs, (((1,), (1,)), ((), ())), preferred_element_type=F32)
        rows = slice(144 * a, 144 * (a + 1))
        out_ref[rows, : got.shape[1]] = got.astype(out_ref.dtype)
        if got.shape[1] < Z:
            out_ref[rows, got.shape[1] :] = jnp.zeros((144, Z - got.shape[1]), out_ref.dtype)


def own_cells(spread_ref):
    return [spread_ref[H + i, :, MID] for i in range(B)]


def activate(value):
    sigmoid = jax.nn.sigmoid(value)
    return 0.2 * value + 0.8 * value * sigmoid, 0.2 + 0.8 * (
        sigmoid + value * sigmoid * (1.0 - sigmoid)
    )


def assemble(parts, frame):
    before, left, right, after, above, below = parts
    own = slice(H, H + B)
    frame[own, :, : H * Z] = before[...]
    frame[own, :, H * Z : 2 * H * Z] = left[...]
    frame[own, :, 2 * H * Z : 3 * H * Z] = right[...]
    frame[own, :, 3 * H * Z :] = after[...]
    frame[:H] = above[...]
    frame[H + B :] = below[...]


def put(pair, i, rows, value):
    left, right = pair
    left[i, rows] = value[:, : H * Z]
    right[i, rows] = value[:, H * Z :]


def wide_sum(blocks):
    total = sum(block.astype(F32) for block in blocks)
    return jnp.broadcast_to(jnp.sum(total, axis=1, keepdims=True), (total.shape[0], Z))


def cell_sum(own):
    return wide_sum([rows[16:32] for rows in own])


def pack_kernel(x_ref, layer_bias, merging_bias, left, right, bias, merge_bias, wide):
    wide[...] = x_ref[...].astype(F32)
    for i in range(B):
        row = [wide[pl.ds(B * i + j, 64, stride=B * B), :].astype(BF16) for j in range(B)]
        put((left, right), i, slice(0, 64), jnp.concatenate(row, axis=1))
    for k in range(4):
        column = as_column(layer_bias[k : k + 1].astype(F32))
        bias[16 * k : 16 * (k + 1)] = jnp.broadcast_to(column, (16, Z))
    merge_bias[...] = jnp.broadcast_to(as_column(merging_bias[...].astype(F32)), (64, Z))


def rows_kernel(before, left, right, after, top, bottom):
    for k, ref in enumerate((before, left, right, after)):
        lanes = slice(k * H * Z, (k + 1) * H * Z)
        top[:, :, lanes] = ref[:H]
        bottom[:, :, lanes] = ref[B - H :]


def prepare_kernel(cot_ref, merge, k0, k1, k2, k3, base, carried, merge_grad, w0, w1, w2, w3, t0, t1, t2, t3, wide):
    for k_ref, w_ref, t_ref in ((k0, w0, t0), (k1, w1, t1), (k2, w2, t2), (k3, w3, t3)):
        w_ref[...] = jnp.concatenate([k_ref[144 * a : 144 * (a + 1)] for a in range(3)], axis=1)
        for b in range(3):
            rows = [k_ref[48 * t : 48 * (t + 1)] for t in (b, 3 + b, 6 + b)]
            t_ref[b] = jnp.transpose(jnp.concatenate(rows, axis=0).astype(F32)).astype(BF16)
    wide[...] = cot_ref[...].astype(F32)
    merge_t = jnp.transpose(merge[...].astype(F32)).astype(BF16)
    for i in range(B):
        cot = jnp.concatenate(
            [wide[pl.ds(B * i + j, 64, stride=B * B), :] for j in range(B)], axis=1
        )
        grad = (BETA * cot).astype(BF16)
        merge_grad[i] = grad
        back = jnp.dot(merge_t, grad, preferred_element_type=F32)
        base[i] = cot + back[:64]
        carried[i] = back[64:]


def first_kernel(
    before, left, right, after, above, below, k0, k1, bias,
    frame, hidden_0, slope_0, slope_1, send_left, send_right,
):
    assemble((before, left, right, after, above, below), frame)

    def ring(i, carry):
        pre = conv_row(k0, [frame], i, RING) + bias[0:16, 0:1]
        value, slope = activate(pre)
        slope_0[i] = slope
        hidden_0[i, :, RING] = (value * inside(i)).astype(BF16)
        return carry

    lax.fori_loop(H - 1, H + B + 1, ring, 0)
    for i in range(B):
        pre = conv_row(k1, [frame, hidden_0], H + i, MID) + bias[16:32, 0:1]
        value, slope = activate(pre)
        slope_1[i] = slope
        put((send_left, send_right), i, slice(0, 16), hidden_0[H + i, :, MID])
        put((send_left, send_right), i, slice(16, 32), value.astype(BF16))


def second_kernel(
    before, left, right, after, above, below, frame, k2, k3, bias, carried,
    hidden_01, hidden_2, hidden_3, slope_2, own_3, send_left, send_right,
):
    assemble((before, left, right, after, above, below), hidden_01)
    moves = one_cell_moves()

    def ring(i, carry):
        pre = conv_row(k2, [frame, hidden_01], i, RING) + bias[32:48, 0:1]
        value, slope = activate(pre)
        slope_2[i] = slope
        hidden_2[i, :, RING] = (value * inside(i)).astype(BF16)
        return carry

    lax.fori_loop(H - 1, H + B + 1, ring, 0)
    for i in range(B):
        pre = conv_row(k3, [frame, hidden_01, hidden_2], H + i, MID) + bias[48:64, 0:1]
        value, slope = activate(pre)
        hidden_3[i] = value.astype(BF16)
        grad = (carried[i, 48:64] * slope).astype(BF16)
        own_3[i] = spread(grad, moves)
        put((send_left, send_right), i, slice(0, 16), grad)
        put((send_left, send_right), i, slice(16, 32), carried[i, 32:48].astype(BF16))


def merge_kernel(
    frame, hidden_01, hidden_2, hidden_3, own_3, merge, merge_bias, merge_grad,
    out_ref, grad_3, grad_merge,
):
    total = jnp.zeros((64, 128), F32)
    for i in range(B):
        base = frame[H + i, :, MID]
        joined = jnp.concatenate(
            [base, hidden_01[H + i, :, MID], hidden_2[H + i, :, MID], hidden_3[i]], axis=0
        )
        merged = jnp.dot(merge[...], joined, preferred_element_type=F32) + merge_bias[:, 0:1]
        out = base.astype(F32) + BETA * merged
        for j in range(B):
            out_ref[pl.ds(B * i + j, 64, stride=B * B), :] = out[:, j * Z : (j + 1) * Z]
        grad = merge_grad[i]
        total = total + lax.dot_general(
            grad, joined, (((1,), (1,)), ((), ())), preferred_element_type=F32
        )
    grad_merge[0:64] = total
    grad_merge[64:128] = wide_sum([merge_grad[i] for i in range(B)])
    own = [own_3[i] for i in range(B)]
    grad_merge[128:144] = cell_sum(own)
    kernel_gradient(grad_3, own, [frame, hidden_01, hidden_2])


def third_kernel(
    before, left, right, after, above, below, t2, t3, slope_1, slope_2, carried,
    spread_3, spread_2, own_1, send_left, send_right, pieces, held,
):
    assemble((before, left, right, after, above, below), pieces)
    moves = one_cell_moves()
    held[...] = pieces[:, 16:32, :].astype(F32)
    for i in range(B):
        held[H + i, :, MID] = carried[i, 32:48]

    def move(i, carry):
        spread_3[i] = spread(pieces[i, 0:16], moves)
        return carry

    lax.fori_loop(0, N, move, 0)

    def ring(i, carry):
        got = held[i, :, RING] + back_row(t3, slice(96, 112), spread_3, i, RING)
        grad = (got * slope_2[i] * inside(i)).astype(BF16)
        spread_2[i, :, RING] = spread(grad, moves)
        return carry

    lax.fori_loop(H - 1, H + B + 1, ring, 0)
    for i in range(B):
        got = (
            carried[i, 16:32]
            + back_row(t3, slice(80, 96), spread_3, H + i, MID)
            + back_row(t2, slice(80, 96), spread_2, H + i, MID)
        )
        grad = (got * slope_1[i]).astype(BF16)
        own_1[i] = spread(grad, moves)
        put((send_left, send_right), i, slice(0, 16), spread_2[H + i, 16:32, MID])
        put((send_left, send_right), i, slice(16, 32), grad)
        put((send_left, send_right), i, slice(32, 48), carried[i, 0:16].astype(BF16))


def beside_kernel(
    frame, hidden_01, spread_3, spread_2, own_1, t3, base,
    grad_2, grad_1, grad_bias, part_0, part_base,
):
    own = [own_1[i] for i in range(B)]
    grad_bias[0:16] = cell_sum(own)
    kernel_gradient(grad_1, own, [frame, hidden_01.at[:, 0:16, :]])
    own = own_cells(spread_2)
    grad_bias[16:32] = cell_sum(own)
    kernel_gradient(grad_2, own, [frame, hidden_01])

    def ring(i, carry):
        part_0[i] = back_row(t3, slice(64, 80), spread_3, i, RING)
        return carry

    lax.fori_loop(H - 1, H + B + 1, ring, 0)
    for i in range(B):
        part_base[i] = base[i] + back_row(t3, slice(0, 64), spread_3, H + i, MID)


def fourth_kernel(
    before, left, right, after, above, below, t1, t2, slope_0, carried, part_0, frame,
    grad_1, grad_2, grad_3, grad_merge, grad_bias,
    spread_2, spread_1, spread_0, kept, sent, sums, pieces, held,
):
    assemble((before, left, right, after, above, below), pieces)
    moves = one_cell_moves()
    held[...] = pieces[:, 32:48, :].astype(F32)
    for i in range(B):
        held[H + i, :, MID] = carried[i, 0:16]

    def move(i, carry):
        spread_2[i] = spread(pieces[i, 0:16], moves)
        spread_1[i] = spread(pieces[i, 16:32], moves)
        return carry

    lax.fori_loop(0, N, move, 0)

    def ring(i, carry):
        got = (
            held[i, :, RING]
            + part_0[i]
            + back_row(t2, slice(64, 80), spread_2, i, RING)
            + back_row(t1, slice(64, 80), spread_1, i, RING)
        )
        grad = (got * slope_0[i] * inside(i)).astype(BF16)
        spread_0[i, :, RING] = spread(grad, moves)
        return carry

    lax.fori_loop(H - 1, H + B + 1, ring, 0)
    own = own_cells(spread_0)
    kernel_gradient(sums.at[0:432], own, [frame])
    sums[432:864] = grad_1[...]
    sums[864:1296] = grad_2[...]
    sums[1296:1728] = grad_3[...]
    sums[1728:1856] = grad_merge[0:128]
    sums[1856:1872] = cell_sum(own)
    sums[1872:1904] = grad_bias[...]
    sums[1904:1920] = grad_merge[128:144]
    sums[1920:] = jnp.zeros((2 * HALF - 1920, Z), F32)
    mine, other = halves()
    kept[...] = sums[pl.ds(mine, HALF), :]
    sent[...] = sums[pl.ds(other, HALF), :].astype(BF16)


def last_kernel(spread_2, spread_1, spread_0, t0, t1, t2, part_base, out_ref):
    for i in range(B):
        out = (
            part_base[i]
            + back_row(t2, slice(0, 64), spread_2, H + i, MID)
            + back_row(t1, slice(0, 64), spread_1, H + i, MID)
            + back_row(t0, slice(0, 64), spread_0, H + i, MID)
        )
        for j in range(B):
            out_ref[pl.ds(B * i + j, 64, stride=B * B), :] = out[:, j * Z : (j + 1) * Z]


def halves():
    first = lax.axis_index("rep") * HALF
    return pl.multiple_of(first, HALF), pl.multiple_of(HALF - first, HALF)


def pair_kernel(kept, came, out_ref):
    out_ref[...] = (kept[...] + came[...].astype(F32)).astype(BF16)


def add_kernel(x_ref, out_ref):
    def step(k, acc):
        return acc + x_ref[pl.ds(pl.multiple_of(k * 128, 128), 128), :].astype(F32)

    acc = lax.fori_loop(0, HALF // 128, step, jnp.zeros((128, Z), F32))
    total = acc[0:ROWS]
    for k in range(1, 128 // ROWS):
        total = total + acc[k * ROWS : (k + 1) * ROWS]
    block = jnp.concatenate([total] * (128 // ROWS), axis=0).astype(BF16)

    def put(k, carry):
        out_ref[pl.ds(pl.multiple_of(k * 128, 128), 128), :] = block
        return carry

    lax.fori_loop(0, HALF // 128, put, 0)


def turned(block):
    rows = lax.broadcasted_iota(jnp.int32, block.shape, 0)
    lanes = lax.broadcasted_iota(jnp.int32, block.shape, 1)
    return jnp.sum(jnp.where(rows == lanes, block, 0.0), axis=0, keepdims=True)


def unpack_kernel(scale, mine_ref, other_ref, g0, g1, g2, g3, bias, weight, weight_bias, sums):
    mine, other = halves()
    sums[pl.ds(mine, HALF), :] = mine_ref[...].astype(F32) * scale
    sums[pl.ds(other, HALF), :] = other_ref[...].astype(F32) * scale
    for k, g in enumerate((g0, g1, g2, g3)):
        g[...] = sums[432 * k : 432 * (k + 1), : g.shape[1]]
    weight[...] = sums[1728:1792]
    weight_bias[...] = turned(sums[1792:1856])[:, :64]
    for k in range(4):
        bias[k : k + 1] = turned(sums[1856 + 16 * k : 1872 + 16 * k])[:, :16]


def exchange(left, right):
    channels = left.shape[1]
    up = [(i, i + 1) for i in range(lax.axis_size("row") - 1)]
    before = lax.ppermute(right, "row", up)
    after = lax.ppermute(left, "row", [(j, i) for i, j in up])
    edge = shape((H, channels, N * Z), BF16)
    top, bottom = call(rows_kernel, [edge, edge], [before, left, right, after], name="rows")
    up = [(i, i + 1) for i in range(lax.axis_size("gx") - 1)]
    above = lax.ppermute(bottom, "gx", up)
    below = lax.ppermute(top, "gx", [(j, i) for i, j in up])
    return [before, left, right, after, above, below]


def body(samples, cotangent, kernel_0, kernel_1, kernel_2, kernel_3, layer_bias, merging_weight, merging_bias):
    kernels = (kernel_0, kernel_1, kernel_2, kernel_3)
    cells = B * B * Z * lax.axis_size("gx") * lax.axis_size("row") * lax.axis_size("rep")
    scale = 1.0 / math.sqrt(cells)
    flat = [k.transpose(1, 0, 2).reshape(432, k.shape[2]) for k in kernels]
    half = shape((B, 64, H * Z), BF16)
    columns = shape((64, Z), F32)
    wide = pltpu.VMEM((1024, Z), F32)
    left, right, bias, merge_bias = call(
        pack_kernel,
        [half, half, columns, columns],
        [samples.reshape(1024, Z), layer_bias, merging_bias.reshape(1, 64)],
        [wide],
        name="pack",
    )
    base, carried, merge_grad, w0, w1, w2, w3, t0, t1, t2, t3 = call(
        prepare_kernel,
        [shape((B, 64, B * Z), F32)] * 2
        + [shape((B, 64, B * Z), BF16)]
        + [shape((144, 3 * k.shape[2]), BF16) for k in kernels]
        + [shape((3, k.shape[2], 144), BF16) for k in kernels],
        [cotangent.reshape(1024, Z), merging_weight] + flat,
        [wide],
        flops=40_000_000,
        name="prepare",
    )
    parts = exchange(left, right)
    ring = shape((N, 16, (B + 2) * Z), F32)
    send = shape((B, 32, H * Z), BF16)
    frame, hidden_0, slope_0, slope_1, left, right = call(
        first_kernel,
        [shape((N, 64, N * Z), BF16), shape((N, 16, N * Z), BF16), ring, shape((B, 16, B * Z), F32), send, send],
        parts + [w0, w1, bias],
        name="layers_0_1",
    )
    parts = exchange(left, right)
    hidden_01, hidden_2, hidden_3, slope_2, own_3, left, right = call(
        second_kernel,
        [
            shape((N, 32, N * Z), BF16),
            shape((N, 16, N * Z), BF16),
            shape((B, 16, B * Z), BF16),
            ring,
            shape((B, 48, B * Z), BF16),
            send,
            send,
        ],
        parts + [frame, w2, w3, bias, carried],
        name="layers_2_3",
    )
    parts = exchange(left, right)
    grads = shape((432, Z), F32)
    output, grad_3, grad_merge = call(
        merge_kernel,
        [shape((1024, Z), F32), grads, shape((144, Z), F32)],
        [frame, hidden_01, hidden_2, hidden_3, own_3, merging_weight, merge_bias, merge_grad],
        flops=100_000_000,
        name="merge",
    )
    send = shape((B, 48, H * Z), BF16)
    spreads = shape((N, 48, N * Z), BF16)
    spread_3, spread_2, own_1, left, right = call(
        third_kernel,
        [spreads, spreads, shape((B, 48, B * Z), BF16), send, send],
        parts + [t2, t3, slope_1, slope_2, carried],
        [pltpu.VMEM((N, 32, N * Z), BF16), pltpu.VMEM((N, 16, N * Z), F32)],
        name="gradients_2_1",
    )
    parts = exchange(left, right)
    grad_2, grad_1, grad_bias, part_0, part_base = call(
        beside_kernel,
        [grads, grads, shape((32, Z), F32), ring, shape((B, 64, B * Z), F32)],
        [frame, hidden_01, spread_3, spread_2, own_1, t3, base],
        flops=200_000_000,
        name="kernel_gradients_2_1",
    )
    spread_2, spread_1, spread_0, kept, sent = call(
        fourth_kernel,
        [spreads, spreads, spreads, shape((HALF, Z), F32), shape((HALF, Z), BF16)],
        parts
        + [t1, t2, slope_0, carried, part_0, frame]
        + [grad_1, grad_2, grad_3, grad_merge, grad_bias],
        [pltpu.VMEM((2 * HALF, Z), F32), pltpu.VMEM((N, 48, N * Z), BF16), pltpu.VMEM((N, 16, N * Z), F32)],
        name="gradient_0",
    )
    axes = ("gx", "row")
    swap = [(0, 1), (1, 0)]
    half_sum = shape((HALF, Z), BF16)
    (paired,) = call(pair_kernel, [half_sum], [kept, lax.ppermute(sent, "rep", swap)], name="pair")
    spread_sums = lax.all_to_all(paired.reshape(GROUP, ROWS, Z), axes, 0, 0, tiled=True)
    (added,) = call(add_kernel, [half_sum], [spread_sums.reshape(HALF, Z)], name="add")
    totals = lax.all_to_all(added.reshape(GROUP, ROWS, Z), axes, 0, 0, tiled=True)
    totals = totals.reshape(HALF, Z)
    others = lax.ppermute(totals, "rep", swap)
    (grad_input,) = call(
        last_kernel,
        [shape((1024, Z), F32)],
        [spread_2, spread_1, spread_0, t0, t1, t2, part_base],
        flops=300_000_000,
        name="input_gradient",
    )
    unpacked = call(
        functools.partial(unpack_kernel, scale),
        [shape((432, k.shape[2]), F32) for k in kernels]
        + [shape((4, 16), F32), shape((64, 128), F32), shape((1, 64), F32)],
        [totals, others],
        [pltpu.VMEM((2 * HALF, Z), F32)],
        name="unpack",
    )
    grad_kernels = [g.reshape(27, 16, g.shape[1]).transpose(1, 0, 2) for g in unpacked[:4]]
    out_shape = (1, 64, B, B, Z)
    return (
        output.reshape(out_shape),
        grad_input.reshape(out_shape),
        *grad_kernels,
        unpacked[4],
        unpacked[5],
        unpacked[6].reshape(64),
    )


def solution(mesh):
    split = P("rep", None, "gx", "row", None)
    return jax.shard_map(
        body,
        mesh=mesh,
        in_specs=(split, split) + (P(),) * 7,
        out_specs=(split, split) + (P(),) * 7,
        check_vma=False,
    )
```

```python
import functools
import math

import jax
import jax.numpy as jnp
from jax import lax
from jax.experimental import pallas as pl
from jax.experimental.pallas import tpu as pltpu
from jax.sharding import PartitionSpec as P

BETA = 0.2
BF16, F32 = jnp.bfloat16, jnp.float32
Z = 128
B = 4
H = 2
N = B + 2 * H
MID = slice(H * Z, (H + B) * Z)
RING = slice((H - 1) * Z, (H + B + 1) * Z)
GROUP = 128
ROWS = 8
HALF = GROUP * ROWS
VMEM_LIMIT = 24 * 2**20


def shape(dims, dtype):
    return jax.ShapeDtypeStruct(dims, dtype)


def call(kernel, outs, args, scratch=(), flops=1_000_000, name=None):
    moved = sum(math.prod(a.shape) * a.dtype.itemsize for a in list(args) + list(outs))
    return pl.pallas_call(
        kernel,
        out_shape=list(outs),
        in_specs=[pl.BlockSpec(memory_space=pltpu.VMEM)] * len(args),
        out_specs=[pl.BlockSpec(memory_space=pltpu.VMEM)] * len(outs),
        scratch_shapes=list(scratch),
        compiler_params=pltpu.CompilerParams(vmem_limit_bytes=VMEM_LIMIT),
        cost_estimate=pl.CostEstimate(flops=flops, bytes_accessed=moved, transcendentals=0),
        name=name,
    )(*args)


def lane_moves(rows, width):
    lane = lax.broadcasted_iota(jnp.int32, (rows, width), 1) % Z
    return lane != 0, lane != Z - 1


def from_left(v, keep):
    return jnp.where(keep, pltpu.roll(v, 1, 1), 0.0)


def from_right(v, keep):
    return jnp.where(keep, pltpu.roll(v, v.shape[1] - 1, 1), 0.0)


def spread(v):
    not_first, not_last = lane_moves(*v.shape)
    return jnp.concatenate([from_right(v, not_last), v, from_left(v, not_first)], axis=0).astype(BF16)


def inside(i):
    x = lax.axis_index("gx") * B + i - H
    block = lax.broadcasted_iota(jnp.int32, (1, (B + 2) * Z), 1) // Z
    y = lax.axis_index("row") * B + block + 1 - H
    in_x = (x >= 0) & (x < lax.axis_size("gx") * B)
    in_y = (y >= 0) & (y < lax.axis_size("row") * B)
    return jnp.where(in_y, 1.0, 0.0) * jnp.where(in_x, 1.0, 0.0)


def as_column(row):
    n = row.shape[1]
    rows = lax.broadcasted_iota(jnp.int32, (n, n), 0)
    lanes = lax.broadcasted_iota(jnp.int32, (n, n), 1)
    return jnp.sum(jnp.where(rows == lanes, row, 0.0), axis=1, keepdims=True)


def conv_row(kernel_ref, sources, i, lanes):
    n = lanes.stop - lanes.start
    cut = slice(lanes.start - Z, lanes.stop + Z)
    rhs = jnp.concatenate([s[i + a - 1, :, cut] for a in range(3) for s in sources], axis=0)
    got = jnp.dot(kernel_ref[...], rhs, preferred_element_type=F32)
    acc = got[:48, :n] + got[48:96, Z : Z + n] + got[96:, 2 * Z :]
    not_first, not_last = lane_moves(16, n)
    return from_left(acc[:16], not_first) + acc[16:32] + from_right(acc[32:], not_last)


def back_row(turned_ref, channels, spread_ref, i, lanes):
    n, q = lanes.stop - lanes.start, channels.stop - channels.start
    cut = slice(lanes.start - Z, lanes.stop + Z)
    lhs = jnp.concatenate([turned_ref[b, channels] for b in range(3)], axis=0)
    rhs = jnp.concatenate([spread_ref[i + 1 - a, :, cut] for a in range(3)], axis=0)
    got = jnp.dot(lhs, rhs, preferred_element_type=F32)
    return got[:q, 2 * Z :] + got[q : 2 * q, Z : Z + n] + got[2 * q :, :n]


def kernel_gradient(out_ref, own, sources):
    gap = jnp.zeros((48, Z), BF16)
    lhs = jnp.concatenate(
        [
            jnp.concatenate(
                [
                    jnp.concatenate([gap] * b + [rows] + [gap] * (2 - b), axis=1)
                    for b in range(3)
                ],
                axis=0,
            )
            for rows in own
        ],
        axis=1,
    )
    for a in range(3):
        rhs = jnp.concatenate(
            [jnp.concatenate([s[H + i + a - 1, :, RING] for s in sources], axis=0) for i in range(B)],
            axis=1,
        )
        got = lax.dot_general(lhs, rhs, (((1,), (1,)), ((), ())), preferred_element_type=F32)
        rows = slice(144 * a, 144 * (a + 1))
        out_ref[rows, : got.shape[1]] = got.astype(out_ref.dtype)
        if got.shape[1] < Z:
            out_ref[rows, got.shape[1] :] = jnp.zeros((144, Z - got.shape[1]), out_ref.dtype)


def own_cells(spread_ref):
    return [spread_ref[H + i, :, MID] for i in range(B)]


def activate(value):
    sigmoid = jax.nn.sigmoid(value)
    return 0.2 * value + 0.8 * value * sigmoid, 0.2 + 0.8 * (
        sigmoid + value * sigmoid * (1.0 - sigmoid)
    )


def assemble(parts, frame):
    before, left, right, after, above, below = parts
    own = slice(H, H + B)
    frame[own, :, : H * Z] = before[...]
    frame[own, :, H * Z : 2 * H * Z] = left[...]
    frame[own, :, 2 * H * Z : 3 * H * Z] = right[...]
    frame[own, :, 3 * H * Z :] = after[...]
    frame[:H] = above[...]
    frame[H + B :] = below[...]


def put(pair, i, rows, value):
    left, right = pair
    left[i, rows] = value[:, : H * Z]
    right[i, rows] = value[:, H * Z :]


def wide_sum(blocks):
    total = sum(block.astype(F32) for block in blocks)
    return jnp.broadcast_to(jnp.sum(total, axis=1, keepdims=True), (total.shape[0], Z))


def cell_sum(own):
    return wide_sum([rows[16:32] for rows in own])


def pack_kernel(x_ref, left, right, wide):
    wide[...] = x_ref[...].astype(F32)
    for i in range(B):
        row = [wide[pl.ds(B * i + j, 64, stride=B * B), :].astype(BF16) for j in range(B)]
        put((left, right), i, slice(0, 64), jnp.concatenate(row, axis=1))


def rows_kernel(before, left, right, after, top, bottom):
    for k, ref in enumerate((before, left, right, after)):
        lanes = slice(k * H * Z, (k + 1) * H * Z)
        top[:, :, lanes] = ref[:H]
        bottom[:, :, lanes] = ref[B - H :]


def prepare_kernel(
    cot_ref, merge, layer_bias, merging_bias, k0, k1, k2, k3,
    base, carried, merge_grad, bias, merge_bias, w0, w1, w2, w3, t0, t1, t2, t3, wide,
):
    for k in range(4):
        column = as_column(layer_bias[k : k + 1].astype(F32))
        bias[16 * k : 16 * (k + 1)] = jnp.broadcast_to(column, (16, Z))
    merge_bias[...] = jnp.broadcast_to(as_column(merging_bias[...].astype(F32)), (64, Z))
    for k_ref, w_ref, t_ref in ((k0, w0, t0), (k1, w1, t1), (k2, w2, t2), (k3, w3, t3)):
        w_ref[...] = jnp.concatenate([k_ref[144 * a : 144 * (a + 1)] for a in range(3)], axis=1)
        for b in range(3):
            rows = [k_ref[48 * t : 48 * (t + 1)] for t in (b, 3 + b, 6 + b)]
            t_ref[b] = jnp.transpose(jnp.concatenate(rows, axis=0).astype(F32)).astype(BF16)
    wide[...] = cot_ref[...].astype(F32)
    merge_t = jnp.transpose(merge[...].astype(F32)).astype(BF16)
    for i in range(B):
        cot = jnp.concatenate(
            [wide[pl.ds(B * i + j, 64, stride=B * B), :] for j in range(B)], axis=1
        )
        grad = (BETA * cot).astype(BF16)
        merge_grad[i] = grad
        back = jnp.dot(merge_t, grad, preferred_element_type=F32)
        base[i] = cot + back[:64]
        carried[i] = back[64:]


def first_kernel(
    before, left, right, after, above, below, k0, k1, bias,
    frame, hidden_0, slope_0, slope_1, send_left, send_right,
):
    assemble((before, left, right, after, above, below), frame)

    for i in range(H - 1, H + B + 1):
        pre = conv_row(k0, [frame], i, RING) + bias[0:16, 0:1]
        value, slope = activate(pre)
        slope_0[i] = slope
        hidden_0[i, :, RING] = (value * inside(i)).astype(BF16)
    for i in range(B):
        pre = conv_row(k1, [frame, hidden_0], H + i, MID) + bias[16:32, 0:1]
        value, slope = activate(pre)
        slope_1[i] = slope
        put((send_left, send_right), i, slice(0, 16), hidden_0[H + i, :, MID])
        put((send_left, send_right), i, slice(16, 32), value.astype(BF16))


def second_kernel(
    before, left, right, after, above, below, frame, k2, k3, bias, carried,
    hidden_01, hidden_2, hidden_3, slope_2, own_3, send_left, send_right,
):
    assemble((before, left, right, after, above, below), hidden_01)

    for i in range(H - 1, H + B + 1):
        pre = conv_row(k2, [frame, hidden_01], i, RING) + bias[32:48, 0:1]
        value, slope = activate(pre)
        slope_2[i] = slope
        hidden_2[i, :, RING] = (value * inside(i)).astype(BF16)
    for i in range(B):
        pre = conv_row(k3, [frame, hidden_01, hidden_2], H + i, MID) + bias[48:64, 0:1]
        value, slope = activate(pre)
        hidden_3[i] = value.astype(BF16)
        grad = (carried[i, 48:64] * slope).astype(BF16)
        own_3[i] = spread(grad.astype(F32))
        put((send_left, send_right), i, slice(0, 16), grad)
        put((send_left, send_right), i, slice(16, 32), carried[i, 32:48].astype(BF16))


def merge_kernel(
    frame, hidden_01, hidden_2, hidden_3, own_3, merge, merge_bias, merge_grad,
    out_ref, grad_3, grad_merge,
):
    total = jnp.zeros((64, 128), F32)
    for i in range(B):
        base = frame[H + i, :, MID]
        joined = jnp.concatenate(
            [base, hidden_01[H + i, :, MID], hidden_2[H + i, :, MID], hidden_3[i]], axis=0
        )
        merged = jnp.dot(merge[...], joined, preferred_element_type=F32) + merge_bias[:, 0:1]
        out = base.astype(F32) + BETA * merged
        for j in range(B):
            out_ref[pl.ds(B * i + j, 64, stride=B * B), :] = out[:, j * Z : (j + 1) * Z]
        grad = merge_grad[i]
        total = total + lax.dot_general(
            grad, joined, (((1,), (1,)), ((), ())), preferred_element_type=F32
        )
    grad_merge[0:64] = total
    grad_merge[64:128] = wide_sum([merge_grad[i] for i in range(B)])
    own = [own_3[i] for i in range(B)]
    grad_merge[128:144] = cell_sum(own)
    kernel_gradient(grad_3, own, [frame, hidden_01, hidden_2])


def third_kernel(
    before, left, right, after, above, below, t2, t3, slope_1, slope_2, carried,
    spread_3, spread_2, own_1, send_left, send_right, pieces, held,
):
    assemble((before, left, right, after, above, below), pieces)
    held[...] = pieces[:, 16:32, :].astype(F32)
    for i in range(B):
        held[H + i, :, MID] = carried[i, 32:48]

    for i in range(N):
        spread_3[i] = spread(pieces[i, 0:16].astype(F32))

    for i in range(H - 1, H + B + 1):
        got = held[i, :, RING] + back_row(t3, slice(96, 112), spread_3, i, RING)
        grad = (got * slope_2[i] * inside(i)).astype(BF16)
        spread_2[i, :, RING] = spread(grad.astype(F32))
    for i in range(B):
        got = (
            carried[i, 16:32]
            + back_row(t3, slice(80, 96), spread_3, H + i, MID)
            + back_row(t2, slice(80, 96), spread_2, H + i, MID)
        )
        grad = (got * slope_1[i]).astype(BF16)
        own_1[i] = spread(grad.astype(F32))
        put((send_left, send_right), i, slice(0, 16), spread_2[H + i, 16:32, MID])
        put((send_left, send_right), i, slice(16, 32), grad)
        put((send_left, send_right), i, slice(32, 48), carried[i, 0:16].astype(BF16))


def beside_kernel(
    frame, hidden_01, spread_3, spread_2, own_1, t3, base,
    grad_2, grad_1, grad_bias, part_0, part_base,
):
    own = [own_1[i] for i in range(B)]
    grad_bias[0:16] = cell_sum(own)
    kernel_gradient(grad_1, own, [frame, hidden_01.at[:, 0:16, :]])
    own = own_cells(spread_2)
    grad_bias[16:32] = cell_sum(own)
    kernel_gradient(grad_2, own, [frame, hidden_01])

    for i in range(H - 1, H + B + 1):
        part_0[i] = back_row(t3, slice(64, 80), spread_3, i, RING)
    for i in range(B):
        part_base[i] = base[i] + back_row(t3, slice(0, 64), spread_3, H + i, MID)


def fourth_kernel(
    before, left, right, after, above, below, t1, t2, slope_0, carried, part_0, frame,
    grad_1, grad_2, grad_3, grad_merge, grad_bias,
    spread_2, spread_1, spread_0, kept, sent, sums, pieces, held,
):
    assemble((before, left, right, after, above, below), pieces)
    held[...] = pieces[:, 32:48, :].astype(F32)
    for i in range(B):
        held[H + i, :, MID] = carried[i, 0:16]

    for i in range(N):
        spread_2[i] = spread(pieces[i, 0:16].astype(F32))
        spread_1[i] = spread(pieces[i, 16:32].astype(F32))

    for i in range(H - 1, H + B + 1):
        got = (
            held[i, :, RING]
            + part_0[i]
            + back_row(t2, slice(64, 80), spread_2, i, RING)
            + back_row(t1, slice(64, 80), spread_1, i, RING)
        )
        grad = (got * slope_0[i] * inside(i)).astype(BF16)
        spread_0[i, :, RING] = spread(grad.astype(F32))
    own = own_cells(spread_0)
    kernel_gradient(sums.at[0:432], own, [frame])
    sums[432:864] = grad_1[...]
    sums[864:1296] = grad_2[...]
    sums[1296:1728] = grad_3[...]
    sums[1728:1856] = grad_merge[0:128]
    sums[1856:1872] = cell_sum(own)
    sums[1872:1904] = grad_bias[...]
    sums[1904:1920] = grad_merge[128:144]
    sums[1920:] = jnp.zeros((2 * HALF - 1920, Z), F32)
    mine, other = halves()
    kept[...] = sums[pl.ds(mine, HALF), :]
    sent[...] = sums[pl.ds(other, HALF), :].astype(BF16)


def last_kernel(spread_2, spread_1, spread_0, t0, t1, t2, part_base, out_ref):
    for i in range(B):
        out = (
            part_base[i]
            + back_row(t2, slice(0, 64), spread_2, H + i, MID)
            + back_row(t1, slice(0, 64), spread_1, H + i, MID)
            + back_row(t0, slice(0, 64), spread_0, H + i, MID)
        )
        for j in range(B):
            out_ref[pl.ds(B * i + j, 64, stride=B * B), :] = out[:, j * Z : (j + 1) * Z]


def halves():
    first = lax.axis_index("rep") * HALF
    return pl.multiple_of(first, HALF), pl.multiple_of(HALF - first, HALF)


def pair_kernel(kept, came, out_ref):
    out_ref[...] = (kept[...] + came[...].astype(F32)).astype(BF16)


def add_kernel(x_ref, out_ref):
    def step(k, acc):
        return acc + x_ref[pl.ds(pl.multiple_of(k * 128, 128), 128), :].astype(F32)

    acc = lax.fori_loop(0, HALF // 128, step, jnp.zeros((128, Z), F32))
    total = acc[0:ROWS]
    for k in range(1, 128 // ROWS):
        total = total + acc[k * ROWS : (k + 1) * ROWS]
    block = jnp.concatenate([total] * (128 // ROWS), axis=0).astype(BF16)

    def put(k, carry):
        out_ref[pl.ds(pl.multiple_of(k * 128, 128), 128), :] = block
        return carry

    lax.fori_loop(0, HALF // 128, put, 0)


def turned(block):
    rows = lax.broadcasted_iota(jnp.int32, block.shape, 0)
    lanes = lax.broadcasted_iota(jnp.int32, block.shape, 1)
    return jnp.sum(jnp.where(rows == lanes, block, 0.0), axis=0, keepdims=True)


def unpack_kernel(scale, mine_ref, other_ref, g0, g1, g2, g3, bias, weight, weight_bias, sums):
    mine, other = halves()
    sums[pl.ds(mine, HALF), :] = mine_ref[...].astype(F32) * scale
    sums[pl.ds(other, HALF), :] = other_ref[...].astype(F32) * scale
    for k, g in enumerate((g0, g1, g2, g3)):
        g[...] = sums[432 * k : 432 * (k + 1), : g.shape[1]]
    weight[...] = sums[1728:1792]
    weight_bias[...] = turned(sums[1792:1856])[:, :64]
    for k in range(4):
        bias[k : k + 1] = turned(sums[1856 + 16 * k : 1872 + 16 * k])[:, :16]


def exchange(left, right):
    channels = left.shape[1]
    up = [(i, i + 1) for i in range(lax.axis_size("row") - 1)]
    before = lax.ppermute(right, "row", up)
    after = lax.ppermute(left, "row", [(j, i) for i, j in up])
    edge = shape((H, channels, N * Z), BF16)
    top, bottom = call(rows_kernel, [edge, edge], [before, left, right, after], name="rows")
    up = [(i, i + 1) for i in range(lax.axis_size("gx") - 1)]
    above = lax.ppermute(bottom, "gx", up)
    below = lax.ppermute(top, "gx", [(j, i) for i, j in up])
    return [before, left, right, after, above, below]


def body(samples, cotangent, kernel_0, kernel_1, kernel_2, kernel_3, layer_bias, merging_weight, merging_bias):
    kernels = (kernel_0, kernel_1, kernel_2, kernel_3)
    cells = B * B * Z * lax.axis_size("gx") * lax.axis_size("row") * lax.axis_size("rep")
    scale = 1.0 / math.sqrt(cells)
    flat = [k.transpose(1, 0, 2).reshape(432, k.shape[2]) for k in kernels]
    half = shape((B, 64, H * Z), BF16)
    columns = shape((64, Z), F32)
    wide = pltpu.VMEM((1024, Z), F32)
    left, right = call(pack_kernel, [half, half], [samples.reshape(1024, Z)], [wide], name="pack")
    base, carried, merge_grad, bias, merge_bias, w0, w1, w2, w3, t0, t1, t2, t3 = call(
        prepare_kernel,
        [shape((B, 64, B * Z), F32)] * 2
        + [shape((B, 64, B * Z), BF16), columns, columns]
        + [shape((144, 3 * k.shape[2]), BF16) for k in kernels]
        + [shape((3, k.shape[2], 144), BF16) for k in kernels],
        [cotangent.reshape(1024, Z), merging_weight, layer_bias, merging_bias.reshape(1, 64)] + flat,
        [wide],
        flops=40_000_000,
        name="prepare",
    )
    parts = exchange(left, right)
    ring = shape((N, 16, (B + 2) * Z), F32)
    send = shape((B, 32, H * Z), BF16)
    frame, hidden_0, slope_0, slope_1, left, right = call(
        first_kernel,
        [shape((N, 64, N * Z), BF16), shape((N, 16, N * Z), BF16), ring, shape((B, 16, B * Z), F32), send, send],
        parts + [w0, w1, bias],
        name="layers_0_1",
    )
    parts = exchange(left, right)
    hidden_01, hidden_2, hidden_3, slope_2, own_3, left, right = call(
        second_kernel,
        [
            shape((N, 32, N * Z), BF16),
            shape((N, 16, N * Z), BF16),
            shape((B, 16, B * Z), BF16),
            ring,
            shape((B, 48, B * Z), BF16),
            send,
            send,
        ],
        parts + [frame, w2, w3, bias, carried],
        name="layers_2_3",
    )
    parts = exchange(left, right)
    grads = shape((432, Z), F32)
    output, grad_3, grad_merge = call(
        merge_kernel,
        [shape((1024, Z), F32), grads, shape((144, Z), F32)],
        [frame, hidden_01, hidden_2, hidden_3, own_3, merging_weight, merge_bias, merge_grad],
        flops=100_000_000,
        name="merge",
    )
    send = shape((B, 48, H * Z), BF16)
    spreads = shape((N, 48, N * Z), BF16)
    spread_3, spread_2, own_1, left, right = call(
        third_kernel,
        [spreads, spreads, shape((B, 48, B * Z), BF16), send, send],
        parts + [t2, t3, slope_1, slope_2, carried],
        [pltpu.VMEM((N, 32, N * Z), BF16), pltpu.VMEM((N, 16, N * Z), F32)],
        name="gradients_2_1",
    )
    parts = exchange(left, right)
    grad_2, grad_1, grad_bias, part_0, part_base = call(
        beside_kernel,
        [grads, grads, shape((32, Z), F32), ring, shape((B, 64, B * Z), F32)],
        [frame, hidden_01, spread_3, spread_2, own_1, t3, base],
        flops=200_000_000,
        name="kernel_gradients_2_1",
    )
    spread_2, spread_1, spread_0, kept, sent = call(
        fourth_kernel,
        [spreads, spreads, spreads, shape((HALF, Z), F32), shape((HALF, Z), BF16)],
        parts
        + [t1, t2, slope_0, carried, part_0, frame]
        + [grad_1, grad_2, grad_3, grad_merge, grad_bias],
        [pltpu.VMEM((2 * HALF, Z), F32), pltpu.VMEM((N, 48, N * Z), BF16), pltpu.VMEM((N, 16, N * Z), F32)],
        name="gradient_0",
    )
    axes = ("gx", "row")
    swap = [(0, 1), (1, 0)]
    half_sum = shape((HALF, Z), BF16)
    (paired,) = call(pair_kernel, [half_sum], [kept, lax.ppermute(sent, "rep", swap)], name="pair")
    spread_sums = lax.all_to_all(paired.reshape(GROUP, ROWS, Z), axes, 0, 0, tiled=True)
    (added,) = call(add_kernel, [half_sum], [spread_sums.reshape(HALF, Z)], name="add")
    totals = lax.all_to_all(added.reshape(GROUP, ROWS, Z), axes, 0, 0, tiled=True)
    totals = totals.reshape(HALF, Z)
    others = lax.ppermute(totals, "rep", swap)
    (grad_input,) = call(
        last_kernel,
        [shape((1024, Z), F32)],
        [spread_2, spread_1, spread_0, t0, t1, t2, part_base],
        flops=300_000_000,
        name="input_gradient",
    )
    unpacked = call(
        functools.partial(unpack_kernel, scale),
        [shape((432, k.shape[2]), F32) for k in kernels]
        + [shape((4, 16), F32), shape((64, 128), F32), shape((1, 64), F32)],
        [totals, others],
        [pltpu.VMEM((2 * HALF, Z), F32)],
        name="unpack",
    )
    grad_kernels = [g.reshape(27, 16, g.shape[1]).transpose(1, 0, 2) for g in unpacked[:4]]
    out_shape = (1, 64, B, B, Z)
    return (
        output.reshape(out_shape),
        grad_input.reshape(out_shape),
        *grad_kernels,
        unpacked[4],
        unpacked[5],
        unpacked[6].reshape(64),
    )


def solution(mesh):
    split = P("rep", None, "gx", "row", None)
    return jax.shard_map(
        body,
        mesh=mesh,
        in_specs=(split, split) + (P(),) * 7,
        out_specs=(split, split) + (P(),) * 7,
        check_vma=False,
    )
```

```python
import functools
import math

import jax
import jax.numpy as jnp
from jax import lax
from jax.experimental import pallas as pl
from jax.experimental.pallas import tpu as pltpu
from jax.sharding import PartitionSpec as P

BETA = 0.2
BF16, F32 = jnp.bfloat16, jnp.float32
Z = 128
B = 4
H = 2
N = B + 2 * H
MID = slice(H * Z, (H + B) * Z)
RING = slice((H - 1) * Z, (H + B + 1) * Z)
GROUP = 128
ROWS = 8
HALF = GROUP * ROWS
VMEM_LIMIT = 24 * 2**20


def shape(dims, dtype):
    return jax.ShapeDtypeStruct(dims, dtype)


def call(kernel, outs, args, scratch=(), flops=1_000_000, name=None):
    moved = sum(math.prod(a.shape) * a.dtype.itemsize for a in list(args) + list(outs))
    return pl.pallas_call(
        kernel,
        out_shape=list(outs),
        in_specs=[pl.BlockSpec(memory_space=pltpu.VMEM)] * len(args),
        out_specs=[pl.BlockSpec(memory_space=pltpu.VMEM)] * len(outs),
        scratch_shapes=list(scratch),
        compiler_params=pltpu.CompilerParams(vmem_limit_bytes=VMEM_LIMIT),
        cost_estimate=pl.CostEstimate(flops=flops, bytes_accessed=moved, transcendentals=0),
        name=name,
    )(*args)


def lane_moves(rows, width):
    lane = lax.broadcasted_iota(jnp.int32, (rows, width), 1) % Z
    return lane != 0, lane != Z - 1


def from_left(v, keep):
    return jnp.where(keep, pltpu.roll(v, 1, 1), 0.0)


def from_right(v, keep):
    return jnp.where(keep, pltpu.roll(v, v.shape[1] - 1, 1), 0.0)


def spread(v):
    not_first, not_last = lane_moves(*v.shape)
    return jnp.concatenate([from_right(v, not_last), v, from_left(v, not_first)], axis=0).astype(BF16)


def inside(x, y, blocks):
    x = lax.axis_index("gx") * B + x
    block = lax.broadcasted_iota(jnp.int32, (1, blocks * Z), 1) // Z
    y = lax.axis_index("row") * B + block + y
    in_x = (x >= 0) & (x < lax.axis_size("gx") * B)
    in_y = (y >= 0) & (y < lax.axis_size("row") * B)
    return jnp.where(in_y, 1.0, 0.0) * jnp.where(in_x, 1.0, 0.0)


def as_column(row):
    n = row.shape[1]
    rows = lax.broadcasted_iota(jnp.int32, (n, n), 0)
    lanes = lax.broadcasted_iota(jnp.int32, (n, n), 1)
    return jnp.sum(jnp.where(rows == lanes, row, 0.0), axis=1, keepdims=True)


def conv_row(kernel_ref, sources, i, lanes):
    n = lanes.stop - lanes.start
    cut = slice(lanes.start - Z, lanes.stop + Z)
    rhs = jnp.concatenate([s(i + a - 1, cut) for a in range(3) for s in sources], axis=0)
    got = jnp.dot(kernel_ref[...], rhs, preferred_element_type=F32)
    acc = got[:48, :n] + got[48:96, Z : Z + n] + got[96:, 2 * Z :]
    not_first, not_last = lane_moves(16, n)
    return from_left(acc[:16], not_first) + acc[16:32] + from_right(acc[32:], not_last)


def back_row(turned_ref, channels, spread_ref, i, lanes):
    n, q = lanes.stop - lanes.start, channels.stop - channels.start
    cut = slice(lanes.start - Z, lanes.stop + Z)
    lhs = jnp.concatenate([turned_ref[b, channels] for b in range(3)], axis=0)
    rhs = jnp.concatenate([spread_ref[i + 1 - a, :, cut] for a in range(3)], axis=0)
    got = jnp.dot(lhs, rhs, preferred_element_type=F32)
    return got[:q, 2 * Z :] + got[q : 2 * q, Z : Z + n] + got[2 * q :, :n]


def kernel_gradient(out_ref, own, sources):
    gap = jnp.zeros((48, Z), BF16)
    lhs = jnp.concatenate(
        [
            jnp.concatenate(
                [
                    jnp.concatenate([gap] * b + [rows] + [gap] * (2 - b), axis=1)
                    for b in range(3)
                ],
                axis=0,
            )
            for rows in own
        ],
        axis=1,
    )
    for a in range(3):
        rhs = jnp.concatenate(
            [jnp.concatenate([s[H + i + a - 1, :, RING] for s in sources], axis=0) for i in range(B)],
            axis=1,
        )
        got = lax.dot_general(lhs, rhs, (((1,), (1,)), ((), ())), preferred_element_type=F32)
        rows = slice(144 * a, 144 * (a + 1))
        out_ref[rows, : got.shape[1]] = got.astype(out_ref.dtype)
        if got.shape[1] < Z:
            out_ref[rows, got.shape[1] :] = jnp.zeros((144, Z - got.shape[1]), out_ref.dtype)


def own_cells(spread_ref):
    return [spread_ref[H + i, :, MID] for i in range(B)]


def activate(value):
    sigmoid = jax.nn.sigmoid(value)
    return 0.2 * value + 0.8 * value * sigmoid, 0.2 + 0.8 * (
        sigmoid + value * sigmoid * (1.0 - sigmoid)
    )


def assemble(parts, frame):
    before, left, right, after, above, below = parts
    own = slice(H, H + B)
    frame[own, :, : H * Z] = before[...]
    frame[own, :, H * Z : 2 * H * Z] = left[...]
    frame[own, :, 2 * H * Z : 3 * H * Z] = right[...]
    frame[own, :, 3 * H * Z :] = after[...]
    frame[:H] = above[...]
    frame[H + B :] = below[...]


def put(pair, i, rows, value):
    left, right = pair
    left[i, rows] = value[:, : H * Z]
    right[i, rows] = value[:, H * Z :]


def wide_sum(blocks):
    total = sum(block.astype(F32) for block in blocks)
    return jnp.broadcast_to(jnp.sum(total, axis=1, keepdims=True), (total.shape[0], Z))


def cell_sum(own):
    return wide_sum([rows[16:32] for rows in own])


def pack_kernel(x_ref, out_ref, wide):
    wide[...] = x_ref[...].astype(F32)
    for i in range(B):
        row = [wide[pl.ds(B * i + j, 64, stride=B * B), :].astype(BF16) for j in range(B)]
        out_ref[i] = jnp.concatenate(row, axis=1)


def band_kernel(before, own, after, out_ref):
    for k, ref in enumerate((before, own, after)):
        out_ref[:, :, k * B * Z : (k + 1) * B * Z] = ref[...]


def rows_kernel(before, left, right, after, top, bottom):
    for k, ref in enumerate((before, left, right, after)):
        lanes = slice(k * H * Z, (k + 1) * H * Z)
        top[:, :, lanes] = ref[:H]
        bottom[:, :, lanes] = ref[B - H :]


def prepare_kernel(
    cot_ref, merge, layer_bias, merging_bias, k0, k1, k2, k3,
    base, carried, merge_grad, bias, merge_bias, w0, w1, w2, w3, t0, t1, t2, t3, wide,
):
    for k in range(4):
        column = as_column(layer_bias[k : k + 1].astype(F32))
        bias[16 * k : 16 * (k + 1)] = jnp.broadcast_to(column, (16, Z))
    merge_bias[...] = jnp.broadcast_to(as_column(merging_bias[...].astype(F32)), (64, Z))
    for k_ref, w_ref, t_ref in ((k0, w0, t0), (k1, w1, t1), (k2, w2, t2), (k3, w3, t3)):
        w_ref[...] = jnp.concatenate([k_ref[144 * a : 144 * (a + 1)] for a in range(3)], axis=1)
        for b in range(3):
            rows = [k_ref[48 * t : 48 * (t + 1)] for t in (b, 3 + b, 6 + b)]
            t_ref[b] = jnp.transpose(jnp.concatenate(rows, axis=0).astype(F32)).astype(BF16)
    wide[...] = cot_ref[...].astype(F32)
    merge_t = jnp.transpose(merge[...].astype(F32)).astype(BF16)
    for i in range(B):
        cot = jnp.concatenate(
            [wide[pl.ds(B * i + j, 64, stride=B * B), :] for j in range(B)], axis=1
        )
        grad = (BETA * cot).astype(BF16)
        merge_grad[i] = grad
        back = jnp.dot(merge_t, grad, preferred_element_type=F32)
        base[i] = cot + back[:64]
        carried[i] = back[64:]


def forward_kernel(
    above, band, below, k0, k1, k2, k3, bias, carried,
    frame, hidden_01, hidden_2, hidden_3, slope_0, slope_1, slope_2, own_3, send_left, send_right,
    wide_0, wide_1, wide_2,
):
    bands = (above, band, below)
    near = slice((B - H) * Z, (2 * B + H) * Z)
    sources = [lambda i, cut: bands[i // B][i % B, :, cut]]
    for i in range(N):
        frame[i] = sources[0](i + B - H, near)
    slopes = (slope_0, slope_1, slope_2)
    for k, (kernel_ref, wide) in enumerate(((k0, wide_0), (k1, wide_1), (k2, wide_2))):
        reach = 3 - k
        lanes = slice((B - reach) * Z, (2 * B + reach) * Z)
        for i in range(B - reach, 2 * B + reach):
            pre = conv_row(kernel_ref, sources, i, lanes) + bias[16 * k : 16 * (k + 1), 0:1]
            value, slope = activate(pre)
            value = value * inside(i - B, -reach, B + 2 * reach)
            wide[i, :, lanes] = value.astype(BF16)
            if k == 1 and B <= i < 2 * B:
                slope_1[i - B] = slope[:, reach * Z : (reach + B) * Z]
            if k != 1 and B - 1 <= i < 2 * B + 1:
                slopes[k][i - B + H] = slope[:, (reach - 1) * Z : (reach + B + 1) * Z]
        sources.append(lambda i, cut, wide=wide: wide[i, :, cut])
    for i in range(N):
        hidden_01[i, 0:16] = wide_0[i + B - H, :, near]
        hidden_01[i, 16:32] = wide_1[i + B - H, :, near]
        if 0 < i < N - 1:
            hidden_2[i, :, RING] = wide_2[i + B - H, :, slice((B - 1) * Z, (2 * B + 1) * Z)]
    for i in range(B):
        pre = conv_row(k3, sources, B + i, slice(B * Z, 2 * B * Z)) + bias[48:64, 0:1]
        value, slope = activate(pre)
        hidden_3[i] = value.astype(BF16)
        grad = (carried[i, 48:64] * slope).astype(BF16)
        own_3[i] = spread(grad.astype(F32))
        put((send_left, send_right), i, slice(0, 16), grad)
        put((send_left, send_right), i, slice(16, 32), carried[i, 32:48].astype(BF16))


def merge_kernel(
    frame, hidden_01, hidden_2, hidden_3, own_3, merge, merge_bias, merge_grad,
    out_ref, grad_3, grad_merge,
):
    total = jnp.zeros((64, 128), F32)
    for i in range(B):
        base = frame[H + i, :, MID]
        joined = jnp.concatenate(
            [base, hidden_01[H + i, :, MID], hidden_2[H + i, :, MID], hidden_3[i]], axis=0
        )
        merged = jnp.dot(merge[...], joined, preferred_element_type=F32) + merge_bias[:, 0:1]
        out = base.astype(F32) + BETA * merged
        for j in range(B):
            out_ref[pl.ds(B * i + j, 64, stride=B * B), :] = out[:, j * Z : (j + 1) * Z]
        grad = merge_grad[i]
        total = total + lax.dot_general(
            grad, joined, (((1,), (1,)), ((), ())), preferred_element_type=F32
        )
    grad_merge[0:64] = total
    grad_merge[64:128] = wide_sum([merge_grad[i] for i in range(B)])
    own = [own_3[i] for i in range(B)]
    grad_merge[128:144] = cell_sum(own)
    kernel_gradient(grad_3, own, [frame, hidden_01, hidden_2])


def third_kernel(
    before, left, right, after, above, below, t2, t3, slope_1, slope_2, carried,
    spread_3, spread_2, own_1, send_left, send_right, pieces, held,
):
    assemble((before, left, right, after, above, below), pieces)
    held[...] = pieces[:, 16:32, :].astype(F32)
    for i in range(B):
        held[H + i, :, MID] = carried[i, 32:48]

    for i in range(N):
        spread_3[i] = spread(pieces[i, 0:16].astype(F32))

    for i in range(H - 1, H + B + 1):
        got = held[i, :, RING] + back_row(t3, slice(96, 112), spread_3, i, RING)
        grad = (got * slope_2[i] * inside(i - H, 1 - H, B + 2)).astype(BF16)
        spread_2[i, :, RING] = spread(grad.astype(F32))
    for i in range(B):
        got = (
            carried[i, 16:32]
            + back_row(t3, slice(80, 96), spread_3, H + i, MID)
            + back_row(t2, slice(80, 96), spread_2, H + i, MID)
        )
        grad = (got * slope_1[i]).astype(BF16)
        own_1[i] = spread(grad.astype(F32))
        put((send_left, send_right), i, slice(0, 16), spread_2[H + i, 16:32, MID])
        put((send_left, send_right), i, slice(16, 32), grad)
        put((send_left, send_right), i, slice(32, 48), carried[i, 0:16].astype(BF16))


def beside_kernel(
    frame, hidden_01, spread_3, spread_2, own_1, t3, base,
    grad_2, grad_1, grad_bias, part_0, part_base,
):
    own = [own_1[i] for i in range(B)]
    grad_bias[0:16] = cell_sum(own)
    kernel_gradient(grad_1, own, [frame, hidden_01.at[:, 0:16, :]])
    own = own_cells(spread_2)
    grad_bias[16:32] = cell_sum(own)
    kernel_gradient(grad_2, own, [frame, hidden_01])

    for i in range(H - 1, H + B + 1):
        part_0[i] = back_row(t3, slice(64, 80), spread_3, i, RING)
    for i in range(B):
        part_base[i] = base[i] + back_row(t3, slice(0, 64), spread_3, H + i, MID)


def fourth_kernel(
    before, left, right, after, above, below, t1, t2, slope_0, carried, part_0, frame,
    grad_1, grad_2, grad_3, grad_merge, grad_bias,
    spread_2, spread_1, spread_0, kept, sent, sums, pieces, held,
):
    assemble((before, left, right, after, above, below), pieces)
    held[...] = pieces[:, 32:48, :].astype(F32)
    for i in range(B):
        held[H + i, :, MID] = carried[i, 0:16]

    for i in range(N):
        spread_2[i] = spread(pieces[i, 0:16].astype(F32))
        spread_1[i] = spread(pieces[i, 16:32].astype(F32))

    for i in range(H - 1, H + B + 1):
        got = (
            held[i, :, RING]
            + part_0[i]
            + back_row(t2, slice(64, 80), spread_2, i, RING)
            + back_row(t1, slice(64, 80), spread_1, i, RING)
        )
        grad = (got * slope_0[i] * inside(i - H, 1 - H, B + 2)).astype(BF16)
        spread_0[i, :, RING] = spread(grad.astype(F32))
    own = own_cells(spread_0)
    kernel_gradient(sums.at[0:432], own, [frame])
    sums[432:864] = grad_1[...]
    sums[864:1296] = grad_2[...]
    sums[1296:1728] = grad_3[...]
    sums[1728:1856] = grad_merge[0:128]
    sums[1856:1872] = cell_sum(own)
    sums[1872:1904] = grad_bias[...]
    sums[1904:1920] = grad_merge[128:144]
    sums[1920:] = jnp.zeros((2 * HALF - 1920, Z), F32)
    mine, other = halves()
    kept[...] = sums[pl.ds(mine, HALF), :]
    sent[...] = sums[pl.ds(other, HALF), :].astype(BF16)


def last_kernel(spread_2, spread_1, spread_0, t0, t1, t2, part_base, out_ref):
    for i in range(B):
        out = (
            part_base[i]
            + back_row(t2, slice(0, 64), spread_2, H + i, MID)
            + back_row(t1, slice(0, 64), spread_1, H + i, MID)
            + back_row(t0, slice(0, 64), spread_0, H + i, MID)
        )
        for j in range(B):
            out_ref[pl.ds(B * i + j, 64, stride=B * B), :] = out[:, j * Z : (j + 1) * Z]


def halves():
    first = lax.axis_index("rep") * HALF
    return pl.multiple_of(first, HALF), pl.multiple_of(HALF - first, HALF)


def pair_kernel(kept, came, out_ref):
    out_ref[...] = (kept[...] + came[...].astype(F32)).astype(BF16)


def add_kernel(x_ref, out_ref):
    def step(k, acc):
        return acc + x_ref[pl.ds(pl.multiple_of(k * 128, 128), 128), :].astype(F32)

    acc = lax.fori_loop(0, HALF // 128, step, jnp.zeros((128, Z), F32))
    total = acc[0:ROWS]
    for k in range(1, 128 // ROWS):
        total = total + acc[k * ROWS : (k + 1) * ROWS]
    block = jnp.concatenate([total] * (128 // ROWS), axis=0).astype(BF16)

    def put(k, carry):
        out_ref[pl.ds(pl.multiple_of(k * 128, 128), 128), :] = block
        return carry

    lax.fori_loop(0, HALF // 128, put, 0)


def turned(block):
    rows = lax.broadcasted_iota(jnp.int32, block.shape, 0)
    lanes = lax.broadcasted_iota(jnp.int32, block.shape, 1)
    return jnp.sum(jnp.where(rows == lanes, block, 0.0), axis=0, keepdims=True)


def unpack_kernel(scale, mine_ref, other_ref, g0, g1, g2, g3, bias, weight, weight_bias, sums):
    mine, other = halves()
    sums[pl.ds(mine, HALF), :] = mine_ref[...].astype(F32) * scale
    sums[pl.ds(other, HALF), :] = other_ref[...].astype(F32) * scale
    for k, g in enumerate((g0, g1, g2, g3)):
        g[...] = sums[432 * k : 432 * (k + 1), : g.shape[1]]
    weight[...] = sums[1728:1792]
    weight_bias[...] = turned(sums[1792:1856])[:, :64]
    for k in range(4):
        bias[k : k + 1] = turned(sums[1856 + 16 * k : 1872 + 16 * k])[:, :16]


def neighbours(low, high, axis):
    up = [(i, i + 1) for i in range(lax.axis_size(axis) - 1)]
    return lax.ppermute(high, axis, up), lax.ppermute(low, axis, [(j, i) for i, j in up])


def exchange(left, right):
    before, after = neighbours(left, right, "row")
    edge = shape((H, left.shape[1], N * Z), BF16)
    top, bottom = call(rows_kernel, [edge, edge], [before, left, right, after], name="rows")
    above, below = neighbours(top, bottom, "gx")
    return [before, left, right, after, above, below]


def body(samples, cotangent, kernel_0, kernel_1, kernel_2, kernel_3, layer_bias, merging_weight, merging_bias):
    kernels = (kernel_0, kernel_1, kernel_2, kernel_3)
    cells = B * B * Z * lax.axis_size("gx") * lax.axis_size("row") * lax.axis_size("rep")
    scale = 1.0 / math.sqrt(cells)
    flat = [k.transpose(1, 0, 2).reshape(432, k.shape[2]) for k in kernels]
    columns = shape((64, Z), F32)
    wide = pltpu.VMEM((1024, Z), F32)
    (own,) = call(
        pack_kernel,
        [shape((B, 64, B * Z), BF16)],
        [samples.reshape(1024, Z)],
        [wide],
        name="pack",
    )
    base, carried, merge_grad, bias, merge_bias, w0, w1, w2, w3, t0, t1, t2, t3 = call(
        prepare_kernel,
        [shape((B, 64, B * Z), F32)] * 2
        + [shape((B, 64, B * Z), BF16), columns, columns]
        + [shape((144, 3 * k.shape[2]), BF16) for k in kernels]
        + [shape((3, k.shape[2], 144), BF16) for k in kernels],
        [cotangent.reshape(1024, Z), merging_weight, layer_bias, merging_bias.reshape(1, 64)] + flat,
        [wide],
        flops=40_000_000,
        name="prepare",
    )
    before, after = neighbours(own, own, "row")
    (band,) = call(band_kernel, [shape((B, 64, 3 * B * Z), BF16)], [before, own, after], name="band")
    above, below = neighbours(band, band, "gx")
    ring = shape((N, 16, (B + 2) * Z), F32)
    send = shape((B, 32, H * Z), BF16)
    (
        frame, hidden_01, hidden_2, hidden_3,
        slope_0, slope_1, slope_2, own_3, left, right,
    ) = call(
        forward_kernel,
        [
            shape((N, 64, N * Z), BF16),
            shape((N, 32, N * Z), BF16),
            shape((N, 16, N * Z), BF16),
            shape((B, 16, B * Z), BF16),
            ring,
            shape((B, 16, B * Z), F32),
            ring,
            shape((B, 48, B * Z), BF16),
            send,
            send,
        ],
        [above, band, below, w0, w1, w2, w3, bias, carried],
        [pltpu.VMEM((3 * B, 16, 3 * B * Z), BF16)] * 3,
        name="forward",
    )
    parts = exchange(left, right)
    grads = shape((432, Z), F32)
    output, grad_3, grad_merge = call(
        merge_kernel,
        [shape((1024, Z), F32), grads, shape((144, Z), F32)],
        [frame, hidden_01, hidden_2, hidden_3, own_3, merging_weight, merge_bias, merge_grad],
        flops=100_000_000,
        name="merge",
    )
    send = shape((B, 48, H * Z), BF16)
    spreads = shape((N, 48, N * Z), BF16)
    spread_3, spread_2, own_1, left, right = call(
        third_kernel,
        [spreads, spreads, shape((B, 48, B * Z), BF16), send, send],
        parts + [t2, t3, slope_1, slope_2, carried],
        [pltpu.VMEM((N, 32, N * Z), BF16), pltpu.VMEM((N, 16, N * Z), F32)],
        name="gradients_2_1",
    )
    parts = exchange(left, right)
    grad_2, grad_1, grad_bias, part_0, part_base = call(
        beside_kernel,
        [grads, grads, shape((32, Z), F32), ring, shape((B, 64, B * Z), F32)],
        [frame, hidden_01, spread_3, spread_2, own_1, t3, base],
        flops=200_000_000,
        name="kernel_gradients_2_1",
    )
    spread_2, spread_1, spread_0, kept, sent = call(
        fourth_kernel,
        [spreads, spreads, spreads, shape((HALF, Z), F32), shape((HALF, Z), BF16)],
        parts
        + [t1, t2, slope_0, carried, part_0, frame]
        + [grad_1, grad_2, grad_3, grad_merge, grad_bias],
        [pltpu.VMEM((2 * HALF, Z), F32), pltpu.VMEM((N, 48, N * Z), BF16), pltpu.VMEM((N, 16, N * Z), F32)],
        name="gradient_0",
    )
    axes = ("gx", "row")
    swap = [(0, 1), (1, 0)]
    half_sum = shape((HALF, Z), BF16)
    (paired,) = call(pair_kernel, [half_sum], [kept, lax.ppermute(sent, "rep", swap)], name="pair")
    spread_sums = lax.all_to_all(paired.reshape(GROUP, ROWS, Z), axes, 0, 0, tiled=True)
    (added,) = call(add_kernel, [half_sum], [spread_sums.reshape(HALF, Z)], name="add")
    totals = lax.all_to_all(added.reshape(GROUP, ROWS, Z), axes, 0, 0, tiled=True)
    totals = totals.reshape(HALF, Z)
    others = lax.ppermute(totals, "rep", swap)
    (grad_input,) = call(
        last_kernel,
        [shape((1024, Z), F32)],
        [spread_2, spread_1, spread_0, t0, t1, t2, part_base],
        flops=300_000_000,
        name="input_gradient",
    )
    unpacked = call(
        functools.partial(unpack_kernel, scale),
        [shape((432, k.shape[2]), F32) for k in kernels]
        + [shape((4, 16), F32), shape((64, 128), F32), shape((1, 64), F32)],
        [totals, others],
        [pltpu.VMEM((2 * HALF, Z), F32)],
        name="unpack",
    )
    grad_kernels = [g.reshape(27, 16, g.shape[1]).transpose(1, 0, 2) for g in unpacked[:4]]
    out_shape = (1, 64, B, B, Z)
    return (
        output.reshape(out_shape),
        grad_input.reshape(out_shape),
        *grad_kernels,
        unpacked[4],
        unpacked[5],
        unpacked[6].reshape(64),
    )


def solution(mesh):
    split = P("rep", None, "gx", "row", None)
    return jax.shard_map(
        body,
        mesh=mesh,
        in_specs=(split, split) + (P(),) * 7,
        out_specs=(split, split) + (P(),) * 7,
        check_vma=False,
    )
```

```python
import functools
import math

import jax
import jax.numpy as jnp
from jax import lax
from jax.experimental import pallas as pl
from jax.experimental.pallas import tpu as pltpu
from jax.sharding import PartitionSpec as P

BETA = 0.2
BF16, F32 = jnp.bfloat16, jnp.float32
Z = 128
B = 4
H = 2
N = B + 2 * H
MID = slice(H * Z, (H + B) * Z)
WIDTHS = (4, 3, 3, 2, 1)
Y_AT = tuple(Z * sum(WIDTHS[:u]) for u in range(6))
X_AT = tuple(Z * sum(w * (B + 2 * w) for w in WIDTHS[:u]) for u in range(6))
RING = slice((H - 1) * Z, (H + B + 1) * Z)
GROUP = 128
ROWS = 8
HALF = GROUP * ROWS
VMEM_LIMIT = 24 * 2**20


def shape(dims, dtype):
    return jax.ShapeDtypeStruct(dims, dtype)


def call(kernel, outs, args, scratch=(), flops=1_000_000, name=None):
    moved = sum(math.prod(a.shape) * a.dtype.itemsize for a in list(args) + list(outs))
    return pl.pallas_call(
        kernel,
        out_shape=list(outs),
        in_specs=[pl.BlockSpec(memory_space=pltpu.VMEM)] * len(args),
        out_specs=[pl.BlockSpec(memory_space=pltpu.VMEM)] * len(outs),
        scratch_shapes=list(scratch),
        compiler_params=pltpu.CompilerParams(vmem_limit_bytes=VMEM_LIMIT),
        cost_estimate=pl.CostEstimate(flops=flops, bytes_accessed=moved, transcendentals=0),
        name=name,
    )(*args)


def lane_moves(rows, width):
    lane = lax.broadcasted_iota(jnp.int32, (rows, width), 1) % Z
    return lane != 0, lane != Z - 1


def from_left(v, keep):
    return jnp.where(keep, pltpu.roll(v, 1, 1), 0.0)


def from_right(v, keep):
    return jnp.where(keep, pltpu.roll(v, v.shape[1] - 1, 1), 0.0)


def spread(v):
    not_first, not_last = lane_moves(*v.shape)
    return jnp.concatenate([from_right(v, not_last), v, from_left(v, not_first)], axis=0).astype(BF16)


def inside(x, y, blocks):
    x = lax.axis_index("gx") * B + x
    block = lax.broadcasted_iota(jnp.int32, (1, blocks * Z), 1) // Z
    y = lax.axis_index("row") * B + block + y
    in_x = (x >= 0) & (x < lax.axis_size("gx") * B)
    in_y = (y >= 0) & (y < lax.axis_size("row") * B)
    return jnp.where(in_y, 1.0, 0.0) * jnp.where(in_x, 1.0, 0.0)


def as_column(row):
    n = row.shape[1]
    rows = lax.broadcasted_iota(jnp.int32, (n, n), 0)
    lanes = lax.broadcasted_iota(jnp.int32, (n, n), 1)
    return jnp.sum(jnp.where(rows == lanes, row, 0.0), axis=1, keepdims=True)


def conv_row(kernel_ref, sources, i, lanes):
    n = lanes.stop - lanes.start
    cut = slice(lanes.start - Z, lanes.stop + Z)
    rhs = jnp.concatenate([s(i + a - 1, cut) for a in range(3) for s in sources], axis=0)
    got = jnp.dot(kernel_ref[...], rhs, preferred_element_type=F32)
    acc = got[:48, :n] + got[48:96, Z : Z + n] + got[96:, 2 * Z :]
    not_first, not_last = lane_moves(16, n)
    return from_left(acc[:16], not_first) + acc[16:32] + from_right(acc[32:], not_last)


def back_row(turned_ref, channels, spread_ref, i, lanes):
    n, q = lanes.stop - lanes.start, channels.stop - channels.start
    cut = slice(lanes.start - Z, lanes.stop + Z)
    lhs = jnp.concatenate([turned_ref[b, channels] for b in range(3)], axis=0)
    rhs = jnp.concatenate([spread_ref[i + 1 - a, :, cut] for a in range(3)], axis=0)
    got = jnp.dot(lhs, rhs, preferred_element_type=F32)
    return got[:q, 2 * Z :] + got[q : 2 * q, Z : Z + n] + got[2 * q :, :n]


def kernel_gradient(own, sources):
    gap = jnp.zeros((48, Z), BF16)

    def shifted(rows):
        return [jnp.concatenate([gap] * b + [rows] + [gap] * (2 - b), axis=1) for b in range(3)]

    lhs = jnp.concatenate(
        [
            jnp.concatenate([part for layer in own for part in shifted(layer[i])], axis=0)
            for i in range(B)
        ],
        axis=1,
    )
    for a in range(3):
        rhs = jnp.concatenate(
            [jnp.concatenate([s[H + i + a - 1, :, RING] for s in sources], axis=0) for i in range(B)],
            axis=1,
        )
        got = lax.dot_general(lhs, rhs, (((1,), (1,)), ((), ())), preferred_element_type=F32)
        gap_lanes = jnp.zeros((got.shape[0], Z - got.shape[1]), F32)
        yield a, jnp.concatenate([got, gap_lanes], axis=1)


def own_cells(spread_ref):
    return [spread_ref[B + i, :, slice(B * Z, 2 * B * Z)] for i in range(B)]


def activate(value):
    sigmoid = jax.nn.sigmoid(value)
    return 0.2 * value + 0.8 * value * sigmoid, 0.2 + 0.8 * (
        sigmoid + value * sigmoid * (1.0 - sigmoid)
    )


def ring_row(parts, u, f):
    above, below, before, own, after = parts
    w = WIDTHS[u]
    if B <= f < 2 * B:
        side = slice(Y_AT[u], Y_AT[u + 1])
        i = f - B
        return jnp.concatenate(
            [before[i, :, side], own[i, 16 * u : 16 * (u + 1)], after[i, :, side]], axis=1
        )
    ref, r = (above, f - B + w) if f < B else (below, f - 2 * B)
    at = X_AT[u] + r * (B + 2 * w) * Z
    return ref[:, at : at + (B + 2 * w) * Z]


def wide_sum(blocks):
    total = sum(block.astype(F32) for block in blocks)
    return jnp.broadcast_to(jnp.sum(total, axis=1, keepdims=True), (total.shape[0], Z))


def cell_sum(own):
    return wide_sum([rows[16:32] for rows in own])


def pack_kernel(x_ref, out_ref, wide):
    wide[...] = x_ref[...].astype(F32)
    for i in range(B):
        row = [wide[pl.ds(B * i + j, 64, stride=B * B), :].astype(BF16) for j in range(B)]
        out_ref[i] = jnp.concatenate(row, axis=1)


def band_kernel(before, own, after, out_ref):
    for k, ref in enumerate((before, own, after)):
        out_ref[:, :, k * B * Z : (k + 1) * B * Z] = ref[...]


def edges_kernel(before, own, after, top, bottom):
    for u, w in enumerate(WIDTHS):
        parts = (top, bottom, before, own, after)
        for r in range(w):
            at = X_AT[u] + r * (B + 2 * w) * Z
            lanes = slice(at, at + (B + 2 * w) * Z)
            top[:, lanes] = ring_row(parts, u, B + r)
            bottom[:, lanes] = ring_row(parts, u, 2 * B - w + r)


def prepare_kernel(
    cot_ref, merge, layer_bias, merging_bias, k0, k1, k2, k3,
    base, carried, merge_grad, bias, merge_bias, w0, w1, w2, w3, t0, t1, t2, t3, wide,
):
    for k in range(4):
        column = as_column(layer_bias[k : k + 1].astype(F32))
        bias[16 * k : 16 * (k + 1)] = jnp.broadcast_to(column, (16, Z))
    merge_bias[...] = jnp.broadcast_to(as_column(merging_bias[...].astype(F32)), (64, Z))
    for k_ref, w_ref, t_ref in ((k0, w0, t0), (k1, w1, t1), (k2, w2, t2), (k3, w3, t3)):
        w_ref[...] = jnp.concatenate([k_ref[144 * a : 144 * (a + 1)] for a in range(3)], axis=1)
        for b in range(3):
            rows = [k_ref[48 * t : 48 * (t + 1)] for t in (b, 3 + b, 6 + b)]
            t_ref[b] = jnp.transpose(jnp.concatenate(rows, axis=0).astype(F32)).astype(BF16)
    wide[...] = cot_ref[...].astype(F32)
    merge_t = jnp.transpose(merge[...].astype(F32)).astype(BF16)
    for i in range(B):
        cot = jnp.concatenate(
            [wide[pl.ds(B * i + j, 64, stride=B * B), :] for j in range(B)], axis=1
        )
        grad = (BETA * cot).astype(BF16)
        merge_grad[i] = grad
        back = jnp.dot(merge_t, grad, preferred_element_type=F32)
        base[i] = cot + back[:64]
        carried[i] = back[64:]


def forward_kernel(
    above, band, below, k0, k1, k2, k3, bias, carried,
    frame, hidden_01, hidden_2, hidden_3, slope_0, slope_1, slope_2, own_3, own, left, right,
    wide_0, wide_1, wide_2,
):
    bands = (above, band, below)
    near = slice((B - H) * Z, (2 * B + H) * Z)
    sources = [lambda i, cut: bands[i // B][i % B, :, cut]]
    for i in range(N):
        frame[i] = sources[0](i + B - H, near)
    for k, (kernel_ref, wide) in enumerate(((k0, wide_0), (k1, wide_1), (k2, wide_2))):
        reach = 3 - k
        lanes = slice((B - reach) * Z, (2 * B + reach) * Z)
        for i in range(B - reach, 2 * B + reach):
            pre = conv_row(kernel_ref, sources, i, lanes) + bias[16 * k : 16 * (k + 1), 0:1]
            value, slope = activate(pre)
            present = inside(i - B, -reach, B + 2 * reach)
            wide[i, :, lanes] = (value * present).astype(BF16)
            slope = slope * present
            if k == 0 and B - 1 <= i < 2 * B + 1:
                slope_0[i - B + 1] = slope[:, 2 * Z : (B + 4) * Z]
            if k == 1:
                slope_1[i - B + 2] = slope
            if k == 2 and B <= i < 2 * B:
                slope_2[i - B] = slope[:, Z : (B + 1) * Z]
        sources.append(lambda i, cut, wide=wide: wide[i, :, cut])
    for i in range(N):
        hidden_01[i, 0:16] = wide_0[i + B - H, :, near]
        hidden_01[i, 16:32] = wide_1[i + B - H, :, near]
        if 0 < i < N - 1:
            hidden_2[i, :, RING] = wide_2[i + B - H, :, slice((B - 1) * Z, (2 * B + 1) * Z)]
    for i in range(B):
        pre = conv_row(k3, sources, B + i, slice(B * Z, 2 * B * Z)) + bias[48:64, 0:1]
        value, slope = activate(pre)
        hidden_3[i] = value.astype(BF16)
        grad = (carried[i, 48:64] * slope).astype(BF16)
        own_3[i] = spread(grad.astype(F32))
        rest = [slope_2[i]] + [carried[i, 16 * k : 16 * (k + 1)] for k in (2, 1, 0)]
        ready = [grad] + [value.astype(BF16) for value in rest]
        own[i] = jnp.concatenate(ready, axis=0)
        left[i] = jnp.concatenate([v[:, : w * Z] for v, w in zip(ready, WIDTHS)], axis=1)
        right[i] = jnp.concatenate([v[:, (B - w) * Z :] for v, w in zip(ready, WIDTHS)], axis=1)


def merge_kernel(
    frame, hidden_01, hidden_2, hidden_3, own_3, merge, merge_bias, merge_grad,
    out_ref, grad_3, grad_merge,
):
    total = jnp.zeros((64, 128), F32)
    for i in range(B):
        base = frame[H + i, :, MID]
        joined = jnp.concatenate(
            [base, hidden_01[H + i, :, MID], hidden_2[H + i, :, MID], hidden_3[i]], axis=0
        )
        merged = jnp.dot(merge[...], joined, preferred_element_type=F32) + merge_bias[:, 0:1]
        out = base.astype(F32) + BETA * merged
        for j in range(B):
            out_ref[pl.ds(B * i + j, 64, stride=B * B), :] = out[:, j * Z : (j + 1) * Z]
        grad = merge_grad[i]
        total = total + lax.dot_general(
            grad, joined, (((1,), (1,)), ((), ())), preferred_element_type=F32
        )
    grad_merge[0:64] = total
    grad_merge[64:128] = wide_sum([merge_grad[i] for i in range(B)])
    own = [own_3[i] for i in range(B)]
    grad_merge[128:144] = cell_sum(own)
    for a, got in kernel_gradient([own], [frame, hidden_01, hidden_2]):
        grad_3[144 * a : 144 * (a + 1)] = got


def backward_kernel(
    above, below, before, own, after, t1, t2, t3, slope_0, slope_1, slope_2, carried,
    frame, hidden_01, grad_3, grad_merge,
    spread_0, spread_1, spread_2, spread_3, kept, sent, sums,
):
    parts = (above, below, before, own, after)
    spreads = (spread_0, spread_1, spread_2, spread_3)
    turned_refs = (None, t1, t2, t3)
    for f in range(3 * B):
        spread_3[f] = spread(ring_row(parts, 0, f).astype(F32))
    for k in (2, 1, 0):
        reach = k + 1
        lanes = slice((B - reach) * Z, (2 * B + reach) * Z)
        middle = slice(reach * Z, (B + reach) * Z)
        channels = slice(64 + 16 * k, 80 + 16 * k)
        for f in range(B - reach, 2 * B + reach):
            i = f - B
            here = 0 <= i < B
            got = ring_row(parts, 4 - k, f).astype(F32)
            if here:
                exact = carried[i, 16 * k : 16 * (k + 1)]
                got = jnp.concatenate([got[:, : middle.start], exact, got[:, middle.stop :]], axis=1)
            for m in range(k + 1, 4):
                got = got + back_row(turned_refs[m], channels, spreads[m], f, lanes)
            if k == 2:
                slope = ring_row(parts, 1, f).astype(F32)
                if here:
                    slope = jnp.concatenate(
                        [slope[:, : middle.start], slope_2[i], slope[:, middle.stop :]], axis=1
                    )
            else:
                slope = (slope_0, slope_1)[k][i + reach]
            grad = (got * slope).astype(BF16)
            spreads[k][f, :, lanes] = spread(grad.astype(F32))
    owns = [own_cells(ref) for ref in spreads[:3]]
    for a, got in kernel_gradient(owns, [frame, hidden_01]):
        for k in range(3):
            at = 432 * k + 144 * a
            sums[at : at + 144] = got[144 * k : 144 * (k + 1)]
    sums[1296:1728] = grad_3[...]
    sums[1728:1856] = grad_merge[0:128]
    for k in range(3):
        sums[1856 + 16 * k : 1872 + 16 * k] = cell_sum(owns[k])
    sums[1904:1920] = grad_merge[128:144]
    sums[1920:] = jnp.zeros((2 * HALF - 1920, Z), F32)
    mine, other = halves()
    kept[...] = sums[pl.ds(mine, HALF), :]
    sent[...] = sums[pl.ds(other, HALF), :].astype(BF16)


def last_kernel(spread_0, spread_1, spread_2, spread_3, t0, t1, t2, t3, base, out_ref):
    for i in range(B):
        out = base[i]
        for ref, turned_ref in zip((spread_0, spread_1, spread_2, spread_3), (t0, t1, t2, t3)):
            out = out + back_row(turned_ref, slice(0, 64), ref, B + i, slice(B * Z, 2 * B * Z))
        for j in range(B):
            out_ref[pl.ds(B * i + j, 64, stride=B * B), :] = out[:, j * Z : (j + 1) * Z]


def halves():
    first = lax.axis_index("rep") * HALF
    return pl.multiple_of(first, HALF), pl.multiple_of(HALF - first, HALF)


def pair_kernel(kept, came, out_ref):
    out_ref[...] = (kept[...] + came[...].astype(F32)).astype(BF16)


def add_kernel(x_ref, out_ref):
    def step(k, acc):
        return acc + x_ref[pl.ds(pl.multiple_of(k * 128, 128), 128), :].astype(F32)

    acc = lax.fori_loop(0, HALF // 128, step, jnp.zeros((128, Z), F32))
    total = acc[0:ROWS]
    for k in range(1, 128 // ROWS):
        total = total + acc[k * ROWS : (k + 1) * ROWS]
    block = jnp.concatenate([total] * (128 // ROWS), axis=0).astype(BF16)

    def put(k, carry):
        out_ref[pl.ds(pl.multiple_of(k * 128, 128), 128), :] = block
        return carry

    lax.fori_loop(0, HALF // 128, put, 0)


def turned(block):
    rows = lax.broadcasted_iota(jnp.int32, block.shape, 0)
    lanes = lax.broadcasted_iota(jnp.int32, block.shape, 1)
    return jnp.sum(jnp.where(rows == lanes, block, 0.0), axis=0, keepdims=True)


def unpack_kernel(scale, mine_ref, other_ref, g0, g1, g2, g3, bias, weight, weight_bias, sums):
    mine, other = halves()
    sums[pl.ds(mine, HALF), :] = mine_ref[...].astype(F32) * scale
    sums[pl.ds(other, HALF), :] = other_ref[...].astype(F32) * scale
    for k, g in enumerate((g0, g1, g2, g3)):
        g[...] = sums[432 * k : 432 * (k + 1), : g.shape[1]]
    weight[...] = sums[1728:1792]
    weight_bias[...] = turned(sums[1792:1856])[:, :64]
    for k in range(4):
        bias[k : k + 1] = turned(sums[1856 + 16 * k : 1872 + 16 * k])[:, :16]


def neighbours(low, high, axis):
    up = [(i, i + 1) for i in range(lax.axis_size(axis) - 1)]
    return lax.ppermute(high, axis, up), lax.ppermute(low, axis, [(j, i) for i, j in up])


def body(samples, cotangent, kernel_0, kernel_1, kernel_2, kernel_3, layer_bias, merging_weight, merging_bias):
    kernels = (kernel_0, kernel_1, kernel_2, kernel_3)
    cells = B * B * Z * lax.axis_size("gx") * lax.axis_size("row") * lax.axis_size("rep")
    scale = 1.0 / math.sqrt(cells)
    flat = [k.transpose(1, 0, 2).reshape(432, k.shape[2]) for k in kernels]
    columns = shape((64, Z), F32)
    wide = pltpu.VMEM((1024, Z), F32)
    (own,) = call(
        pack_kernel,
        [shape((B, 64, B * Z), BF16)],
        [samples.reshape(1024, Z)],
        [wide],
        name="pack",
    )
    base, carried, merge_grad, bias, merge_bias, w0, w1, w2, w3, t0, t1, t2, t3 = call(
        prepare_kernel,
        [shape((B, 64, B * Z), F32)] * 2
        + [shape((B, 64, B * Z), BF16), columns, columns]
        + [shape((144, 3 * k.shape[2]), BF16) for k in kernels]
        + [shape((3, k.shape[2], 144), BF16) for k in kernels],
        [cotangent.reshape(1024, Z), merging_weight, layer_bias, merging_bias.reshape(1, 64)] + flat,
        [wide],
        flops=40_000_000,
        name="prepare",
    )
    before, after = neighbours(own, own, "row")
    (band,) = call(band_kernel, [shape((B, 64, 3 * B * Z), BF16)], [before, own, after], name="band")
    above, below = neighbours(band, band, "gx")
    side = shape((B, 16, Y_AT[5]), BF16)
    (
        frame, hidden_01, hidden_2, hidden_3,
        slope_0, slope_1, slope_2, own_3, own, left, right,
    ) = call(
        forward_kernel,
        [
            shape((N, 64, N * Z), BF16),
            shape((N, 32, N * Z), BF16),
            shape((N, 16, N * Z), BF16),
            shape((B, 16, B * Z), BF16),
            shape((B + 2, 16, (B + 2) * Z), F32),
            shape((B + 4, 16, (B + 4) * Z), F32),
            shape((B, 16, B * Z), F32),
            shape((B, 48, B * Z), BF16),
            shape((B, 80, B * Z), BF16),
            side,
            side,
        ],
        [above, band, below, w0, w1, w2, w3, bias, carried],
        [pltpu.VMEM((3 * B, 16, 3 * B * Z), BF16)] * 3,
        name="forward",
    )
    before, after = neighbours(left, right, "row")
    edge = shape((16, X_AT[5]), BF16)
    top, bottom = call(edges_kernel, [edge, edge], [before, own, after], name="edges")
    above, below = neighbours(top, bottom, "gx")
    output, grad_3, grad_merge = call(
        merge_kernel,
        [shape((1024, Z), F32), shape((432, Z), F32), shape((144, Z), F32)],
        [frame, hidden_01, hidden_2, hidden_3, own_3, merging_weight, merge_bias, merge_grad],
        flops=100_000_000,
        name="merge",
    )
    spreads = [shape((3 * B, 48, 3 * B * Z), BF16)] * 4
    *spreads, kept, sent = call(
        backward_kernel,
        spreads + [shape((HALF, Z), F32), shape((HALF, Z), BF16)],
        [above, below, before, own, after, t1, t2, t3, slope_0, slope_1, slope_2, carried]
        + [frame, hidden_01, grad_3, grad_merge],
        [pltpu.VMEM((2 * HALF, Z), F32)],
        name="backward",
    )
    axes = ("gx", "row")
    swap = [(0, 1), (1, 0)]
    half_sum = shape((HALF, Z), BF16)
    (paired,) = call(pair_kernel, [half_sum], [kept, lax.ppermute(sent, "rep", swap)], name="pair")
    spread_sums = lax.all_to_all(paired.reshape(GROUP, ROWS, Z), axes, 0, 0, tiled=True)
    (added,) = call(add_kernel, [half_sum], [spread_sums.reshape(HALF, Z)], name="add")
    totals = lax.all_to_all(added.reshape(GROUP, ROWS, Z), axes, 0, 0, tiled=True)
    totals = totals.reshape(HALF, Z)
    others = lax.ppermute(totals, "rep", swap)
    (grad_input,) = call(
        last_kernel,
        [shape((1024, Z), F32)],
        spreads + [t0, t1, t2, t3, base],
        flops=300_000_000,
        name="input_gradient",
    )
    unpacked = call(
        functools.partial(unpack_kernel, scale),
        [shape((432, k.shape[2]), F32) for k in kernels]
        + [shape((4, 16), F32), shape((64, 128), F32), shape((1, 64), F32)],
        [totals, others],
        [pltpu.VMEM((2 * HALF, Z), F32)],
        name="unpack",
    )
    grad_kernels = [g.reshape(27, 16, g.shape[1]).transpose(1, 0, 2) for g in unpacked[:4]]
    out_shape = (1, 64, B, B, Z)
    return (
        output.reshape(out_shape),
        grad_input.reshape(out_shape),
        *grad_kernels,
        unpacked[4],
        unpacked[5],
        unpacked[6].reshape(64),
    )


def solution(mesh):
    split = P("rep", None, "gx", "row", None)
    return jax.shard_map(
        body,
        mesh=mesh,
        in_specs=(split, split) + (P(),) * 7,
        out_specs=(split, split) + (P(),) * 7,
        check_vma=False,
    )
```

```python
import functools
import math

import jax
import jax.numpy as jnp
from jax import lax
from jax.experimental import pallas as pl
from jax.experimental.pallas import tpu as pltpu
from jax.sharding import PartitionSpec as P

BETA = 0.2
BF16, F32 = jnp.bfloat16, jnp.float32
Z = 128
B = 4
H = 2
N = B + 2 * H
MID = slice(H * Z, (H + B) * Z)
EARLY, LATE = (3, 2, 1), (4, 3)
RING = slice((H - 1) * Z, (H + B + 1) * Z)
GROUP = 128
ROWS = 8
HALF = GROUP * ROWS
VMEM_LIMIT = 24 * 2**20


def shape(dims, dtype):
    return jax.ShapeDtypeStruct(dims, dtype)


def call(kernel, outs, args, scratch=(), flops=1_000_000, name=None):
    moved = sum(math.prod(a.shape) * a.dtype.itemsize for a in list(args) + list(outs))
    return pl.pallas_call(
        kernel,
        out_shape=list(outs),
        in_specs=[pl.BlockSpec(memory_space=pltpu.VMEM)] * len(args),
        out_specs=[pl.BlockSpec(memory_space=pltpu.VMEM)] * len(outs),
        scratch_shapes=list(scratch),
        compiler_params=pltpu.CompilerParams(vmem_limit_bytes=VMEM_LIMIT),
        cost_estimate=pl.CostEstimate(flops=flops, bytes_accessed=moved, transcendentals=0),
        name=name,
    )(*args)


def lane_moves(rows, width):
    lane = lax.broadcasted_iota(jnp.int32, (rows, width), 1) % Z
    return lane != 0, lane != Z - 1


def from_left(v, keep):
    parts = [pltpu.roll(v[:, k * Z : (k + 1) * Z], 1, 1) for k in range(v.shape[1] // Z)]
    return jnp.where(keep, jnp.concatenate(parts, axis=1), jnp.zeros_like(v))


def from_right(v, keep):
    parts = [pltpu.roll(v[:, k * Z : (k + 1) * Z], Z - 1, 1) for k in range(v.shape[1] // Z)]
    return jnp.where(keep, jnp.concatenate(parts, axis=1), jnp.zeros_like(v))


def spread(v):
    not_first, not_last = lane_moves(*v.shape)
    return jnp.concatenate([from_right(v, not_last), v, from_left(v, not_first)], axis=0)


def inside(x, y, blocks):
    x = lax.axis_index("gx") * B + x
    block = lax.broadcasted_iota(jnp.int32, (1, blocks * Z), 1) // Z
    y = lax.axis_index("row") * B + block + y
    in_x = (x >= 0) & (x < lax.axis_size("gx") * B)
    in_y = (y >= 0) & (y < lax.axis_size("row") * B)
    return jnp.where(in_y, 1.0, 0.0) * jnp.where(in_x, 1.0, 0.0)


def as_column(row):
    n = row.shape[1]
    rows = lax.broadcasted_iota(jnp.int32, (n, n), 0)
    lanes = lax.broadcasted_iota(jnp.int32, (n, n), 1)
    return jnp.sum(jnp.where(rows == lanes, row, 0.0), axis=1, keepdims=True)


def conv_row(kernel_ref, sources, i, lanes):
    n = lanes.stop - lanes.start
    cut = slice(lanes.start - Z, lanes.stop + Z)
    rhs = jnp.concatenate([s(i + a - 1, cut) for a in range(3) for s in sources], axis=0)
    got = jnp.dot(kernel_ref[...], rhs, preferred_element_type=F32)
    acc = got[:48, :n] + got[48:96, Z : Z + n] + got[96:, 2 * Z :]
    not_first, not_last = lane_moves(16, n)
    return from_left(acc[:16], not_first) + acc[16:32] + from_right(acc[32:], not_last)


def back_row(turned_ref, channels, spread_ref, i, lanes):
    n, q = lanes.stop - lanes.start, channels.stop - channels.start
    cut = slice(lanes.start - Z, lanes.stop + Z)
    lhs = jnp.concatenate([turned_ref[b, channels] for b in range(3)], axis=0)
    rhs = jnp.concatenate([spread_ref[i + 1 - a, :, cut] for a in range(3)], axis=0)
    got = jnp.dot(lhs, rhs, preferred_element_type=F32)
    return got[:q, 2 * Z :] + got[q : 2 * q, Z : Z + n] + got[2 * q :, :n]


def kernel_gradient(own, sources):
    lhs = jnp.concatenate(
        [jnp.concatenate([layer[i] for layer in own], axis=0) for i in range(B)], axis=1
    )
    for a in range(3):
        taps = [
            jnp.concatenate(
                [
                    jnp.concatenate(
                        [s[H + i + a - 1, :, pl.ds((H + b - 1) * Z, B * Z)] for s in sources], axis=0
                    )
                    for i in range(B)
                ],
                axis=1,
            )
            for b in range(3)
        ]
        q = taps[0].shape[0]
        got = lax.dot_general(
            lhs, jnp.concatenate(taps, axis=0), (((1,), (1,)), ((), ())), preferred_element_type=F32
        )
        gap = jnp.zeros((got.shape[0], Z - q), F32)
        for b in range(3):
            yield 3 * a + b, jnp.concatenate([got[:, q * b : q * (b + 1)], gap], axis=1)


def own_cells(spread_ref):
    return [spread_ref[B + i, :, slice(B * Z, 2 * B * Z)] for i in range(B)]


def activate(value):
    sigmoid = jax.nn.sigmoid(value)
    return 0.2 * value + 0.8 * value * sigmoid, 0.2 + 0.8 * (
        sigmoid + value * sigmoid * (1.0 - sigmoid)
    )


def y_at(widths, u):
    return Z * sum(widths[:u])


def x_at(widths, u):
    return Z * sum(w * (B + 2 * w) for w in widths[:u])


def ring_row(parts, widths, u, f):
    above, below, before, own, after = parts
    w = widths[u]
    if B <= f < 2 * B:
        side = slice(y_at(widths, u), y_at(widths, u + 1))
        i = f - B
        return jnp.concatenate(
            [before[i, :, side], own[i, 16 * u : 16 * (u + 1)], after[i, :, side]], axis=1
        )
    ref, r = (above, f - B + w) if f < B else (below, f - 2 * B)
    at = x_at(widths, u) + r * (B + 2 * w) * Z
    return ref[:, at : at + (B + 2 * w) * Z]


def put(widths, i, ready, own, left, right):
    own[i] = jnp.concatenate(ready, axis=0)
    left[i] = jnp.concatenate([v[:, : w * Z] for v, w in zip(ready, widths)], axis=1)
    right[i] = jnp.concatenate([v[:, (B - w) * Z :] for v, w in zip(ready, widths)], axis=1)


def wide_sum(blocks):
    total = sum(block.astype(F32) for block in blocks)
    return jnp.broadcast_to(jnp.sum(total, axis=1, keepdims=True), (total.shape[0], Z))


def cell_sum(own):
    return wide_sum([rows[16:32] for rows in own])


def pack_kernel(x_ref, out_ref, wide):
    wide[...] = x_ref[...].astype(F32)
    for i in range(B):
        row = [wide[pl.ds(B * i + j, 64, stride=B * B), :].astype(BF16) for j in range(B)]
        out_ref[i] = jnp.concatenate(row, axis=1)


def band_kernel(before, own, after, out_ref):
    for k, ref in enumerate((before, own, after)):
        out_ref[:, :, k * B * Z : (k + 1) * B * Z] = ref[...]


def edges_kernel(widths, before, own, after, top, bottom):
    for u, w in enumerate(widths):
        parts = (top, bottom, before, own, after)
        for r in range(w):
            at = x_at(widths, u) + r * (B + 2 * w) * Z
            lanes = slice(at, at + (B + 2 * w) * Z)
            top[:, lanes] = ring_row(parts, widths, u, B + r)
            bottom[:, lanes] = ring_row(parts, widths, u, 2 * B - w + r)


def prepare_kernel(
    cot_ref, merge, layer_bias, merging_bias, k0, k1, k2, k3,
    base, carried, merge_grad, bias, merge_bias, w0, w1, w2, w3, t0, t1, t2, t3, own, left, right, wide,
):
    for k in range(4):
        column = as_column(layer_bias[k : k + 1].astype(F32))
        bias[16 * k : 16 * (k + 1)] = jnp.broadcast_to(column, (16, Z))
    merge_bias[...] = jnp.broadcast_to(as_column(merging_bias[...].astype(F32)), (64, Z))
    for k_ref, w_ref, t_ref in ((k0, w0, t0), (k1, w1, t1), (k2, w2, t2), (k3, w3, t3)):
        w_ref[...] = jnp.concatenate([k_ref[144 * a : 144 * (a + 1)] for a in range(3)], axis=1)
        for b in range(3):
            rows = [k_ref[48 * t : 48 * (t + 1)] for t in (b, 3 + b, 6 + b)]
            t_ref[b] = jnp.transpose(jnp.concatenate(rows, axis=0).astype(F32)).astype(BF16)
    wide[...] = cot_ref[...].astype(F32)
    merge_t = jnp.transpose(merge[...].astype(F32)).astype(BF16)
    for i in range(B):
        cot = jnp.concatenate(
            [wide[pl.ds(B * i + j, 64, stride=B * B), :] for j in range(B)], axis=1
        )
        grad = (BETA * cot).astype(BF16)
        merge_grad[i] = grad
        back = jnp.dot(merge_t, grad, preferred_element_type=F32)
        base[i] = cot + back[:64]
        carried[i] = back[64:]
        ready = [back[64 + 16 * k : 80 + 16 * k].astype(BF16) for k in (2, 1, 0)]
        put(EARLY, i, ready, own, left, right)


def forward_kernel(
    above, band, below, k0, k1, k2, k3, bias, carried,
    frame, hidden_01, hidden_2, hidden_3, slope_0, slope_1, slope_2, own_3, own, left, right,
    wide_0, wide_1, wide_2,
):
    bands = (above, band, below)
    near = slice((B - H) * Z, (2 * B + H) * Z)
    sources = [lambda i, cut: bands[i // B][i % B, :, cut]]
    for i in range(N):
        frame[i] = sources[0](i + B - H, near)
    for k, (kernel_ref, wide) in enumerate(((k0, wide_0), (k1, wide_1), (k2, wide_2))):
        reach = 3 - k
        lanes = slice((B - reach) * Z, (2 * B + reach) * Z)
        for i in range(B - reach, 2 * B + reach):
            pre = conv_row(kernel_ref, sources, i, lanes) + bias[16 * k : 16 * (k + 1), 0:1]
            value, slope = activate(pre)
            present = inside(i - B, -reach, B + 2 * reach)
            wide[i, :, lanes] = (value * present).astype(BF16)
            slope = slope * present
            if k == 0 and B - 1 <= i < 2 * B + 1:
                slope_0[i - B + 1] = slope[:, 2 * Z : (B + 4) * Z]
            if k == 1:
                slope_1[i - B + 2] = slope
            if k == 2 and B <= i < 2 * B:
                slope_2[i - B] = slope[:, Z : (B + 1) * Z]
        sources.append(lambda i, cut, wide=wide: wide[i, :, cut])
    for i in range(N):
        hidden_01[i, 0:16] = wide_0[i + B - H, :, near]
        hidden_01[i, 16:32] = wide_1[i + B - H, :, near]
        if 0 < i < N - 1:
            hidden_2[i, :, RING] = wide_2[i + B - H, :, slice((B - 1) * Z, (2 * B + 1) * Z)]
    for i in range(B):
        pre = conv_row(k3, sources, B + i, slice(B * Z, 2 * B * Z)) + bias[48:64, 0:1]
        value, slope = activate(pre)
        hidden_3[i] = value.astype(BF16)
        grad = (carried[i, 48:64] * slope).astype(BF16)
        own_3[i] = spread(grad)
        put(LATE, i, [grad, slope_2[i].astype(BF16)], own, left, right)


def merge_kernel(
    frame, hidden_01, hidden_2, hidden_3, own_3, merge, merge_bias, merge_grad,
    out_ref, grad_3, grad_merge,
):
    total = jnp.zeros((64, 128), F32)
    for i in range(B):
        base = frame[H + i, :, MID]
        joined = jnp.concatenate(
            [base, hidden_01[H + i, :, MID], hidden_2[H + i, :, MID], hidden_3[i]], axis=0
        )
        merged = jnp.dot(merge[...], joined, preferred_element_type=F32) + merge_bias[:, 0:1]
        out = base.astype(F32) + BETA * merged
        for j in range(B):
            out_ref[pl.ds(B * i + j, 64, stride=B * B), :] = out[:, j * Z : (j + 1) * Z]
        grad = merge_grad[i]
        total = total + lax.dot_general(
            grad, joined, (((1,), (1,)), ((), ())), preferred_element_type=F32
        )
    grad_merge[0:64] = total
    grad_merge[64:128] = wide_sum([merge_grad[i] for i in range(B)])
    own = [own_3[i] for i in range(B)]
    grad_merge[128:144] = cell_sum(own)
    for t, got in kernel_gradient([own], [frame, hidden_01, hidden_2]):
        grad_3[48 * t : 48 * (t + 1)] = got


def backward_kernel(
    above, below, before, own, after, c_above, c_below, c_before, c_own, c_after,
    t1, t2, t3, slope_0, slope_1, slope_2, carried,
    frame, hidden_01, grad_3, grad_merge,
    spread_0, spread_1, spread_2, spread_3, kept, sent, sums,
):
    late = (above, below, before, own, after)
    early = (c_above, c_below, c_before, c_own, c_after)
    spreads = (spread_0, spread_1, spread_2, spread_3)
    turned_refs = (None, t1, t2, t3)
    for f in range(3 * B):
        spread_3[f] = spread(ring_row(late, LATE, 0, f))
    for k in (2, 1, 0):
        reach = k + 1
        lanes = slice((B - reach) * Z, (2 * B + reach) * Z)
        middle = slice(reach * Z, (B + reach) * Z)
        channels = slice(64 + 16 * k, 80 + 16 * k)
        for f in range(B - reach, 2 * B + reach):
            i = f - B
            here = 0 <= i < B
            got = ring_row(early, EARLY, 2 - k, f).astype(F32)
            if here:
                exact = carried[i, 16 * k : 16 * (k + 1)]
                got = jnp.concatenate([got[:, : middle.start], exact, got[:, middle.stop :]], axis=1)
            for m in range(k + 1, 4):
                got = got + back_row(turned_refs[m], channels, spreads[m], f, lanes)
            if k == 2:
                slope = ring_row(late, LATE, 1, f).astype(F32)
                if here:
                    slope = jnp.concatenate(
                        [slope[:, : middle.start], slope_2[i], slope[:, middle.stop :]], axis=1
                    )
            else:
                slope = (slope_0, slope_1)[k][i + reach]
            grad = (got * slope).astype(BF16)
            spreads[k][f, :, lanes] = spread(grad)
    owns = [own_cells(ref) for ref in spreads[:3]]
    for t, got in kernel_gradient(owns, [frame, hidden_01]):
        for k in range(3):
            at = 432 * k + 48 * t
            sums[at : at + 48] = got[48 * k : 48 * (k + 1)]
    sums[1296:1728] = grad_3[...]
    sums[1728:1856] = grad_merge[0:128]
    for k in range(3):
        sums[1856 + 16 * k : 1872 + 16 * k] = cell_sum(owns[k])
    sums[1904:1920] = grad_merge[128:144]
    sums[1920:] = jnp.zeros((2 * HALF - 1920, Z), F32)
    mine, other = halves()
    kept[...] = sums[pl.ds(mine, HALF), :]
    sent[...] = sums[pl.ds(other, HALF), :].astype(BF16)


def last_kernel(spread_0, spread_1, spread_2, spread_3, t0, t1, t2, t3, base, out_ref):
    for i in range(B):
        out = base[i]
        for ref, turned_ref in zip((spread_0, spread_1, spread_2, spread_3), (t0, t1, t2, t3)):
            out = out + back_row(turned_ref, slice(0, 64), ref, B + i, slice(B * Z, 2 * B * Z))
        for j in range(B):
            out_ref[pl.ds(B * i + j, 64, stride=B * B), :] = out[:, j * Z : (j + 1) * Z]


def halves():
    first = lax.axis_index("rep") * HALF
    return pl.multiple_of(first, HALF), pl.multiple_of(HALF - first, HALF)


def pair_kernel(kept, came, out_ref):
    out_ref[...] = (kept[...] + came[...].astype(F32)).astype(BF16)


def add_kernel(x_ref, out_ref):
    def step(k, acc):
        return acc + x_ref[pl.ds(pl.multiple_of(k * 128, 128), 128), :].astype(F32)

    acc = lax.fori_loop(0, HALF // 128, step, jnp.zeros((128, Z), F32))
    total = acc[0:ROWS]
    for k in range(1, 128 // ROWS):
        total = total + acc[k * ROWS : (k + 1) * ROWS]
    block = jnp.concatenate([total] * (128 // ROWS), axis=0).astype(BF16)

    def put(k, carry):
        out_ref[pl.ds(pl.multiple_of(k * 128, 128), 128), :] = block
        return carry

    lax.fori_loop(0, HALF // 128, put, 0)


def turned(block):
    rows = lax.broadcasted_iota(jnp.int32, block.shape, 0)
    lanes = lax.broadcasted_iota(jnp.int32, block.shape, 1)
    return jnp.sum(jnp.where(rows == lanes, block, 0.0), axis=0, keepdims=True)


def unpack_kernel(scale, mine_ref, other_ref, g0, g1, g2, g3, bias, weight, weight_bias, sums):
    mine, other = halves()
    sums[pl.ds(mine, HALF), :] = mine_ref[...].astype(F32) * scale
    sums[pl.ds(other, HALF), :] = other_ref[...].astype(F32) * scale
    for k, g in enumerate((g0, g1, g2, g3)):
        g[...] = sums[432 * k : 432 * (k + 1), : g.shape[1]]
    weight[...] = sums[1728:1792]
    weight_bias[...] = turned(sums[1792:1856])[:, :64]
    for k in range(4):
        bias[k : k + 1] = turned(sums[1856 + 16 * k : 1872 + 16 * k])[:, :16]


def neighbours(low, high, axis):
    up = [(i, i + 1) for i in range(lax.axis_size(axis) - 1)]
    return lax.ppermute(high, axis, up), lax.ppermute(low, axis, [(j, i) for i, j in up])


def edges(widths, before, own, after):
    edge = shape((16, x_at(widths, len(widths))), BF16)
    kernel = functools.partial(edges_kernel, widths)
    return call(kernel, [edge, edge], [before, own, after], name="edges")


def body(samples, cotangent, kernel_0, kernel_1, kernel_2, kernel_3, layer_bias, merging_weight, merging_bias):
    kernels = (kernel_0, kernel_1, kernel_2, kernel_3)
    cells = B * B * Z * lax.axis_size("gx") * lax.axis_size("row") * lax.axis_size("rep")
    scale = 1.0 / math.sqrt(cells)
    flat = [k.transpose(1, 0, 2).reshape(432, k.shape[2]) for k in kernels]
    columns = shape((64, Z), F32)
    wide = pltpu.VMEM((1024, Z), F32)
    (own,) = call(
        pack_kernel,
        [shape((B, 64, B * Z), BF16)],
        [samples.reshape(1024, Z)],
        [wide],
        name="pack",
    )
    base, carried, merge_grad, bias, merge_bias, w0, w1, w2, w3, t0, t1, t2, t3, c_own, c_left, c_right = call(
        prepare_kernel,
        [shape((B, 64, B * Z), F32)] * 2
        + [shape((B, 64, B * Z), BF16), columns, columns]
        + [shape((144, 3 * k.shape[2]), BF16) for k in kernels]
        + [shape((3, k.shape[2], 144), BF16) for k in kernels]
        + [shape((B, 48, B * Z), BF16)]
        + [shape((B, 16, y_at(EARLY, 3)), BF16)] * 2,
        [cotangent.reshape(1024, Z), merging_weight, layer_bias, merging_bias.reshape(1, 64)] + flat,
        [wide],
        flops=40_000_000,
        name="prepare",
    )
    before, after = neighbours(own, own, "row")
    (band,) = call(band_kernel, [shape((B, 64, 3 * B * Z), BF16)], [before, own, after], name="band")
    above, below = neighbours(band, band, "gx")
    c_before, c_after = neighbours(c_left, c_right, "row")
    above, below, c_before, c_after = lax.optimization_barrier((above, below, c_before, c_after))
    c_top, c_bottom = edges(EARLY, c_before, c_own, c_after)
    side = shape((B, 16, y_at(LATE, 2)), BF16)
    (
        frame, hidden_01, hidden_2, hidden_3,
        slope_0, slope_1, slope_2, own_3, own, left, right,
    ) = call(
        forward_kernel,
        [
            shape((N, 64, N * Z), BF16),
            shape((N, 32, N * Z), BF16),
            shape((N, 16, N * Z), BF16),
            shape((B, 16, B * Z), BF16),
            shape((B + 2, 16, (B + 2) * Z), F32),
            shape((B + 4, 16, (B + 4) * Z), F32),
            shape((B, 16, B * Z), F32),
            shape((B, 48, B * Z), BF16),
            shape((B, 32, B * Z), BF16),
            side,
            side,
        ],
        [above, band, below, w0, w1, w2, w3, bias, carried],
        [pltpu.VMEM((3 * B, 16, 3 * B * Z), BF16)] * 3,
        name="forward",
    )
    before, after = neighbours(left, right, "row")
    c_top, c_bottom, _ = lax.optimization_barrier((c_top, c_bottom, left))
    c_above, c_below = neighbours(c_top, c_bottom, "gx")
    before, after, c_above, c_below = lax.optimization_barrier((before, after, c_above, c_below))
    top, bottom = edges(LATE, before, own, after)
    above, below = neighbours(top, bottom, "gx")
    output, grad_3, grad_merge = call(
        merge_kernel,
        [shape((1024, Z), F32), shape((432, Z), F32), shape((144, Z), F32)],
        [frame, hidden_01, hidden_2, hidden_3, own_3, merging_weight, merge_bias, merge_grad],
        flops=100_000_000,
        name="merge",
    )
    spreads = [shape((3 * B, 48, 3 * B * Z), BF16)] * 4
    *spreads, kept, sent = call(
        backward_kernel,
        spreads + [shape((HALF, Z), F32), shape((HALF, Z), BF16)],
        [above, below, before, own, after, c_above, c_below, c_before, c_own, c_after, t1, t2, t3, slope_0, slope_1, slope_2, carried]
        + [frame, hidden_01, grad_3, grad_merge],
        [pltpu.VMEM((2 * HALF, Z), F32)],
        name="backward",
    )
    axes = ("gx", "row")
    swap = [(0, 1), (1, 0)]
    half_sum = shape((HALF, Z), BF16)
    (paired,) = call(pair_kernel, [half_sum], [kept, lax.ppermute(sent, "rep", swap)], name="pair")
    spread_sums = lax.all_to_all(paired.reshape(GROUP, ROWS, Z), axes, 0, 0, tiled=True)
    (added,) = call(add_kernel, [half_sum], [spread_sums.reshape(HALF, Z)], name="add")
    totals = lax.all_to_all(added.reshape(GROUP, ROWS, Z), axes, 0, 0, tiled=True)
    totals = totals.reshape(HALF, Z)
    others = lax.ppermute(totals, "rep", swap)
    (grad_input,) = call(
        last_kernel,
        [shape((1024, Z), F32)],
        spreads + [t0, t1, t2, t3, base],
        flops=300_000_000,
        name="input_gradient",
    )
    unpacked = call(
        functools.partial(unpack_kernel, scale),
        [shape((432, k.shape[2]), F32) for k in kernels]
        + [shape((4, 16), F32), shape((64, 128), F32), shape((1, 64), F32)],
        [totals, others],
        [pltpu.VMEM((2 * HALF, Z), F32)],
        name="unpack",
    )
    grad_kernels = [g.reshape(27, 16, g.shape[1]).transpose(1, 0, 2) for g in unpacked[:4]]
    out_shape = (1, 64, B, B, Z)
    return (
        output.reshape(out_shape),
        grad_input.reshape(out_shape),
        *grad_kernels,
        unpacked[4],
        unpacked[5],
        unpacked[6].reshape(64),
    )


def solution(mesh):
    split = P("rep", None, "gx", "row", None)
    return jax.shard_map(
        body,
        mesh=mesh,
        in_specs=(split, split) + (P(),) * 7,
        out_specs=(split, split) + (P(),) * 7,
        check_vma=False,
    )
```

```python
import functools
import math

import jax
import jax.numpy as jnp
from jax import lax
from jax.experimental import pallas as pl
from jax.experimental.pallas import tpu as pltpu
from jax.sharding import PartitionSpec as P

BETA = 0.2
BF16, F32 = jnp.bfloat16, jnp.float32
Z = 128
B = 4
H = 2
N = B + 2 * H
MID = slice(H * Z, (H + B) * Z)
EARLY, LATE = (3, 2, 1), (4, 3)
RING = slice((H - 1) * Z, (H + B + 1) * Z)
GROUP = 128
ROWS = 8
HALF = GROUP * ROWS
VMEM_LIMIT = 24 * 2**20


def shape(dims, dtype):
    return jax.ShapeDtypeStruct(dims, dtype)


def call(kernel, outs, args, scratch=(), flops=1_000_000, name=None):
    moved = sum(math.prod(a.shape) * a.dtype.itemsize for a in list(args) + list(outs))
    return pl.pallas_call(
        kernel,
        out_shape=list(outs),
        in_specs=[pl.BlockSpec(memory_space=pltpu.VMEM)] * len(args),
        out_specs=[pl.BlockSpec(memory_space=pltpu.VMEM)] * len(outs),
        scratch_shapes=list(scratch),
        compiler_params=pltpu.CompilerParams(vmem_limit_bytes=VMEM_LIMIT),
        cost_estimate=pl.CostEstimate(flops=flops, bytes_accessed=moved, transcendentals=0),
        name=name,
    )(*args)


def lane_moves(rows, width):
    lane = lax.broadcasted_iota(jnp.int32, (rows, width), 1) % Z
    return lane != 0, lane != Z - 1


def from_left(v, keep):
    parts = [pltpu.roll(v[:, k * Z : (k + 1) * Z], 1, 1) for k in range(v.shape[1] // Z)]
    return jnp.where(keep, jnp.concatenate(parts, axis=1), jnp.zeros_like(v))


def from_right(v, keep):
    parts = [pltpu.roll(v[:, k * Z : (k + 1) * Z], Z - 1, 1) for k in range(v.shape[1] // Z)]
    return jnp.where(keep, jnp.concatenate(parts, axis=1), jnp.zeros_like(v))


def spread(v):
    not_first, not_last = lane_moves(*v.shape)
    return jnp.concatenate([from_right(v, not_last), v, from_left(v, not_first)], axis=0)


def inside(x, y, blocks):
    x = lax.axis_index("gx") * B + x
    block = lax.broadcasted_iota(jnp.int32, (1, blocks * Z), 1) // Z
    y = lax.axis_index("row") * B + block + y
    in_x = (x >= 0) & (x < lax.axis_size("gx") * B)
    in_y = (y >= 0) & (y < lax.axis_size("row") * B)
    return jnp.where(in_y, 1.0, 0.0) * jnp.where(in_x, 1.0, 0.0)


def as_column(row):
    n = row.shape[1]
    rows = lax.broadcasted_iota(jnp.int32, (n, n), 0)
    lanes = lax.broadcasted_iota(jnp.int32, (n, n), 1)
    return jnp.sum(jnp.where(rows == lanes, row, 0.0), axis=1, keepdims=True)


def conv_row(kernel_ref, sources, i, lanes):
    n = lanes.stop - lanes.start
    cut = slice(lanes.start - Z, lanes.stop + Z)
    rhs = jnp.concatenate([s(i + a - 1, cut) for a in range(3) for s in sources], axis=0)
    got = jnp.dot(kernel_ref[...], rhs, preferred_element_type=F32)
    acc = got[:48, :n] + got[48:96, Z : Z + n] + got[96:, 2 * Z :]
    not_first, not_last = lane_moves(16, n)
    return from_left(acc[:16], not_first) + acc[16:32] + from_right(acc[32:], not_last)


def back_row(turned_ref, channels, spread_ref, i, lanes):
    n, q = lanes.stop - lanes.start, channels.stop - channels.start
    cut = slice(lanes.start - Z, lanes.stop + Z)
    lhs = jnp.concatenate([turned_ref[b, channels] for b in range(3)], axis=0)
    rhs = jnp.concatenate([spread_ref[i + 1 - a, :, cut] for a in range(3)], axis=0)
    got = jnp.dot(lhs, rhs, preferred_element_type=F32)
    return got[:q, 2 * Z :] + got[q : 2 * q, Z : Z + n] + got[2 * q :, :n]


def kernel_gradient(own, sources):
    lhs = jnp.concatenate(
        [jnp.concatenate([layer[i] for layer in own], axis=0) for i in range(B)], axis=1
    )
    for a in range(3):
        taps = [
            jnp.concatenate(
                [
                    jnp.concatenate(
                        [s[H + i + a - 1, :, pl.ds((H + b - 1) * Z, B * Z)] for s in sources], axis=0
                    )
                    for i in range(B)
                ],
                axis=1,
            )
            for b in range(3)
        ]
        q = taps[0].shape[0]
        got = lax.dot_general(
            lhs, jnp.concatenate(taps, axis=0), (((1,), (1,)), ((), ())), preferred_element_type=F32
        )
        gap = jnp.zeros((got.shape[0], Z - q), F32)
        for b in range(3):
            yield 3 * a + b, jnp.concatenate([got[:, q * b : q * (b + 1)], gap], axis=1)


def own_cells(spread_ref):
    return [spread_ref[B + i, :, slice(B * Z, 2 * B * Z)] for i in range(B)]


def activate(value):
    sigmoid = jax.nn.sigmoid(value)
    return 0.2 * value + 0.8 * value * sigmoid, 0.2 + 0.8 * (
        sigmoid + value * sigmoid * (1.0 - sigmoid)
    )


def y_at(widths, u):
    return Z * sum(widths[:u])


def x_at(widths, u):
    return Z * sum(w * (B + 2 * w) for w in widths[:u])


def ring_row(parts, widths, u, f):
    above, below, before, own, after = parts
    w = widths[u]
    if B <= f < 2 * B:
        side = slice(y_at(widths, u), y_at(widths, u + 1))
        i = f - B
        return jnp.concatenate(
            [before[i, :, side], own[i, 16 * u : 16 * (u + 1)], after[i, :, side]], axis=1
        )
    ref, r = (above, f - B + w) if f < B else (below, f - 2 * B)
    at = x_at(widths, u) + r * (B + 2 * w) * Z
    return ref[:, at : at + (B + 2 * w) * Z]


def put(widths, i, ready, own, left, right):
    own[i] = jnp.concatenate(ready, axis=0)
    left[i] = jnp.concatenate([v[:, : w * Z] for v, w in zip(ready, widths)], axis=1)
    right[i] = jnp.concatenate([v[:, (B - w) * Z :] for v, w in zip(ready, widths)], axis=1)


def wide_sum(blocks):
    total = sum(block.astype(F32) for block in blocks)
    return jnp.broadcast_to(jnp.sum(total, axis=1, keepdims=True), (total.shape[0], Z))


def cell_sum(own):
    return wide_sum([rows[16:32] for rows in own])


def pack_kernel(x_ref, out_ref, wide):
    wide[...] = x_ref[...].astype(F32)
    for i in range(B):
        row = [wide[pl.ds(B * i + j, 64, stride=B * B), :].astype(BF16) for j in range(B)]
        out_ref[i] = jnp.concatenate(row, axis=1)


def band_kernel(before, own, after, out_ref):
    for k, ref in enumerate((before, own, after)):
        out_ref[:, :, k * B * Z : (k + 1) * B * Z] = ref[...]


def edges_kernel(c_before, c_own, c_after, before, own, after, top, bottom):
    first = 0
    for widths, *y_parts in ((EARLY, c_before, c_own, c_after), (LATE, before, own, after)):
        parts = (None, None, *y_parts)
        for u, w in enumerate(widths):
            for r in range(w):
                at = first + x_at(widths, u) + r * (B + 2 * w) * Z
                lanes = slice(at, at + (B + 2 * w) * Z)
                top[:, lanes] = ring_row(parts, widths, u, B + r)
                bottom[:, lanes] = ring_row(parts, widths, u, 2 * B - w + r)
        first += x_at(widths, len(widths))


def prepare_kernel(
    cot_ref, merge, layer_bias, merging_bias, k0, k1, k2, k3,
    base, carried, merge_grad, bias, merge_bias, w0, w1, w2, w3, t0, t1, t2, t3, own, left, right, wide,
):
    for k in range(4):
        column = as_column(layer_bias[k : k + 1].astype(F32))
        bias[16 * k : 16 * (k + 1)] = jnp.broadcast_to(column, (16, Z))
    merge_bias[...] = jnp.broadcast_to(as_column(merging_bias[...].astype(F32)), (64, Z))
    for k_ref, w_ref, t_ref in ((k0, w0, t0), (k1, w1, t1), (k2, w2, t2), (k3, w3, t3)):
        w_ref[...] = jnp.concatenate([k_ref[144 * a : 144 * (a + 1)] for a in range(3)], axis=1)
        for b in range(3):
            rows = [k_ref[48 * t : 48 * (t + 1)] for t in (b, 3 + b, 6 + b)]
            t_ref[b] = jnp.transpose(jnp.concatenate(rows, axis=0).astype(F32)).astype(BF16)
    wide[...] = cot_ref[...].astype(F32)
    merge_t = jnp.transpose(merge[...].astype(F32)).astype(BF16)
    for i in range(B):
        cot = jnp.concatenate(
            [wide[pl.ds(B * i + j, 64, stride=B * B), :] for j in range(B)], axis=1
        )
        grad = (BETA * cot).astype(BF16)
        merge_grad[i] = grad
        back = jnp.dot(merge_t, grad, preferred_element_type=F32)
        base[i] = cot + back[:64]
        carried[i] = back[64:]
        ready = [back[64 + 16 * k : 80 + 16 * k].astype(BF16) for k in (2, 1, 0)]
        put(EARLY, i, ready, own, left, right)


def forward_kernel(
    above, band, below, k0, k1, k2, k3, bias, carried,
    frame, hidden_01, hidden_2, hidden_3, slope_0, slope_1, slope_2, own_3, own, left, right,
    wide_0, wide_1, wide_2,
):
    bands = (above, band, below)
    near = slice((B - H) * Z, (2 * B + H) * Z)
    sources = [lambda i, cut: bands[i // B][i % B, :, cut]]
    for i in range(N):
        frame[i] = sources[0](i + B - H, near)
    for k, (kernel_ref, wide) in enumerate(((k0, wide_0), (k1, wide_1), (k2, wide_2))):
        reach = 3 - k
        lanes = slice((B - reach) * Z, (2 * B + reach) * Z)
        for i in range(B - reach, 2 * B + reach):
            pre = conv_row(kernel_ref, sources, i, lanes) + bias[16 * k : 16 * (k + 1), 0:1]
            value, slope = activate(pre)
            present = inside(i - B, -reach, B + 2 * reach)
            wide[i, :, lanes] = (value * present).astype(BF16)
            slope = slope * present
            if k == 0 and B - 1 <= i < 2 * B + 1:
                slope_0[i - B + 1] = slope[:, 2 * Z : (B + 4) * Z]
            if k == 1:
                slope_1[i - B + 2] = slope
            if k == 2 and B <= i < 2 * B:
                slope_2[i - B] = slope[:, Z : (B + 1) * Z]
        sources.append(lambda i, cut, wide=wide: wide[i, :, cut])
    for i in range(N):
        hidden_01[i, 0:16] = wide_0[i + B - H, :, near]
        hidden_01[i, 16:32] = wide_1[i + B - H, :, near]
        if 0 < i < N - 1:
            hidden_2[i, :, RING] = wide_2[i + B - H, :, slice((B - 1) * Z, (2 * B + 1) * Z)]
    for i in range(B):
        pre = conv_row(k3, sources, B + i, slice(B * Z, 2 * B * Z)) + bias[48:64, 0:1]
        value, slope = activate(pre)
        hidden_3[i] = value.astype(BF16)
        grad = (carried[i, 48:64] * slope).astype(BF16)
        own_3[i] = spread(grad)
        put(LATE, i, [grad, slope_2[i].astype(BF16)], own, left, right)


def merge_kernel(
    frame, hidden_01, hidden_2, hidden_3, own_3, merge, merge_bias, merge_grad,
    out_ref, grad_3, grad_merge,
):
    total = jnp.zeros((64, 128), F32)
    for i in range(B):
        base = frame[H + i, :, MID]
        joined = jnp.concatenate(
            [base, hidden_01[H + i, :, MID], hidden_2[H + i, :, MID], hidden_3[i]], axis=0
        )
        merged = jnp.dot(merge[...], joined, preferred_element_type=F32) + merge_bias[:, 0:1]
        out = base.astype(F32) + BETA * merged
        for j in range(B):
            out_ref[pl.ds(B * i + j, 64, stride=B * B), :] = out[:, j * Z : (j + 1) * Z]
        grad = merge_grad[i]
        total = total + lax.dot_general(
            grad, joined, (((1,), (1,)), ((), ())), preferred_element_type=F32
        )
    grad_merge[0:64] = total
    grad_merge[64:128] = wide_sum([merge_grad[i] for i in range(B)])
    own = [own_3[i] for i in range(B)]
    grad_merge[128:144] = cell_sum(own)
    for t, got in kernel_gradient([own], [frame, hidden_01, hidden_2]):
        grad_3[48 * t : 48 * (t + 1)] = got


def backward_kernel(
    above, below, before, own, after, c_before, c_own, c_after,
    t1, t2, t3, slope_0, slope_1, slope_2, carried,
    frame, hidden_01, grad_3, grad_merge,
    spread_0, spread_1, spread_2, spread_3, kept, sent, sums,
):
    cut = x_at(EARLY, 3)
    early = (above.at[:, :cut], below.at[:, :cut], c_before, c_own, c_after)
    late = (above.at[:, cut:], below.at[:, cut:], before, own, after)
    spreads = (spread_0, spread_1, spread_2, spread_3)
    turned_refs = (None, t1, t2, t3)
    for f in range(3 * B):
        spread_3[f] = spread(ring_row(late, LATE, 0, f))
    for k in (2, 1, 0):
        reach = k + 1
        lanes = slice((B - reach) * Z, (2 * B + reach) * Z)
        middle = slice(reach * Z, (B + reach) * Z)
        channels = slice(64 + 16 * k, 80 + 16 * k)
        for f in range(B - reach, 2 * B + reach):
            i = f - B
            here = 0 <= i < B
            got = ring_row(early, EARLY, 2 - k, f).astype(F32)
            if here:
                exact = carried[i, 16 * k : 16 * (k + 1)]
                got = jnp.concatenate([got[:, : middle.start], exact, got[:, middle.stop :]], axis=1)
            for m in range(k + 1, 4):
                got = got + back_row(turned_refs[m], channels, spreads[m], f, lanes)
            if k == 2:
                slope = ring_row(late, LATE, 1, f).astype(F32)
                if here:
                    slope = jnp.concatenate(
                        [slope[:, : middle.start], slope_2[i], slope[:, middle.stop :]], axis=1
                    )
            else:
                slope = (slope_0, slope_1)[k][i + reach]
            grad = (got * slope).astype(BF16)
            spreads[k][f, :, lanes] = spread(grad)
    owns = [own_cells(ref) for ref in spreads[:3]]
    for t, got in kernel_gradient(owns, [frame, hidden_01]):
        for k in range(3):
            at = 432 * k + 48 * t
            sums[at : at + 48] = got[48 * k : 48 * (k + 1)]
    sums[1296:1728] = grad_3[...]
    sums[1728:1856] = grad_merge[0:128]
    for k in range(3):
        sums[1856 + 16 * k : 1872 + 16 * k] = cell_sum(owns[k])
    sums[1904:1920] = grad_merge[128:144]
    sums[1920:] = jnp.zeros((2 * HALF - 1920, Z), F32)
    mine, other = halves()
    kept[...] = sums[pl.ds(mine, HALF), :]
    sent[...] = sums[pl.ds(other, HALF), :].astype(BF16)


def last_kernel(spread_0, spread_1, spread_2, spread_3, t0, t1, t2, t3, base, out_ref):
    for i in range(B):
        out = base[i]
        for ref, turned_ref in zip((spread_0, spread_1, spread_2, spread_3), (t0, t1, t2, t3)):
            out = out + back_row(turned_ref, slice(0, 64), ref, B + i, slice(B * Z, 2 * B * Z))
        for j in range(B):
            out_ref[pl.ds(B * i + j, 64, stride=B * B), :] = out[:, j * Z : (j + 1) * Z]


def halves():
    first = lax.axis_index("rep") * HALF
    return pl.multiple_of(first, HALF), pl.multiple_of(HALF - first, HALF)


def pair_kernel(kept, came, out_ref):
    out_ref[...] = (kept[...] + came[...].astype(F32)).astype(BF16)


def add_kernel(x_ref, out_ref):
    def step(k, acc):
        return acc + x_ref[pl.ds(pl.multiple_of(k * 128, 128), 128), :].astype(F32)

    acc = lax.fori_loop(0, HALF // 128, step, jnp.zeros((128, Z), F32))
    total = acc[0:ROWS]
    for k in range(1, 128 // ROWS):
        total = total + acc[k * ROWS : (k + 1) * ROWS]
    block = jnp.concatenate([total] * (128 // ROWS), axis=0).astype(BF16)

    def put(k, carry):
        out_ref[pl.ds(pl.multiple_of(k * 128, 128), 128), :] = block
        return carry

    lax.fori_loop(0, HALF // 128, put, 0)


def turned(block):
    rows = lax.broadcasted_iota(jnp.int32, block.shape, 0)
    lanes = lax.broadcasted_iota(jnp.int32, block.shape, 1)
    return jnp.sum(jnp.where(rows == lanes, block, 0.0), axis=0, keepdims=True)


def unpack_kernel(scale, mine_ref, other_ref, g0, g1, g2, g3, bias, weight, weight_bias, sums):
    mine, other = halves()
    sums[pl.ds(mine, HALF), :] = mine_ref[...].astype(F32) * scale
    sums[pl.ds(other, HALF), :] = other_ref[...].astype(F32) * scale
    for k, g in enumerate((g0, g1, g2, g3)):
        g[...] = sums[432 * k : 432 * (k + 1), : g.shape[1]]
    weight[...] = sums[1728:1792]
    weight_bias[...] = turned(sums[1792:1856])[:, :64]
    for k in range(4):
        bias[k : k + 1] = turned(sums[1856 + 16 * k : 1872 + 16 * k])[:, :16]


def neighbours(low, high, axis):
    up = [(i, i + 1) for i in range(lax.axis_size(axis) - 1)]
    return lax.ppermute(high, axis, up), lax.ppermute(low, axis, [(j, i) for i, j in up])


def body(samples, cotangent, kernel_0, kernel_1, kernel_2, kernel_3, layer_bias, merging_weight, merging_bias):
    kernels = (kernel_0, kernel_1, kernel_2, kernel_3)
    cells = B * B * Z * lax.axis_size("gx") * lax.axis_size("row") * lax.axis_size("rep")
    scale = 1.0 / math.sqrt(cells)
    flat = [k.transpose(1, 0, 2).reshape(432, k.shape[2]) for k in kernels]
    columns = shape((64, Z), F32)
    wide = pltpu.VMEM((1024, Z), F32)
    (own,) = call(
        pack_kernel,
        [shape((B, 64, B * Z), BF16)],
        [samples.reshape(1024, Z)],
        [wide],
        name="pack",
    )
    base, carried, merge_grad, bias, merge_bias, w0, w1, w2, w3, t0, t1, t2, t3, c_own, c_left, c_right = call(
        prepare_kernel,
        [shape((B, 64, B * Z), F32)] * 2
        + [shape((B, 64, B * Z), BF16), columns, columns]
        + [shape((144, 3 * k.shape[2]), BF16) for k in kernels]
        + [shape((3, k.shape[2], 144), BF16) for k in kernels]
        + [shape((B, 48, B * Z), BF16)]
        + [shape((B, 16, y_at(EARLY, 3)), BF16)] * 2,
        [cotangent.reshape(1024, Z), merging_weight, layer_bias, merging_bias.reshape(1, 64)] + flat,
        [wide],
        flops=40_000_000,
        name="prepare",
    )
    before, after = neighbours(own, own, "row")
    (band,) = call(band_kernel, [shape((B, 64, 3 * B * Z), BF16)], [before, own, after], name="band")
    above, below = neighbours(band, band, "gx")
    c_before, c_after = neighbours(c_left, c_right, "row")
    above, below, c_before, c_after = lax.optimization_barrier((above, below, c_before, c_after))
    side = shape((B, 16, y_at(LATE, 2)), BF16)
    (
        frame, hidden_01, hidden_2, hidden_3,
        slope_0, slope_1, slope_2, own_3, own, left, right,
    ) = call(
        forward_kernel,
        [
            shape((N, 64, N * Z), BF16),
            shape((N, 32, N * Z), BF16),
            shape((N, 16, N * Z), BF16),
            shape((B, 16, B * Z), BF16),
            shape((B + 2, 16, (B + 2) * Z), F32),
            shape((B + 4, 16, (B + 4) * Z), F32),
            shape((B, 16, B * Z), F32),
            shape((B, 48, B * Z), BF16),
            shape((B, 32, B * Z), BF16),
            side,
            side,
        ],
        [above, band, below, w0, w1, w2, w3, bias, carried],
        [pltpu.VMEM((3 * B, 16, 3 * B * Z), BF16)] * 3,
        name="forward",
    )
    before, after = neighbours(left, right, "row")
    edge = shape((16, x_at(EARLY, 3) + x_at(LATE, 2)), BF16)
    top, bottom = call(
        edges_kernel,
        [edge, edge],
        [c_before, c_own, c_after, before, own, after],
        name="edges",
    )
    above, below = neighbours(top, bottom, "gx")
    output, grad_3, grad_merge = call(
        merge_kernel,
        [shape((1024, Z), F32), shape((432, Z), F32), shape((144, Z), F32)],
        [frame, hidden_01, hidden_2, hidden_3, own_3, merging_weight, merge_bias, merge_grad],
        flops=100_000_000,
        name="merge",
    )
    spreads = [shape((3 * B, 48, 3 * B * Z), BF16)] * 4
    *spreads, kept, sent = call(
        backward_kernel,
        spreads + [shape((HALF, Z), F32), shape((HALF, Z), BF16)],
        [above, below, before, own, after, c_before, c_own, c_after, t1, t2, t3, slope_0, slope_1, slope_2, carried]
        + [frame, hidden_01, grad_3, grad_merge],
        [pltpu.VMEM((2 * HALF, Z), F32)],
        name="backward",
    )
    axes = ("gx", "row")
    swap = [(0, 1), (1, 0)]
    half_sum = shape((HALF, Z), BF16)
    (paired,) = call(pair_kernel, [half_sum], [kept, lax.ppermute(sent, "rep", swap)], name="pair")
    spread_sums = lax.all_to_all(paired.reshape(GROUP, ROWS, Z), axes, 0, 0, tiled=True)
    (added,) = call(add_kernel, [half_sum], [spread_sums.reshape(HALF, Z)], name="add")
    totals = lax.all_to_all(added.reshape(GROUP, ROWS, Z), axes, 0, 0, tiled=True)
    totals = totals.reshape(HALF, Z)
    others = lax.ppermute(totals, "rep", swap)
    (grad_input,) = call(
        last_kernel,
        [shape((1024, Z), F32)],
        spreads + [t0, t1, t2, t3, base],
        flops=300_000_000,
        name="input_gradient",
    )
    unpacked = call(
        functools.partial(unpack_kernel, scale),
        [shape((432, k.shape[2]), F32) for k in kernels]
        + [shape((4, 16), F32), shape((64, 128), F32), shape((1, 64), F32)],
        [totals, others],
        [pltpu.VMEM((2 * HALF, Z), F32)],
        name="unpack",
    )
    grad_kernels = [g.reshape(27, 16, g.shape[1]).transpose(1, 0, 2) for g in unpacked[:4]]
    out_shape = (1, 64, B, B, Z)
    return (
        output.reshape(out_shape),
        grad_input.reshape(out_shape),
        *grad_kernels,
        unpacked[4],
        unpacked[5],
        unpacked[6].reshape(64),
    )


def solution(mesh):
    split = P("rep", None, "gx", "row", None)
    return jax.shard_map(
        body,
        mesh=mesh,
        in_specs=(split, split) + (P(),) * 7,
        out_specs=(split, split) + (P(),) * 7,
        check_vma=False,
    )
```

```python
import functools
import math

import jax
import jax.numpy as jnp
from jax import lax
from jax.experimental import pallas as pl
from jax.experimental.pallas import tpu as pltpu
from jax.sharding import PartitionSpec as P

BETA = 0.2
BF16, F32 = jnp.bfloat16, jnp.float32
Z = 128
B = 4
H = 2
N = B + 2 * H
MID = slice(H * Z, (H + B) * Z)
WIDTHS = (4, 3, 3, 2, 1)
Y_AT = tuple(Z * sum(WIDTHS[:u]) for u in range(6))
X_AT = tuple(Z * sum(w * (B + 2 * w) for w in WIDTHS[:u]) for u in range(6))
RING = slice((H - 1) * Z, (H + B + 1) * Z)
GROUP = 128
ROWS = 8
HALF = GROUP * ROWS
VMEM_LIMIT = 24 * 2**20


def shape(dims, dtype):
    return jax.ShapeDtypeStruct(dims, dtype)


def call(kernel, outs, args, scratch=(), flops=1_000_000, name=None):
    moved = sum(math.prod(a.shape) * a.dtype.itemsize for a in list(args) + list(outs))
    return pl.pallas_call(
        kernel,
        out_shape=list(outs),
        in_specs=[pl.BlockSpec(memory_space=pltpu.VMEM)] * len(args),
        out_specs=[pl.BlockSpec(memory_space=pltpu.VMEM)] * len(outs),
        scratch_shapes=list(scratch),
        compiler_params=pltpu.CompilerParams(vmem_limit_bytes=VMEM_LIMIT),
        cost_estimate=pl.CostEstimate(flops=flops, bytes_accessed=moved, transcendentals=0),
        name=name,
    )(*args)


def lane_moves(rows, width):
    lane = lax.broadcasted_iota(jnp.int32, (rows, width), 1) % Z
    return lane != 0, lane != Z - 1


def from_left(v, keep):
    parts = [pltpu.roll(v[:, k * Z : (k + 1) * Z], 1, 1) for k in range(v.shape[1] // Z)]
    return jnp.where(keep, jnp.concatenate(parts, axis=1), jnp.zeros_like(v))


def from_right(v, keep):
    parts = [pltpu.roll(v[:, k * Z : (k + 1) * Z], Z - 1, 1) for k in range(v.shape[1] // Z)]
    return jnp.where(keep, jnp.concatenate(parts, axis=1), jnp.zeros_like(v))


def spread(v):
    not_first, not_last = lane_moves(*v.shape)
    return jnp.concatenate([from_right(v, not_last), v, from_left(v, not_first)], axis=0)


def inside(x, y, blocks):
    x = lax.axis_index("gx") * B + x
    block = lax.broadcasted_iota(jnp.int32, (1, blocks * Z), 1) // Z
    y = lax.axis_index("row") * B + block + y
    in_x = (x >= 0) & (x < lax.axis_size("gx") * B)
    in_y = (y >= 0) & (y < lax.axis_size("row") * B)
    return jnp.where(in_y, 1.0, 0.0) * jnp.where(in_x, 1.0, 0.0)


def as_column(row):
    n = row.shape[1]
    rows = lax.broadcasted_iota(jnp.int32, (n, n), 0)
    lanes = lax.broadcasted_iota(jnp.int32, (n, n), 1)
    return jnp.sum(jnp.where(rows == lanes, row, 0.0), axis=1, keepdims=True)


def conv_row(kernel_ref, sources, i, lanes):
    n = lanes.stop - lanes.start
    cut = slice(lanes.start - Z, lanes.stop + Z)
    rhs = jnp.concatenate([s(i + a - 1, cut) for a in range(3) for s in sources], axis=0)
    got = jnp.dot(kernel_ref[...], rhs, preferred_element_type=F32)
    acc = got[:48, :n] + got[48:96, Z : Z + n] + got[96:, 2 * Z :]
    not_first, not_last = lane_moves(16, n)
    return from_left(acc[:16], not_first) + acc[16:32] + from_right(acc[32:], not_last)


def back_row(turned_ref, channels, spread_ref, i, lanes):
    n, q = lanes.stop - lanes.start, channels.stop - channels.start
    cut = slice(lanes.start - Z, lanes.stop + Z)
    lhs = jnp.concatenate([turned_ref[b, channels] for b in range(3)], axis=0)
    rhs = jnp.concatenate([spread_ref[i + 1 - a, :, cut] for a in range(3)], axis=0)
    got = jnp.dot(lhs, rhs, preferred_element_type=F32)
    return got[:q, 2 * Z :] + got[q : 2 * q, Z : Z + n] + got[2 * q :, :n]


def kernel_gradient(own, sources):
    lhs = jnp.concatenate(
        [jnp.concatenate([layer[i] for layer in own], axis=0) for i in range(B)], axis=1
    )
    for a in range(3):
        taps = [
            jnp.concatenate(
                [
                    jnp.concatenate(
                        [s[H + i + a - 1, :, pl.ds((H + b - 1) * Z, B * Z)] for s in sources], axis=0
                    )
                    for i in range(B)
                ],
                axis=1,
            )
            for b in range(3)
        ]
        q = taps[0].shape[0]
        got = lax.dot_general(
            lhs, jnp.concatenate(taps, axis=0), (((1,), (1,)), ((), ())), preferred_element_type=F32
        )
        gap = jnp.zeros((got.shape[0], Z - q), F32)
        for b in range(3):
            yield 3 * a + b, jnp.concatenate([got[:, q * b : q * (b + 1)], gap], axis=1)


def own_cells(spread_ref):
    return [spread_ref[B + i, :, slice(B * Z, 2 * B * Z)] for i in range(B)]


def activate(value):
    sigmoid = jax.nn.sigmoid(value)
    return 0.2 * value + 0.8 * value * sigmoid, 0.2 + 0.8 * (
        sigmoid + value * sigmoid * (1.0 - sigmoid)
    )


def ring_row(parts, u, f):
    above, below, before, own, after = parts
    w = WIDTHS[u]
    if B <= f < 2 * B:
        side = slice(Y_AT[u], Y_AT[u + 1])
        i = f - B
        return jnp.concatenate(
            [before[i, :, side], own[i, 16 * u : 16 * (u + 1)], after[i, :, side]], axis=1
        )
    ref, r = (above, f - B + w) if f < B else (below, f - 2 * B)
    at = X_AT[u] + r * (B + 2 * w) * Z
    return ref[:, at : at + (B + 2 * w) * Z]


def wide_sum(blocks):
    total = sum(block.astype(F32) for block in blocks)
    return jnp.broadcast_to(jnp.sum(total, axis=1, keepdims=True), (total.shape[0], Z))


def cell_sum(own):
    return wide_sum([rows[16:32] for rows in own])


def pack_kernel(x_ref, out_ref, wide):
    wide[...] = x_ref[...].astype(F32)
    for i in range(B):
        row = [wide[pl.ds(B * i + j, 64, stride=B * B), :].astype(BF16) for j in range(B)]
        out_ref[i] = jnp.concatenate(row, axis=1)


def band_kernel(before, own, after, out_ref):
    for k, ref in enumerate((before, own, after)):
        out_ref[:, :, k * B * Z : (k + 1) * B * Z] = ref[...]


def edges_kernel(before, own, after, top, bottom):
    for u, w in enumerate(WIDTHS):
        parts = (top, bottom, before, own, after)
        for r in range(w):
            at = X_AT[u] + r * (B + 2 * w) * Z
            lanes = slice(at, at + (B + 2 * w) * Z)
            top[:, lanes] = ring_row(parts, u, B + r)
            bottom[:, lanes] = ring_row(parts, u, 2 * B - w + r)


def prepare_kernel(
    cot_ref, merge, layer_bias, merging_bias, k0, k1, k2, k3,
    base, carried, merge_grad, bias, merge_bias, w0, w1, w2, w3, t0, t1, t2, t3, wide,
):
    for k in range(4):
        column = as_column(layer_bias[k : k + 1].astype(F32))
        bias[16 * k : 16 * (k + 1)] = jnp.broadcast_to(column, (16, Z))
    merge_bias[...] = jnp.broadcast_to(as_column(merging_bias[...].astype(F32)), (64, Z))
    for k_ref, w_ref, t_ref in ((k0, w0, t0), (k1, w1, t1), (k2, w2, t2), (k3, w3, t3)):
        w_ref[...] = jnp.concatenate([k_ref[144 * a : 144 * (a + 1)] for a in range(3)], axis=1)
        for b in range(3):
            rows = [k_ref[48 * t : 48 * (t + 1)] for t in (b, 3 + b, 6 + b)]
            t_ref[b] = jnp.transpose(jnp.concatenate(rows, axis=0).astype(F32)).astype(BF16)
    wide[...] = cot_ref[...].astype(F32)
    merge_t = jnp.transpose(merge[...].astype(F32)).astype(BF16)
    for i in range(B):
        cot = jnp.concatenate(
            [wide[pl.ds(B * i + j, 64, stride=B * B), :] for j in range(B)], axis=1
        )
        grad = (BETA * cot).astype(BF16)
        merge_grad[i] = grad
        back = jnp.dot(merge_t, grad, preferred_element_type=F32)
        base[i] = cot + back[:64]
        carried[i] = back[64:]


def forward_kernel(
    above, band, below, k0, k1, k2, k3, bias, carried,
    frame, hidden_01, hidden_2, hidden_3, slope_0, slope_1, slope_2, own_3, own, left, right,
    wide_0, wide_1, wide_2,
):
    bands = (above, band, below)
    near = slice((B - H) * Z, (2 * B + H) * Z)
    sources = [lambda i, cut: bands[i // B][i % B, :, cut]]
    for i in range(N):
        frame[i] = sources[0](i + B - H, near)
    for k, (kernel_ref, wide) in enumerate(((k0, wide_0), (k1, wide_1), (k2, wide_2))):
        reach = 3 - k
        lanes = slice((B - reach) * Z, (2 * B + reach) * Z)
        for i in range(B - reach, 2 * B + reach):
            pre = conv_row(kernel_ref, sources, i, lanes) + bias[16 * k : 16 * (k + 1), 0:1]
            value, slope = activate(pre)
            present = inside(i - B, -reach, B + 2 * reach)
            wide[i, :, lanes] = (value * present).astype(BF16)
            slope = slope * present
            if k == 0 and B - 1 <= i < 2 * B + 1:
                slope_0[i - B + 1] = slope[:, 2 * Z : (B + 4) * Z]
            if k == 1:
                slope_1[i - B + 2] = slope
            if k == 2 and B <= i < 2 * B:
                slope_2[i - B] = slope[:, Z : (B + 1) * Z]
        sources.append(lambda i, cut, wide=wide: wide[i, :, cut])
    for i in range(N):
        hidden_01[i, 0:16] = wide_0[i + B - H, :, near]
        hidden_01[i, 16:32] = wide_1[i + B - H, :, near]
        if 0 < i < N - 1:
            hidden_2[i, :, RING] = wide_2[i + B - H, :, slice((B - 1) * Z, (2 * B + 1) * Z)]
    for i in range(B):
        pre = conv_row(k3, sources, B + i, slice(B * Z, 2 * B * Z)) + bias[48:64, 0:1]
        value, slope = activate(pre)
        hidden_3[i] = value.astype(BF16)
        grad = (carried[i, 48:64] * slope).astype(BF16)
        own_3[i] = spread(grad)
        rest = [slope_2[i]] + [carried[i, 16 * k : 16 * (k + 1)] for k in (2, 1, 0)]
        ready = [grad] + [value.astype(BF16) for value in rest]
        own[i] = jnp.concatenate(ready, axis=0)
        left[i] = jnp.concatenate([v[:, : w * Z] for v, w in zip(ready, WIDTHS)], axis=1)
        right[i] = jnp.concatenate([v[:, (B - w) * Z :] for v, w in zip(ready, WIDTHS)], axis=1)


def merge_kernel(
    frame, hidden_01, hidden_2, hidden_3, own_3, merge, merge_bias, merge_grad,
    out_ref, grad_3, grad_merge,
):
    total = jnp.zeros((64, 128), F32)
    for i in range(B):
        base = frame[H + i, :, MID]
        joined = jnp.concatenate(
            [base, hidden_01[H + i, :, MID], hidden_2[H + i, :, MID], hidden_3[i]], axis=0
        )
        merged = jnp.dot(merge[...], joined, preferred_element_type=F32) + merge_bias[:, 0:1]
        out = base.astype(F32) + BETA * merged
        for j in range(B):
            out_ref[pl.ds(B * i + j, 64, stride=B * B), :] = out[:, j * Z : (j + 1) * Z]
        grad = merge_grad[i]
        total = total + lax.dot_general(
            grad, joined, (((1,), (1,)), ((), ())), preferred_element_type=F32
        )
    grad_merge[0:64] = total
    grad_merge[64:128] = wide_sum([merge_grad[i] for i in range(B)])
    own = [own_3[i] for i in range(B)]
    grad_merge[128:144] = cell_sum(own)
    for t, got in kernel_gradient([own], [frame, hidden_01, hidden_2]):
        grad_3[48 * t : 48 * (t + 1)] = got


def backward_kernel(
    above, below, before, own, after, t1, t2, t3, slope_0, slope_1, slope_2, carried,
    frame, hidden_01, grad_3, grad_merge,
    spread_0, spread_1, spread_2, spread_3, kept, sent, sums,
):
    parts = (above, below, before, own, after)
    spreads = (spread_0, spread_1, spread_2, spread_3)
    turned_refs = (None, t1, t2, t3)
    for f in range(3 * B):
        spread_3[f] = spread(ring_row(parts, 0, f))
    for k in (2, 1, 0):
        reach = k + 1
        lanes = slice((B - reach) * Z, (2 * B + reach) * Z)
        middle = slice(reach * Z, (B + reach) * Z)
        channels = slice(64 + 16 * k, 80 + 16 * k)
        for f in range(B - reach, 2 * B + reach):
            i = f - B
            here = 0 <= i < B
            got = ring_row(parts, 4 - k, f).astype(F32)
            if here:
                exact = carried[i, 16 * k : 16 * (k + 1)]
                got = jnp.concatenate([got[:, : middle.start], exact, got[:, middle.stop :]], axis=1)
            for m in range(k + 1, 4):
                got = got + back_row(turned_refs[m], channels, spreads[m], f, lanes)
            if k == 2:
                slope = ring_row(parts, 1, f).astype(F32)
                if here:
                    slope = jnp.concatenate(
                        [slope[:, : middle.start], slope_2[i], slope[:, middle.stop :]], axis=1
                    )
            else:
                slope = (slope_0, slope_1)[k][i + reach]
            grad = (got * slope).astype(BF16)
            spreads[k][f, :, lanes] = spread(grad)
    owns = [own_cells(ref) for ref in spreads[:3]]
    for t, got in kernel_gradient(owns, [frame, hidden_01]):
        for k in range(3):
            at = 432 * k + 48 * t
            sums[at : at + 48] = got[48 * k : 48 * (k + 1)]
    sums[1296:1728] = grad_3[...]
    sums[1728:1856] = grad_merge[0:128]
    for k in range(3):
        sums[1856 + 16 * k : 1872 + 16 * k] = cell_sum(owns[k])
    sums[1904:1920] = grad_merge[128:144]
    sums[1920:] = jnp.zeros((2 * HALF - 1920, Z), F32)
    mine, other = halves()
    kept[...] = sums[pl.ds(mine, HALF), :]
    sent[...] = sums[pl.ds(other, HALF), :].astype(BF16)


def last_kernel(spread_0, spread_1, spread_2, spread_3, t0, t1, t2, t3, base, out_ref):
    for i in range(B):
        out = base[i]
        for ref, turned_ref in zip((spread_0, spread_1, spread_2, spread_3), (t0, t1, t2, t3)):
            out = out + back_row(turned_ref, slice(0, 64), ref, B + i, slice(B * Z, 2 * B * Z))
        for j in range(B):
            out_ref[pl.ds(B * i + j, 64, stride=B * B), :] = out[:, j * Z : (j + 1) * Z]


def halves():
    first = lax.axis_index("rep") * HALF
    return pl.multiple_of(first, HALF), pl.multiple_of(HALF - first, HALF)


def pair_kernel(kept, came, out_ref):
    out_ref[...] = (kept[...] + came[...].astype(F32)).astype(BF16)


def add_kernel(x_ref, out_ref):
    def step(k, acc):
        return acc + x_ref[pl.ds(pl.multiple_of(k * 128, 128), 128), :].astype(F32)

    acc = lax.fori_loop(0, HALF // 128, step, jnp.zeros((128, Z), F32))
    total = acc[0:ROWS]
    for k in range(1, 128 // ROWS):
        total = total + acc[k * ROWS : (k + 1) * ROWS]
    block = jnp.concatenate([total] * (128 // ROWS), axis=0).astype(BF16)

    def put(k, carry):
        out_ref[pl.ds(pl.multiple_of(k * 128, 128), 128), :] = block
        return carry

    lax.fori_loop(0, HALF // 128, put, 0)


def turned(block):
    rows = lax.broadcasted_iota(jnp.int32, block.shape, 0)
    lanes = lax.broadcasted_iota(jnp.int32, block.shape, 1)
    return jnp.sum(jnp.where(rows == lanes, block, 0.0), axis=0, keepdims=True)


def unpack_kernel(scale, mine_ref, other_ref, g0, g1, g2, g3, bias, weight, weight_bias, sums):
    mine, other = halves()
    sums[pl.ds(mine, HALF), :] = mine_ref[...].astype(F32) * scale
    sums[pl.ds(other, HALF), :] = other_ref[...].astype(F32) * scale
    for k, g in enumerate((g0, g1, g2, g3)):
        g[...] = sums[432 * k : 432 * (k + 1), : g.shape[1]]
    weight[...] = sums[1728:1792]
    weight_bias[...] = turned(sums[1792:1856])[:, :64]
    for k in range(4):
        bias[k : k + 1] = turned(sums[1856 + 16 * k : 1872 + 16 * k])[:, :16]


def neighbours(low, high, axis):
    up = [(i, i + 1) for i in range(lax.axis_size(axis) - 1)]
    return lax.ppermute(high, axis, up), lax.ppermute(low, axis, [(j, i) for i, j in up])


def body(samples, cotangent, kernel_0, kernel_1, kernel_2, kernel_3, layer_bias, merging_weight, merging_bias):
    kernels = (kernel_0, kernel_1, kernel_2, kernel_3)
    cells = B * B * Z * lax.axis_size("gx") * lax.axis_size("row") * lax.axis_size("rep")
    scale = 1.0 / math.sqrt(cells)
    flat = [k.transpose(1, 0, 2).reshape(432, k.shape[2]) for k in kernels]
    columns = shape((64, Z), F32)
    wide = pltpu.VMEM((1024, Z), F32)
    (own,) = call(
        pack_kernel,
        [shape((B, 64, B * Z), BF16)],
        [samples.reshape(1024, Z)],
        [wide],
        name="pack",
    )
    base, carried, merge_grad, bias, merge_bias, w0, w1, w2, w3, t0, t1, t2, t3 = call(
        prepare_kernel,
        [shape((B, 64, B * Z), F32)] * 2
        + [shape((B, 64, B * Z), BF16), columns, columns]
        + [shape((144, 3 * k.shape[2]), BF16) for k in kernels]
        + [shape((3, k.shape[2], 144), BF16) for k in kernels],
        [cotangent.reshape(1024, Z), merging_weight, layer_bias, merging_bias.reshape(1, 64)] + flat,
        [wide],
        flops=40_000_000,
        name="prepare",
    )
    before, after = neighbours(own, own, "row")
    (band,) = call(band_kernel, [shape((B, 64, 3 * B * Z), BF16)], [before, own, after], name="band")
    above, below = neighbours(band, band, "gx")
    side = shape((B, 16, Y_AT[5]), BF16)
    (
        frame, hidden_01, hidden_2, hidden_3,
        slope_0, slope_1, slope_2, own_3, own, left, right,
    ) = call(
        forward_kernel,
        [
            shape((N, 64, N * Z), BF16),
            shape((N, 32, N * Z), BF16),
            shape((N, 16, N * Z), BF16),
            shape((B, 16, B * Z), BF16),
            shape((B + 2, 16, (B + 2) * Z), F32),
            shape((B + 4, 16, (B + 4) * Z), F32),
            shape((B, 16, B * Z), F32),
            shape((B, 48, B * Z), BF16),
            shape((B, 80, B * Z), BF16),
            side,
            side,
        ],
        [above, band, below, w0, w1, w2, w3, bias, carried],
        [pltpu.VMEM((3 * B, 16, 3 * B * Z), BF16)] * 3,
        name="forward",
    )
    before, after = neighbours(left, right, "row")
    edge = shape((16, X_AT[5]), BF16)
    top, bottom = call(edges_kernel, [edge, edge], [before, own, after], name="edges")
    above, below = neighbours(top, bottom, "gx")
    output, grad_3, grad_merge = call(
        merge_kernel,
        [shape((1024, Z), F32), shape((432, Z), F32), shape((144, Z), F32)],
        [frame, hidden_01, hidden_2, hidden_3, own_3, merging_weight, merge_bias, merge_grad],
        flops=100_000_000,
        name="merge",
    )
    spreads = [shape((3 * B, 48, 3 * B * Z), BF16)] * 4
    *spreads, kept, sent = call(
        backward_kernel,
        spreads + [shape((HALF, Z), F32), shape((HALF, Z), BF16)],
        [above, below, before, own, after, t1, t2, t3, slope_0, slope_1, slope_2, carried]
        + [frame, hidden_01, grad_3, grad_merge],
        [pltpu.VMEM((2 * HALF, Z), F32)],
        name="backward",
    )
    axes = ("gx", "row")
    swap = [(0, 1), (1, 0)]
    half_sum = shape((HALF, Z), BF16)
    (paired,) = call(pair_kernel, [half_sum], [kept, lax.ppermute(sent, "rep", swap)], name="pair")
    spread_sums = lax.all_to_all(paired.reshape(GROUP, ROWS, Z), axes, 0, 0, tiled=True)
    (added,) = call(add_kernel, [half_sum], [spread_sums.reshape(HALF, Z)], name="add")
    totals = lax.all_to_all(added.reshape(GROUP, ROWS, Z), axes, 0, 0, tiled=True)
    totals = totals.reshape(HALF, Z)
    others = lax.ppermute(totals, "rep", swap)
    (grad_input,) = call(
        last_kernel,
        [shape((1024, Z), F32)],
        spreads + [t0, t1, t2, t3, base],
        flops=300_000_000,
        name="input_gradient",
    )
    unpacked = call(
        functools.partial(unpack_kernel, scale),
        [shape((432, k.shape[2]), F32) for k in kernels]
        + [shape((4, 16), F32), shape((64, 128), F32), shape((1, 64), F32)],
        [totals, others],
        [pltpu.VMEM((2 * HALF, Z), F32)],
        name="unpack",
    )
    grad_kernels = [g.reshape(27, 16, g.shape[1]).transpose(1, 0, 2) for g in unpacked[:4]]
    out_shape = (1, 64, B, B, Z)
    return (
        output.reshape(out_shape),
        grad_input.reshape(out_shape),
        *grad_kernels,
        unpacked[4],
        unpacked[5],
        unpacked[6].reshape(64),
    )


def solution(mesh):
    split = P("rep", None, "gx", "row", None)
    return jax.shard_map(
        body,
        mesh=mesh,
        in_specs=(split, split) + (P(),) * 7,
        out_specs=(split, split) + (P(),) * 7,
        check_vma=False,
    )
```

```python
import functools
import math

import jax
import jax.numpy as jnp
from jax import lax
from jax.experimental import pallas as pl
from jax.experimental.pallas import tpu as pltpu
from jax.sharding import PartitionSpec as P

BETA = 0.2
BF16, F32 = jnp.bfloat16, jnp.float32
Z = 128
B = 4
H = 2
N = B + 2 * H
MID = slice(H * Z, (H + B) * Z)
WIDTHS = (4, 3, 3, 2, 1)
Y_AT = tuple(Z * sum(WIDTHS[:u]) for u in range(6))
X_AT = tuple(Z * sum(w * (B + 2 * w) for w in WIDTHS[:u]) for u in range(6))
RING = slice((H - 1) * Z, (H + B + 1) * Z)
GROUP = 128
ROWS = 8
HALF = GROUP * ROWS
VMEM_LIMIT = 24 * 2**20


def shape(dims, dtype):
    return jax.ShapeDtypeStruct(dims, dtype)


def call(kernel, outs, args, scratch=(), flops=1_000_000, name=None):
    moved = sum(math.prod(a.shape) * a.dtype.itemsize for a in list(args) + list(outs))
    return pl.pallas_call(
        kernel,
        out_shape=list(outs),
        in_specs=[pl.BlockSpec(memory_space=pltpu.VMEM)] * len(args),
        out_specs=[pl.BlockSpec(memory_space=pltpu.VMEM)] * len(outs),
        scratch_shapes=list(scratch),
        compiler_params=pltpu.CompilerParams(vmem_limit_bytes=VMEM_LIMIT),
        cost_estimate=pl.CostEstimate(flops=flops, bytes_accessed=moved, transcendentals=0),
        name=name,
    )(*args)


def lane_moves(rows, width):
    lane = lax.broadcasted_iota(jnp.int32, (rows, width), 1) % Z
    return lane != 0, lane != Z - 1


def from_left(v, keep):
    parts = [pltpu.roll(v[:, k * Z : (k + 1) * Z], 1, 1) for k in range(v.shape[1] // Z)]
    return jnp.where(keep, jnp.concatenate(parts, axis=1), jnp.zeros_like(v))


def from_right(v, keep):
    parts = [pltpu.roll(v[:, k * Z : (k + 1) * Z], Z - 1, 1) for k in range(v.shape[1] // Z)]
    return jnp.where(keep, jnp.concatenate(parts, axis=1), jnp.zeros_like(v))


def spread(v):
    not_first, not_last = lane_moves(*v.shape)
    return jnp.concatenate([from_right(v, not_last), v, from_left(v, not_first)], axis=0)


def inside(x, y, blocks):
    x = lax.axis_index("gx") * B + x
    block = lax.broadcasted_iota(jnp.int32, (1, blocks * Z), 1) // Z
    y = lax.axis_index("row") * B + block + y
    in_x = (x >= 0) & (x < lax.axis_size("gx") * B)
    in_y = (y >= 0) & (y < lax.axis_size("row") * B)
    return jnp.where(in_y, 1.0, 0.0) * jnp.where(in_x, 1.0, 0.0)


def as_column(row):
    n = row.shape[1]
    rows = lax.broadcasted_iota(jnp.int32, (n, n), 0)
    lanes = lax.broadcasted_iota(jnp.int32, (n, n), 1)
    return jnp.sum(jnp.where(rows == lanes, row, 0.0), axis=1, keepdims=True)


def conv_row(kernel_ref, sources, i, lanes):
    n = lanes.stop - lanes.start
    cut = slice(lanes.start - Z, lanes.stop + Z)
    rhs = jnp.concatenate([s(i + a - 1, cut) for a in range(3) for s in sources], axis=0)
    got = jnp.dot(kernel_ref[...], rhs, preferred_element_type=F32)
    acc = got[:48, :n] + got[48:96, Z : Z + n] + got[96:, 2 * Z :]
    not_first, not_last = lane_moves(16, n)
    return from_left(acc[:16], not_first) + acc[16:32] + from_right(acc[32:], not_last)


def back_row(turned_ref, channels, spread_ref, i, lanes):
    n, q = lanes.stop - lanes.start, channels.stop - channels.start
    cut = slice(lanes.start - Z, lanes.stop + Z)
    lhs = jnp.concatenate([turned_ref[b, channels] for b in range(3)], axis=0)
    rhs = jnp.concatenate([spread_ref[i + 1 - a, :, cut] for a in range(3)], axis=0)
    got = jnp.dot(lhs, rhs, preferred_element_type=F32)
    return got[:q, 2 * Z :] + got[q : 2 * q, Z : Z + n] + got[2 * q :, :n]


def kernel_gradient(own, sources):
    lhs = jnp.concatenate(
        [jnp.concatenate([layer[i] for layer in own], axis=0) for i in range(B)], axis=1
    )
    for a in range(3):
        taps = [
            jnp.concatenate(
                [
                    jnp.concatenate(
                        [s[H + i + a - 1, :, pl.ds((H + b - 1) * Z, B * Z)] for s in sources], axis=0
                    )
                    for i in range(B)
                ],
                axis=1,
            )
            for b in range(3)
        ]
        q = taps[0].shape[0]
        got = lax.dot_general(
            lhs, jnp.concatenate(taps, axis=0), (((1,), (1,)), ((), ())), preferred_element_type=F32
        )
        gap = jnp.zeros((got.shape[0], Z - q), F32)
        for b in range(3):
            yield 3 * a + b, jnp.concatenate([got[:, q * b : q * (b + 1)], gap], axis=1)


def own_cells(spread_ref):
    return [spread_ref[B + i, :, slice(B * Z, 2 * B * Z)] for i in range(B)]


def activate(value):
    sigmoid = jax.nn.sigmoid(value)
    return 0.2 * value + 0.8 * value * sigmoid, 0.2 + 0.8 * (
        sigmoid + value * sigmoid * (1.0 - sigmoid)
    )


def ring_row(parts, u, f):
    above, below, before, own, after = parts
    w = WIDTHS[u]
    if B <= f < 2 * B:
        side = slice(Y_AT[u], Y_AT[u + 1])
        i = f - B
        return jnp.concatenate(
            [before[i, :, side], own[i, 16 * u : 16 * (u + 1)], after[i, :, side]], axis=1
        )
    ref, r = (above, f - B + w) if f < B else (below, f - 2 * B)
    at = X_AT[u] + r * (B + 2 * w) * Z
    return ref[:, at : at + (B + 2 * w) * Z]


def wide_sum(blocks):
    total = sum(block.astype(F32) for block in blocks)
    return jnp.broadcast_to(jnp.sum(total, axis=1, keepdims=True), (total.shape[0], Z))


def cell_sum(own):
    return wide_sum([rows[16:32] for rows in own])


def pack_kernel(x_ref, out_ref, wide):
    wide[...] = x_ref[...].astype(F32)
    for i in range(B):
        row = [wide[pl.ds(B * i + j, 64, stride=B * B), :].astype(BF16) for j in range(B)]
        out_ref[i] = jnp.concatenate(row, axis=1)


def band_kernel(before, own, after, out_ref):
    for k, ref in enumerate((before, own, after)):
        out_ref[:, :, k * B * Z : (k + 1) * B * Z] = ref[...]


def edges_kernel(before, own, after, top, bottom):
    for u, w in enumerate(WIDTHS):
        parts = (top, bottom, before, own, after)
        for r in range(w):
            at = X_AT[u] + r * (B + 2 * w) * Z
            lanes = slice(at, at + (B + 2 * w) * Z)
            top[:, lanes] = ring_row(parts, u, B + r)
            bottom[:, lanes] = ring_row(parts, u, 2 * B - w + r)


def prepare_kernel(
    cot_ref, merge, layer_bias, merging_bias, k0, k1, k2, k3,
    base, carried, merge_grad, bias, merge_bias, w0, w1, w2, w3, t0, t1, t2, t3, wide,
):
    for k in range(4):
        column = as_column(layer_bias[k : k + 1].astype(F32))
        bias[16 * k : 16 * (k + 1)] = jnp.broadcast_to(column, (16, Z))
    merge_bias[...] = jnp.broadcast_to(as_column(merging_bias[...].astype(F32)), (64, Z))
    for k_ref, w_ref, t_ref in ((k0, w0, t0), (k1, w1, t1), (k2, w2, t2), (k3, w3, t3)):
        w_ref[...] = jnp.concatenate([k_ref[144 * a : 144 * (a + 1)] for a in range(3)], axis=1)
        for b in range(3):
            rows = [k_ref[48 * t : 48 * (t + 1)] for t in (b, 3 + b, 6 + b)]
            t_ref[b] = jnp.transpose(jnp.concatenate(rows, axis=0).astype(F32)).astype(BF16)
    wide[...] = cot_ref[...].astype(F32)
    merge_t = jnp.transpose(merge[...].astype(F32)).astype(BF16)
    for i in range(B):
        cot = jnp.concatenate(
            [wide[pl.ds(B * i + j, 64, stride=B * B), :] for j in range(B)], axis=1
        )
        grad = (BETA * cot).astype(BF16)
        merge_grad[i] = grad
        back = jnp.dot(merge_t, grad, preferred_element_type=F32)
        base[i] = cot + back[:64]
        carried[i] = back[64:]


def forward_kernel(
    above, band, below, k0, k1, k2, k3, bias, carried,
    frame, hidden_01, hidden_2, hidden_3, slope_0, slope_1, slope_2, own_3, own, left, right,
    wide_0, wide_1, wide_2,
):
    bands = (above, band, below)
    near = slice((B - H) * Z, (2 * B + H) * Z)
    sources = [lambda i, cut: bands[i // B][i % B, :, cut]]
    for i in range(N):
        frame[i] = sources[0](i + B - H, near)
    for k, (kernel_ref, wide) in enumerate(((k0, wide_0), (k1, wide_1), (k2, wide_2))):
        reach = 3 - k
        lanes = slice((B - reach) * Z, (2 * B + reach) * Z)
        for i in range(B - reach, 2 * B + reach):
            pre = conv_row(kernel_ref, sources, i, lanes) + bias[16 * k : 16 * (k + 1), 0:1]
            value, slope = activate(pre)
            present = inside(i - B, -reach, B + 2 * reach)
            wide[i, :, lanes] = (value * present).astype(BF16)
            slope = slope * present
            if k == 0 and B - 1 <= i < 2 * B + 1:
                slope_0[i - B + 1] = slope[:, 2 * Z : (B + 4) * Z]
            if k == 1:
                slope_1[i - B + 2] = slope
            if k == 2 and B <= i < 2 * B:
                slope_2[i - B] = slope[:, Z : (B + 1) * Z]
        sources.append(lambda i, cut, wide=wide: wide[i, :, cut])
    for i in range(N):
        hidden_01[i, 0:16] = wide_0[i + B - H, :, near]
        hidden_01[i, 16:32] = wide_1[i + B - H, :, near]
        if 0 < i < N - 1:
            hidden_2[i, :, RING] = wide_2[i + B - H, :, slice((B - 1) * Z, (2 * B + 1) * Z)]
    for i in range(B):
        pre = conv_row(k3, sources, B + i, slice(B * Z, 2 * B * Z)) + bias[48:64, 0:1]
        value, slope = activate(pre)
        hidden_3[i] = value.astype(BF16)
        grad = (carried[i, 48:64] * slope).astype(BF16)
        own_3[i] = spread(grad)
        rest = [slope_2[i]] + [carried[i, 16 * k : 16 * (k + 1)] for k in (2, 1, 0)]
        ready = [grad] + [value.astype(BF16) for value in rest]
        own[i] = jnp.concatenate(ready, axis=0)
        left[i] = jnp.concatenate([v[:, : w * Z] for v, w in zip(ready, WIDTHS)], axis=1)
        right[i] = jnp.concatenate([v[:, (B - w) * Z :] for v, w in zip(ready, WIDTHS)], axis=1)


def merge_kernel(
    frame, hidden_01, hidden_2, hidden_3, own_3, merge, merge_bias, merge_grad,
    out_ref, grad_3, grad_merge,
):
    total = jnp.zeros((64, 128), F32)
    for i in range(B):
        base = frame[H + i, :, MID]
        joined = jnp.concatenate(
            [base, hidden_01[H + i, :, MID], hidden_2[H + i, :, MID], hidden_3[i]], axis=0
        )
        merged = jnp.dot(merge[...], joined, preferred_element_type=F32) + merge_bias[:, 0:1]
        out = base.astype(F32) + BETA * merged
        for j in range(B):
            out_ref[pl.ds(B * i + j, 64, stride=B * B), :] = out[:, j * Z : (j + 1) * Z]
        grad = merge_grad[i]
        total = total + lax.dot_general(
            grad, joined, (((1,), (1,)), ((), ())), preferred_element_type=F32
        )
    grad_merge[0:64] = total
    grad_merge[64:128] = wide_sum([merge_grad[i] for i in range(B)])
    own = [own_3[i] for i in range(B)]
    grad_merge[128:144] = cell_sum(own)
    for t, got in kernel_gradient([own], [frame, hidden_01, hidden_2]):
        grad_3[48 * t : 48 * (t + 1)] = got


def backward_kernel(
    above, below, before, own, after, t1, t2, t3, slope_0, slope_1, slope_2, carried,
    frame, hidden_01, grad_3, grad_merge,
    spread_0, spread_1, spread_2, spread_3, kept, sent, sums,
):
    parts = (above, below, before, own, after)
    spreads = (spread_0, spread_1, spread_2, spread_3)
    turned_refs = (None, t1, t2, t3)
    for f in range(3 * B):
        spread_3[f] = spread(ring_row(parts, 0, f))
    for k in (2, 1, 0):
        reach = k + 1
        lanes = slice((B - reach) * Z, (2 * B + reach) * Z)
        middle = slice(reach * Z, (B + reach) * Z)
        channels = slice(64 + 16 * k, 80 + 16 * k)
        for f in range(B - reach, 2 * B + reach):
            i = f - B
            here = 0 <= i < B
            got = ring_row(parts, 4 - k, f).astype(F32)
            if here:
                exact = carried[i, 16 * k : 16 * (k + 1)]
                got = jnp.concatenate([got[:, : middle.start], exact, got[:, middle.stop :]], axis=1)
            for m in range(k + 1, 4):
                got = got + back_row(turned_refs[m], channels, spreads[m], f, lanes)
            if k == 2:
                slope = ring_row(parts, 1, f).astype(F32)
                if here:
                    slope = jnp.concatenate(
                        [slope[:, : middle.start], slope_2[i], slope[:, middle.stop :]], axis=1
                    )
            else:
                slope = (slope_0, slope_1)[k][i + reach]
            grad = (got * slope).astype(BF16)
            spreads[k][f, :, lanes] = spread(grad)
    owns = [own_cells(ref) for ref in spreads[:3]]
    for t, got in kernel_gradient(owns, [frame, hidden_01]):
        for k in range(3):
            at = 432 * k + 48 * t
            sums[at : at + 48] = got[48 * k : 48 * (k + 1)]
    sums[1296:1728] = grad_3[...]
    sums[1728:1856] = grad_merge[0:128]
    for k in range(3):
        sums[1856 + 16 * k : 1872 + 16 * k] = cell_sum(owns[k])
    sums[1904:1920] = grad_merge[128:144]
    sums[1920:] = jnp.zeros((2 * HALF - 1920, Z), F32)
    mine, other = halves()
    kept[...] = sums[pl.ds(mine, HALF), :]
    sent[...] = sums[pl.ds(other, HALF), :].astype(BF16)


def pulled(i, refs, turned_refs):
    lanes = slice(B * Z, 2 * B * Z)
    return sum(back_row(t, slice(0, 64), ref, B + i, lanes) for ref, t in zip(refs, turned_refs))


def half_kernel(spread_2, spread_3, t2, t3, base, out_ref):
    for i in range(B):
        out_ref[i] = base[i] + pulled(i, (spread_2, spread_3), (t2, t3))


def last_kernel(spread_0, spread_1, t0, t1, base, out_ref):
    for i in range(B):
        out = base[i] + pulled(i, (spread_0, spread_1), (t0, t1))
        for j in range(B):
            out_ref[pl.ds(B * i + j, 64, stride=B * B), :] = out[:, j * Z : (j + 1) * Z]


def halves():
    first = lax.axis_index("rep") * HALF
    return pl.multiple_of(first, HALF), pl.multiple_of(HALF - first, HALF)


def pair_kernel(kept, came, out_ref):
    out_ref[...] = (kept[...] + came[...].astype(F32)).astype(BF16)


def add_kernel(x_ref, out_ref):
    def step(k, acc):
        return acc + x_ref[pl.ds(pl.multiple_of(k * 128, 128), 128), :].astype(F32)

    acc = lax.fori_loop(0, HALF // 128, step, jnp.zeros((128, Z), F32))
    total = acc[0:ROWS]
    for k in range(1, 128 // ROWS):
        total = total + acc[k * ROWS : (k + 1) * ROWS]
    block = jnp.concatenate([total] * (128 // ROWS), axis=0).astype(BF16)

    def put(k, carry):
        out_ref[pl.ds(pl.multiple_of(k * 128, 128), 128), :] = block
        return carry

    lax.fori_loop(0, HALF // 128, put, 0)


def turned(block):
    rows = lax.broadcasted_iota(jnp.int32, block.shape, 0)
    lanes = lax.broadcasted_iota(jnp.int32, block.shape, 1)
    return jnp.sum(jnp.where(rows == lanes, block, 0.0), axis=0, keepdims=True)


def unpack_kernel(scale, mine_ref, other_ref, g0, g1, g2, g3, bias, weight, weight_bias, sums):
    mine, other = halves()
    sums[pl.ds(mine, HALF), :] = mine_ref[...].astype(F32) * scale
    sums[pl.ds(other, HALF), :] = other_ref[...].astype(F32) * scale
    for k, g in enumerate((g0, g1, g2, g3)):
        g[...] = sums[432 * k : 432 * (k + 1), : g.shape[1]]
    weight[...] = sums[1728:1792]
    weight_bias[...] = turned(sums[1792:1856])[:, :64]
    for k in range(4):
        bias[k : k + 1] = turned(sums[1856 + 16 * k : 1872 + 16 * k])[:, :16]


def neighbours(low, high, axis):
    up = [(i, i + 1) for i in range(lax.axis_size(axis) - 1)]
    return lax.ppermute(high, axis, up), lax.ppermute(low, axis, [(j, i) for i, j in up])


def body(samples, cotangent, kernel_0, kernel_1, kernel_2, kernel_3, layer_bias, merging_weight, merging_bias):
    kernels = (kernel_0, kernel_1, kernel_2, kernel_3)
    cells = B * B * Z * lax.axis_size("gx") * lax.axis_size("row") * lax.axis_size("rep")
    scale = 1.0 / math.sqrt(cells)
    flat = [k.transpose(1, 0, 2).reshape(432, k.shape[2]) for k in kernels]
    columns = shape((64, Z), F32)
    wide = pltpu.VMEM((1024, Z), F32)
    (own,) = call(
        pack_kernel,
        [shape((B, 64, B * Z), BF16)],
        [samples.reshape(1024, Z)],
        [wide],
        name="pack",
    )
    base, carried, merge_grad, bias, merge_bias, w0, w1, w2, w3, t0, t1, t2, t3 = call(
        prepare_kernel,
        [shape((B, 64, B * Z), F32)] * 2
        + [shape((B, 64, B * Z), BF16), columns, columns]
        + [shape((144, 3 * k.shape[2]), BF16) for k in kernels]
        + [shape((3, k.shape[2], 144), BF16) for k in kernels],
        [cotangent.reshape(1024, Z), merging_weight, layer_bias, merging_bias.reshape(1, 64)] + flat,
        [wide],
        flops=40_000_000,
        name="prepare",
    )
    before, after = neighbours(own, own, "row")
    (band,) = call(band_kernel, [shape((B, 64, 3 * B * Z), BF16)], [before, own, after], name="band")
    above, below = neighbours(band, band, "gx")
    side = shape((B, 16, Y_AT[5]), BF16)
    (
        frame, hidden_01, hidden_2, hidden_3,
        slope_0, slope_1, slope_2, own_3, own, left, right,
    ) = call(
        forward_kernel,
        [
            shape((N, 64, N * Z), BF16),
            shape((N, 32, N * Z), BF16),
            shape((N, 16, N * Z), BF16),
            shape((B, 16, B * Z), BF16),
            shape((B + 2, 16, (B + 2) * Z), F32),
            shape((B + 4, 16, (B + 4) * Z), F32),
            shape((B, 16, B * Z), F32),
            shape((B, 48, B * Z), BF16),
            shape((B, 80, B * Z), BF16),
            side,
            side,
        ],
        [above, band, below, w0, w1, w2, w3, bias, carried],
        [pltpu.VMEM((3 * B, 16, 3 * B * Z), BF16)] * 3,
        name="forward",
    )
    before, after = neighbours(left, right, "row")
    edge = shape((16, X_AT[5]), BF16)
    top, bottom = call(edges_kernel, [edge, edge], [before, own, after], name="edges")
    above, below = neighbours(top, bottom, "gx")
    output, grad_3, grad_merge = call(
        merge_kernel,
        [shape((1024, Z), F32), shape((432, Z), F32), shape((144, Z), F32)],
        [frame, hidden_01, hidden_2, hidden_3, own_3, merging_weight, merge_bias, merge_grad],
        flops=100_000_000,
        name="merge",
    )
    spreads = [shape((3 * B, 48, 3 * B * Z), BF16)] * 4
    *spreads, kept, sent = call(
        backward_kernel,
        spreads + [shape((HALF, Z), F32), shape((HALF, Z), BF16)],
        [above, below, before, own, after, t1, t2, t3, slope_0, slope_1, slope_2, carried]
        + [frame, hidden_01, grad_3, grad_merge],
        [pltpu.VMEM((2 * HALF, Z), F32)],
        name="backward",
    )
    axes = ("gx", "row")
    swap = [(0, 1), (1, 0)]
    half_sum = shape((HALF, Z), BF16)
    (part,) = call(
        half_kernel,
        [shape((B, 64, B * Z), F32)],
        spreads[2:] + [t2, t3, base],
        flops=150_000_000,
        name="input_gradient_3_2",
    )
    came, part = lax.optimization_barrier((lax.ppermute(sent, "rep", swap), part))
    (paired,) = call(pair_kernel, [half_sum], [kept, came], name="pair")
    spread_sums = lax.all_to_all(paired.reshape(GROUP, ROWS, Z), axes, 0, 0, tiled=True)
    (added,) = call(add_kernel, [half_sum], [spread_sums.reshape(HALF, Z)], name="add")
    totals = lax.all_to_all(added.reshape(GROUP, ROWS, Z), axes, 0, 0, tiled=True)
    totals = totals.reshape(HALF, Z)
    others = lax.ppermute(totals, "rep", swap)
    (grad_input,) = call(
        last_kernel,
        [shape((1024, Z), F32)],
        spreads[:2] + [t0, t1, part],
        flops=300_000_000,
        name="input_gradient",
    )
    unpacked = call(
        functools.partial(unpack_kernel, scale),
        [shape((432, k.shape[2]), F32) for k in kernels]
        + [shape((4, 16), F32), shape((64, 128), F32), shape((1, 64), F32)],
        [totals, others],
        [pltpu.VMEM((2 * HALF, Z), F32)],
        name="unpack",
    )
    grad_kernels = [g.reshape(27, 16, g.shape[1]).transpose(1, 0, 2) for g in unpacked[:4]]
    out_shape = (1, 64, B, B, Z)
    return (
        output.reshape(out_shape),
        grad_input.reshape(out_shape),
        *grad_kernels,
        unpacked[4],
        unpacked[5],
        unpacked[6].reshape(64),
    )


def solution(mesh):
    split = P("rep", None, "gx", "row", None)
    return jax.shard_map(
        body,
        mesh=mesh,
        in_specs=(split, split) + (P(),) * 7,
        out_specs=(split, split) + (P(),) * 7,
        check_vma=False,
    )
```
